32 devices in a mesh: seq: 8 (over z, x), blk: 4 (over y, core).
Axes of the slice: x: 2, y: 2, z: 4, core: 2. Of those that a mesh axis runs over, the one named last changes fastest.
Arguments:
- words: bfloat16 [8, 512, 768], P('seq', 'blk'), may hold values from -6 to 6
- entities: bfloat16 [8, 128, 768], P('seq'), may hold values from -6 to 6
- segments: int32 [8, 512], P('seq'), may hold values from 0 to 2, as said below
- entity_counts: int32 [8], P('seq'), may hold values from 32 to 128, as said below
- entity_anchor: int32 [8, 128], P('seq'), may hold values from 0 to 511
- query_weights: bfloat16 [1, 4, 768, 768], P(None, None, ('seq', 'blk')), may hold values from -0.21875 to 0.21875
- kv_weights: bfloat16 [1, 2, 768, 768], P(None, None, ('seq', 'blk')), may hold values from -0.21875 to 0.21875
- out_weight: bfloat16 [1, 768, 768], P(None, ('seq', 'blk')), may hold values from -2.5 to 2.5
- ff_in: bfloat16 [1, 768, 3072], P(None, ('seq', 'blk')), may hold values from -0.21875 to 0.21875
- ff_out: bfloat16 [1, 3072, 768], P(None, ('seq', 'blk')), may hold values from -0.109375 to 0.109375
- norm_gain: bfloat16 [1, 2, 768], P(None, None, ('seq', 'blk')), may hold values from 0.5 to 1.5
- norm_bias: bfloat16 [1, 2, 768], P(None, None, ('seq', 'blk')), may hold values from -1.5 to 1.5
- grad_words: bfloat16 [8, 512, 768], P('seq', 'blk'), may hold values from -6 to 6
- grad_entities: bfloat16 [8, 128, 768], P('seq'), may hold values from -6 to 6
Outputs:
- out_words: bfloat16 [8, 512, 768], P('seq', 'blk')
- out_entities: bfloat16 [8, 128, 768], P('seq')
- input_grad_words: float32 [8, 512, 768], P('seq', 'blk')
- input_grad_entities: float32 [8, 128, 768], P('seq')
- grad_query: float32 [1, 4, 768, 768], P(None, None, ('seq', 'blk'))
- grad_kv: float32 [1, 2, 768, 768], P(None, None, ('seq', 'blk'))
- grad_out: float32 [1, 768, 768], P(None, ('seq', 'blk'))
- grad_ff_in: float32 [1, 768, 3072], P(None, ('seq', 'blk'))
- grad_ff_out: float32 [1, 3072, 768], P(None, ('seq', 'blk'))
- grad_gain: float32 [1, 2, 768], P(None, None, ('seq', 'blk'))
- grad_bias: float32 [1, 2, 768], P(None, None, ('seq', 'blk'))
The draws below stay inside these ranges and needn't reach their ends.
Inputs may be any that keep to these rules, and one draw needn't show every extreme that they name: `segments`: within a sequence segment numbers never fall: 0, then 1 from one of the words 1 to 64, then 2 from one of the last 64 words. `entity_counts`: entities at and past a sequence's count are padding; some sequence has 128 and some has 32.
All inputs are finite; a program needn't handle non-finite values.
Results may differ from the reference program's by a relative error of at most 0.025.
Values may be sent and summed in bfloat16 or wider, within the bound.
No kernel may reach another device: no remote copies, remote signals or barrier semaphores. Data moves between devices by JAX's collectives and lax.ppermute only.
A program may use at most 192 MiB of HBM per device.

```python
import jax
import jax.numpy as jnp
from jax import lax

D = 768
HEADS = 12
FF = 3072
WORDS = 512
ENT = 128
LAYERS = 1
SEQS = 8


def draw_segments(key, part):
    key = jax.random.fold_in(key, 11)
    key_one, key_two = jax.random.split(key)
    begin_one = jax.random.randint(key_one, (SEQS, 1), 1, WORDS // 8 + 1)
    begin_two = jax.random.randint(key_two, (SEQS, 1), WORDS - WORDS // 8, WORDS)
    position = jnp.arange(WORDS, dtype=jnp.int32)[None, :]
    return (position >= begin_one).astype(jnp.int32) + (position >= begin_two).astype(jnp.int32)


def draw_entity_counts(key, part):
    key = jax.random.fold_in(key, 23)
    key_one, key_two = jax.random.split(key)
    counts = jax.random.randint(key_one, (SEQS,), ENT // 4, ENT + 1)
    shuffled = jax.random.permutation(key_two, SEQS)
    counts = counts.at[shuffled[0]].set(ENT)
    counts = counts.at[shuffled[1]].set(ENT // 4)
    return counts.astype(jnp.int32)


def with_ends(values, own_key, smallest, top_value):
    longest = values.shape.index(max(values.shape))
    spots = []
    for shift in (0, 1):
        where = [jax.random.randint(jax.random.fold_in(own_key, axis), (), 0, length) for axis, length in enumerate(values.shape)]
        where[longest] = (where[longest] + shift) % values.shape[longest]
        spots.append(tuple(where))
    return values.at[spots[0]].set(smallest).at[spots[1]].set(top_value)


def level_of(own_key, shape, cuts, smallest, high):
    gain, own = 1.0, jax.random.fold_in(own_key, 6)
    for axis_at, shards_of in cuts:
        draws = jnp.exp(jax.random.uniform(jax.random.fold_in(own, axis_at), (shards_of,), jnp.float32, smallest / len(cuts), high / len(cuts)))
        gain = gain * jnp.repeat(draws, shape[axis_at] // shards_of).reshape([-1 if axis == axis_at else 1 for axis in range(len(shape))])
    return gain


def gaussian(stream_key, dims, scale, most, shards=(), kind=jnp.bfloat16):
    drawn = scale * jax.random.normal(stream_key, dims, jnp.float32)
    if shards:
        drawn = drawn * level_of(stream_key, dims, shards, -0.22, 0.18)
    return jnp.clip(drawn, -most, most).astype(kind)


def setup_inputs(seed: int = 0) -> dict:
    splits = jax.random.split(jax.random.key(seed), 15)
    return {
        "words": gaussian(splits[0], (SEQS, WORDS, D), 1.0, 6.0, ((0, 8), (1, 4))),
        "entities": gaussian(splits[1], (SEQS, ENT, D), 1.0, 6.0, ((0, 8),)),
        "segments": draw_segments(jax.random.fold_in(splits[14], 71), 0),
        "entity_counts": draw_entity_counts(jax.random.fold_in(splits[14], 71), 0),
        "entity_anchor": with_ends(jax.random.randint(splits[4], (SEQS, ENT), 0, WORDS), jax.random.fold_in(splits[4], 1), 0, WORDS - 1).astype(jnp.int32),
        "query_weights": gaussian(splits[5], (LAYERS, 4, D, D), D ** -0.5, 0.21875, ((2, 32),)),
        "kv_weights": gaussian(splits[6], (LAYERS, 2, D, D), D ** -0.5, 0.21875, ((2, 32),)),
        "out_weight": gaussian(splits[7], (LAYERS, D, D), (D // 128) ** -0.5, 2.5, ((1, 32),)),
        "ff_in": gaussian(splits[8], (LAYERS, D, FF), D ** -0.5, 0.21875, ((1, 32),)),
        "ff_out": gaussian(splits[9], (LAYERS, FF, D), FF ** -0.5, 0.109375, ((1, 32),)),
        "norm_gain": jnp.clip(1.0 + 0.1 * jax.random.normal(splits[10], (LAYERS, 2, D), jnp.float32), 0.5, 1.5).astype(jnp.bfloat16),
        "norm_bias": gaussian(splits[11], (LAYERS, 2, D), 0.3, 1.5, ((2, 32),)),
        "grad_words": gaussian(splits[12], (SEQS, WORDS, D), 1.0, 6.0, ((0, 8), (1, 4))),
        "grad_entities": gaussian(splits[13], (SEQS, ENT, D), 1.0, 6.0, ((0, 8),)),
    }


@jax.custom_vjp
def low(v):
    return lax.optimization_barrier(v.astype(jnp.bfloat16)).astype(jnp.float32)

@jax.custom_vjp
def low_back(v):
    return v

def low_keep(v):
    return (low(v), None)

def low_pass(kept, grad):
    return (grad,)

def back_keep(v):
    return (v, None)

def back_low(kept, grad):
    return (low(grad),)
low.defvjp(low_keep, low_pass)
low_back.defvjp(back_keep, back_low)
epsilon = 1e-05
masked_score = -1e+30

def rounded_both(tensor):
    return low(low_back(tensor))

def product(operand, matrix):
    return jnp.dot(operand, matrix, precision=lax.Precision.HIGHEST)

def normalize(tensor, norm_scale, norm_shift):
    center = tensor - lax.optimization_barrier(jnp.mean(tensor, axis=-1, keepdims=True))
    inverse = lax.rsqrt(lax.optimization_barrier(jnp.mean(center * center, axis=-1, keepdims=True)) + epsilon)
    return center * inverse * norm_scale + norm_shift

def split_heads(tensor):
    return tensor.reshape(tensor.shape[0], HEADS, tensor.shape[1] // HEADS)

def attend(near_queries, far_queries, word_keys, entity_keys, word_values, entity_values, word_allowed, entity_allowed):
    near = jnp.einsum('qhd,khd->hqk', split_heads(near_queries), split_heads(word_keys), precision=lax.Precision.HIGHEST)
    far = jnp.einsum('qhd,khd->hqk', split_heads(far_queries), split_heads(entity_keys), precision=lax.Precision.HIGHEST)
    scores = low_back(jnp.concatenate([near, far], axis=-1))
    allowed = jnp.concatenate([word_allowed, entity_allowed], axis=-1)[None]
    masked = jnp.where(allowed, scores, masked_score)
    row_top = lax.optimization_barrier(jnp.max(masked, axis=-1, keepdims=True))
    weights = jnp.where(allowed, jnp.exp(masked - row_top), 0.0)
    probabilities = low(weights / lax.optimization_barrier(jnp.sum(weights, axis=-1, keepdims=True)))
    values = jnp.concatenate([word_values, entity_values], axis=0)
    context = jnp.einsum('hqk,khd->qhd', probabilities, split_heads(values), precision=lax.Precision.HIGHEST)
    return rounded_both(context.reshape(near_queries.shape[0], -1))

def one_layer(layer_weights, words, entities, masks):
    query_mats, kv_mats, out_mat, ff_in_mat, ff_out_mat, gains, shifts = layer_weights
    same_ww, same_we, same_ew, same_ee = masks
    word_count = words.shape[0]
    factor = (words.shape[1] // HEADS) ** (-0.5)
    word_low = low(words)
    entity_low = low(entities)
    word_word_query = rounded_both(product(word_low, query_mats[0]) * factor)
    word_entity_query = rounded_both(product(word_low, query_mats[1]) * factor)
    entity_word_query = rounded_both(product(entity_low, query_mats[2]) * factor)
    entity_entity_query = rounded_both(product(entity_low, query_mats[3]) * factor)
    word_keys = rounded_both(product(word_low, kv_mats[0]))
    word_values = rounded_both(product(word_low, kv_mats[1]))
    entity_keys = rounded_both(product(entity_low, kv_mats[0]))
    entity_values = rounded_both(product(entity_low, kv_mats[1]))
    word_context = attend(word_word_query, word_entity_query, word_keys, entity_keys, word_values, entity_values, same_ww, same_we)
    entity_context = attend(entity_word_query, entity_entity_query, word_keys, entity_keys, word_values, entity_values, same_ew, same_ee)
    joined = jnp.concatenate([words, entities], axis=0)
    contexts = jnp.concatenate([word_context, entity_context], axis=0)
    mixed_rows = normalize(joined + low_back(product(contexts, out_mat)), gains[0], shifts[0])
    hidden = low_back(product(low(mixed_rows), ff_in_mat))
    active = low(jax.nn.gelu(hidden, approximate=False))
    result = normalize(mixed_rows + low_back(product(active, ff_out_mat)), gains[1], shifts[1])
    return (result[:word_count], result[word_count:])

def sequence_pass(weights, words, entities, segment_row, count_value, anchor_row):
    entity_segments = jnp.take(segment_row, anchor_row)
    live_ents = jnp.arange(ENT, dtype=jnp.int32) < count_value
    same_ww = segment_row[:, None] == segment_row[None, :]
    same_we = (segment_row[:, None] == entity_segments[None, :]) & live_ents[None, :]
    same_ew = entity_segments[:, None] == segment_row[None, :]
    same_ee = (entity_segments[:, None] == entity_segments[None, :]) & live_ents[None, :]
    masks = (same_ww, same_we, same_ew, same_ee)
    for layer_index in range(LAYERS):
        layer_weights = tuple((member[layer_index] for member in weights))
        words, entities = one_layer(layer_weights, words, entities, masks)
    return (words, entities)

def reference(words, entities, segments, entity_counts, entity_anchor, query_weights, kv_weights, out_weight, ff_in, ff_out, norm_gain, norm_bias, grad_words, grad_entities):
    weights = tuple((member.astype(jnp.float32) for member in (query_weights, kv_weights, out_weight, ff_in, ff_out, norm_gain, norm_bias)))
    checked = jax.checkpoint(sequence_pass)

    def forward(weights, words_in, entities_in):

        def one_step(unused, item):
            return (unused, checked(weights, item[0], item[1], item[2], item[3], item[4]))
        unused_end, outputs = lax.scan(one_step, jnp.zeros((), jnp.float32), (words_in, entities_in, segments, entity_counts, entity_anchor))
        return outputs
    outputs, pullback = jax.vjp(forward, weights, words.astype(jnp.float32), entities.astype(jnp.float32))
    weight_grads, word_grads, entity_grads = pullback((grad_words.astype(jnp.float32), grad_entities.astype(jnp.float32)))
    return (outputs[0].astype(jnp.bfloat16), outputs[1].astype(jnp.bfloat16), word_grads, entity_grads, weight_grads[0], weight_grads[1], weight_grads[2], weight_grads[3], weight_grads[4], weight_grads[5], weight_grads[6])
```

```python
import jax
import jax.numpy as jnp
from jax import lax
from jax.experimental import pallas as pl
from jax.experimental.pallas import tpu as pltpu
from jax.sharding import PartitionSpec as P

HEADS = 12
RANKS = 4
epsilon = 1e-05
masked_score = -1e30
bf16 = jnp.bfloat16
f32 = jnp.float32


def dot_nn(a, b):
    return jnp.dot(a, b, preferred_element_type=f32)


def dot_nt(a, b):
    return lax.dot_general(a, b, (((1,), (1,)), ((), ())), preferred_element_type=f32)


def dot_tn(a, b):
    return lax.dot_general(a, b, (((0,), (0,)), ((), ())), preferred_element_type=f32)


def block(ref, index, size):
    return pl.ds(pl.multiple_of(index * size, size), size)


def call(body, name, outs, scratch=(), vmem=10, us=1, held=0, same=0):
    def run(*args):
        return pl.pallas_call(
            body,
            name=name,
            out_shape=[jax.ShapeDtypeStruct(s, t) for s, t in outs],
            in_specs=[pl.BlockSpec(memory_space=pltpu.HBM)] * held
            + [pl.BlockSpec(memory_space=pltpu.VMEM)] * (len(args) - held),
            out_specs=[pl.BlockSpec(memory_space=pltpu.VMEM)] * len(outs),
            scratch_shapes=list(scratch),
            input_output_aliases={i: i for i in range(same)},
            compiler_params=pltpu.CompilerParams(vmem_limit_bytes=vmem << 20),
            cost_estimate=pl.CostEstimate(
                flops=int(us * 1e6), bytes_accessed=int(us * 1e3), transcendentals=0
            ),
        )(*args)

    return run


def partner(k):
    return jnp.bitwise_xor(lax.axis_index("blk"), k)


def ring_seat(k, e):
    s = lax.axis_index("seq")
    z = lax.div(s, 2)
    at = lax.rem(jnp.bitwise_xor(z, lax.div(z, 2)) + (k + 4), 4)
    return 2 * jnp.bitwise_xor(at, lax.div(at, 2)) + jnp.bitwise_xor(lax.rem(s, 2), e)


def ff_rank():
    return 2 * lax.rem(lax.axis_index("seq"), 2) + lax.rem(lax.axis_index("blk"), 2)


def ff_seat(k, e):
    z = lax.div(lax.axis_index("seq"), 2)
    at = lax.rem(jnp.bitwise_xor(z, lax.div(z, 2)) + (k + 4), 4)
    y = jnp.bitwise_xor(lax.div(lax.axis_index("blk"), 2), e)
    return 2 * jnp.bitwise_xor(at, lax.div(at, 2)) + y


def ff_column(rank, j, part):
    return (8 * (j // 2) + 4 * (rank // 2) + 2 * (j % 2) + rank % 2) * part


def ff_rows(seat, x, rows):
    at = 4 * lax.div(seat, 2) + 2 * x + lax.rem(seat, 2)
    return pl.ds(pl.multiple_of(2 * rows * at, 16), 2 * rows)


def norm_stats(u):
    center = u - jnp.mean(u, axis=-1, keepdims=True)
    inverse = lax.rsqrt(jnp.mean(center * center, axis=-1, keepdims=True) + epsilon)
    return center * inverse, inverse


def norm_pull(scaled, normed, inverse):
    return inverse * (
        scaled
        - jnp.mean(scaled, axis=-1, keepdims=True)
        - normed * jnp.mean(scaled * normed, axis=-1, keepdims=True)
    )


def pack_body(*refs):
    sources, firsts, seconds = refs[:6], refs[6:10], refs[10:14]
    scr, scr_ff, here, sems = refs[14], refs[15], refs[16:22], refs[22]
    copies = [
        pltpu.make_async_copy(source, target, sems.at[i])
        for i, (source, target) in enumerate(zip(sources, here))
    ]
    for copy in copies:
        copy.start()
    for copy in copies:
        copy.wait()
    q, kv, wo, gain, bias, ff = here
    rows, wide = q.shape[1], q.shape[2] // RANKS
    part = ff.shape[1] // (8 * RANKS)
    eye = lax.broadcasted_iota(jnp.int32, (rows, rows), 0) == lax.broadcasted_iota(
        jnp.int32, (rows, rows), 1
    )
    lane = lax.broadcasted_iota(jnp.int32, (rows, 64), 1)
    vec = jnp.zeros((rows, 64), f32)
    for j, row in enumerate((gain[0:1], gain[1:2], bias[0:1], bias[1:2])):
        column = jnp.sum(jnp.where(eye, row.astype(f32), 0.0), axis=1, keepdims=True)
        vec = jnp.where(lane == j, column, vec)
    for t in range(RANKS):
        cut = slice(wide * t, wide * t + wide)
        for j, piece in enumerate((q[0], q[1], kv[0], kv[1], q[2], q[3], wo[...])):
            scr[t, :, wide * j : wide * j + wide] = piece[:, cut]
        scr[t, :, 7 * wide :] = vec.astype(bf16)
        for j in range(8):
            at = ff_column(t, j, part)
            scr_ff[t, :, part * j : part * j + part] = ff[:, at : at + part]
    for k in range(RANKS):
        firsts[k][...] = scr[partner(k)]
        seconds[k][...] = scr_ff[jnp.bitwise_xor(ff_rank(), k)]


def arrange_own_body(p0, out):
    out[block(out, partner(0), p0.shape[0])] = p0[...].astype(f32)


def arrange_body(own, p1, p2, p3, slab, scr):
    rows = p1.shape[0]
    scr[...] = own[...]
    for k, p in ((1, p1), (2, p2), (3, p3)):
        scr[block(scr, partner(k), rows)] = p[...].astype(f32)
    slab[...] = scr[...].astype(bf16)


def arrange_ff_body(p0, p1, p2, p3, ff_out, slab, scr):
    rows, cols = p0.shape
    for k, p in enumerate((p0, p1, p2, p3)):
        scr[block(scr, jnp.bitwise_xor(ff_rank(), k), rows)] = p[...].astype(f32)
    slab[:, :cols] = scr[...].astype(bf16)
    slab[:, cols:] = ff_out[...]


def place_body(slots, *refs):
    shards, (wq, wo_first, rest) = refs[-3 - len(slots) : -3], refs[-3:]
    rows, first = shards[0].shape[0], wq.shape[1]
    for j, shard in zip(slots, shards):
        at = block(shard, ring_seat(-(j // 2), j % 2) if rows < wq.shape[0] else 0, rows)
        wq[at] = shard[:, :first]
        wo_first[at] = shard[:, first : first + 128]
        rest[at] = shard[:, first + 128 :]


def place_last_body(slots, *refs):
    wide = refs[0].shape[1] // 6
    ins, (wq, wo_first, rest, wo_col, norms) = refs[:-5], refs[-5:]
    place_body(slots, *ins, wq, wo_first, rest)
    width = wq.shape[0]
    half = width // 2
    tail = rest[...]
    wo_col[:width] = wo_first[...]
    wo_col[width:] = jnp.concatenate([tail[:half, : wide - 128], tail[half:, : wide - 128]], 1)
    norms[...] = tail.astype(f32).T[wide - 128 : wide - 120]


def place_ff_body(slots, *refs):
    shards, w1, w2 = refs[-2 - len(slots) : -2], refs[-2], refs[-1]
    rows, cut = shards[0].shape[0], w1.shape[1]
    if rows == w1.shape[0]:
        w1[...] = shards[0][:, :cut]
        w2[...] = shards[0][:, cut:]
        return
    for j, shard in zip(slots, shards):
        seat = ff_seat(-(j // 2), j % 2)
        for x in (0, 1):
            w1[ff_rows(seat, x, rows // 4)] = shard[rows // 2 * x : rows // 2 * (x + 1), :cut]
        w2[block(shard, seat, rows)] = shard[:, cut:]


def join_out_body(w0, w1, w2, w3, wo, scr):
    wide = wo.shape[1] // RANKS
    half = wo.shape[0] // 2
    for k, w in enumerate((w0, w1, w2, w3)):
        scr[partner(k)] = w[...]
    for t in range(RANKS):
        wo[:, wide * t : wide * t + 128] = scr[t, : 2 * half]
        tail = scr[t, 2 * half :]
        wo[:half, wide * t + 128 : wide * t + wide] = tail[:, : wide - 128]
        wo[half:, wide * t + 128 : wide * t + wide] = tail[:, wide - 128 :]


def join_rows_body(x0, x1, x2, x3, xw):
    local = x0.shape[0]
    for k, x in enumerate((x0, x1, x2, x3)):
        xw[block(xw, partner(k), local)] = x[...]


def attend_body(wide, factor, xw, xe, wq, segq, segk, c0, c1, c2, c3, qw, qe, kk, vv, p_ref, c_scr):
    words, ents = xw.shape[0], xe.shape[0]
    local = words // RANKS
    share = ents // RANKS
    hl = HEADS // RANKS
    dh = wide // hl
    rows = words + ents
    w = dot_nn(xw[...], wq[:, : 4 * wide])
    e_kv = dot_nn(xe[...], wq[:, 2 * wide : 4 * wide])
    e_q = dot_nn(xe[...], wq[:, 4 * wide :])
    qw[:words] = (w[:, :wide] * factor).astype(bf16)
    qe[:words] = (w[:, wide : 2 * wide] * factor).astype(bf16)
    kk[:words] = w[:, 2 * wide : 3 * wide].astype(bf16)
    vv[:words] = w[:, 3 * wide :].astype(bf16)
    qw[words:] = (e_q[:, :wide] * factor).astype(bf16)
    qe[words:] = (e_q[:, wide:] * factor).astype(bf16)
    kk[words:] = e_kv[:, :wide].astype(bf16)
    vv[words:] = e_kv[:, wide:].astype(bf16)
    values_t = vv[...].astype(f32).T.astype(bf16)
    lane_head = lax.broadcasted_iota(jnp.int32, (128, wide), 1) // dh
    segcol = segk[...]

    def query_block(i, carry):
        at = pl.ds(pl.multiple_of(i * 128, 128), 128)
        q_word, q_ent = qw[at], qe[at]
        zero = jnp.zeros_like(q_word)
        stack_w = jnp.concatenate([jnp.where(lane_head == h, q_word, zero) for h in range(hl)], 0)
        stack_e = jnp.concatenate([jnp.where(lane_head == h, q_ent, zero) for h in range(hl)], 0)
        s_w = dot_nt(kk[:words], stack_w)
        s_e = dot_nt(kk[words:], stack_e)
        allowed = segcol == segq[0:1, at]
        probs = []
        for h in range(hl):
            lanes = slice(128 * h, 128 * h + 128)
            s = jnp.concatenate([s_w[:, lanes], s_e[:, lanes]], 0)
            s = jnp.where(allowed, s, masked_score)
            top = jnp.max(s, axis=0, keepdims=True)
            e = jnp.exp(s - top)
            probs.append((e * (1.0 / jnp.sum(e, axis=0, keepdims=True))).astype(bf16))
        prob = jnp.concatenate(probs, 1)
        p_ref[i] = prob
        ctx = dot_nn(values_t, prob)
        ctx = jnp.concatenate(
            [ctx[dh * h : dh * h + dh, 128 * h : 128 * h + 128] for h in range(hl)], 0
        )
        c_scr[at] = ctx.T.astype(bf16)
        return carry

    lax.fori_loop(0, rows // 128, query_block, 0)
    b = lax.axis_index("blk")
    for k, out in enumerate((c0, c1, c2, c3)):
        to = jnp.bitwise_xor(b, k)
        out[:local] = c_scr[block(c_scr, to, local)]
        out[local:] = c_scr[pl.ds(pl.multiple_of(words + to * share, share), share)]


def mix_body(c0, c1, c2, c3, w0, w1, w2, w3, norms, xw, xe, hr, n1, i1, scr):
    b = lax.axis_index("blk")
    rows = c0.shape[0]
    width = xw.shape[1]
    share = rows - xw.shape[0]
    half = width // 2
    cs, ws = (c0, c1, c2, c3), (w0, w1, w2, w3)
    for rank in range(RANKS):

        @pl.when(b == rank)
        def _():
            ctx = jnp.concatenate([cs[rank ^ q][...] for q in range(RANKS)], 1)
            u = []
            for t in range(RANKS):
                w = ws[rank ^ t]
                low = dot_nn(ctx[:, :half], w[width:])[:, :64]
                high = dot_nn(ctx[:, half:], w[width:])[:, 64:]
                u += [dot_nn(ctx, w[:width]), low + high]
            scr[...] = jnp.concatenate(u, 1)

    u = scr[...] + jnp.concatenate([xw[...].astype(f32), xe[block(xe, b, share)].astype(f32)], 0)
    normed, inverse = norm_stats(u)
    n1[...] = normed
    i1[...] = inverse
    hr[...] = (normed * norms[0:1] + norms[2:3]).astype(bf16)


def feed_body(h0, h1, h2, h3, w1, w2, own, across, core, g_all, gp_all):
    outs = (own, core.at[1], across, core.at[0])
    for k, h in enumerate((h0, h1, h2, h3)):
        z = dot_nn(h[...], w1[...])
        cdf = 0.5 * (1.0 + lax.erf(z * 0.7071067811865476))
        g = (z * cdf).astype(bf16)
        g_all[k] = g
        gp_all[k] = (cdf + z * (0.3989422804014327 * jnp.exp(-0.5 * z * z))).astype(bf16)
        outs[k][...] = dot_nn(g, w2[...]).astype(outs[k].dtype)


def turn_body(f0, f1, f2, n1, norms, gw, ge, yw, ye, df, du2, sums):
    b = lax.axis_index("blk")
    local = gw.shape[0]
    rows = n1.shape[0]
    share = rows - local
    n = norms[...]
    u = n1[...] * n[0:1] + n[2:3]
    u = u + (f0[...] + f1[1].astype(f32) + f2[...].astype(f32))
    normed, inverse = norm_stats(u)
    y = (normed * n[1:2] + n[3:4]).astype(bf16)
    yw[...] = y[:local]
    ye[...] = y[local:]
    dy = jnp.concatenate([gw[...].astype(f32), ge[block(ge, b, share)].astype(f32)], 0)
    sums[...] = jnp.concatenate(
        [jnp.sum(dy * normed, axis=0, keepdims=True), jnp.sum(dy, axis=0, keepdims=True)]
        + [jnp.zeros((6, dy.shape[1]), f32)],
        0,
    )
    d = norm_pull(dy * n[1:2], normed, inverse)
    du2[...] = d
    df[...] = d.astype(bf16)


def feed_back_near_body(d0, d1, gp_all, w1, w2, own, beside, dz):
    for k, (d, out) in enumerate(((d0, own), (d1, beside))):
        z = (dot_nt(d[...], w2[...]) * gp_all[k].astype(f32)).astype(bf16)
        dz[k] = z
        out[...] = dot_nt(z, w1[...]).astype(out.dtype)


def feed_back_far_body(d2, d3, gp_all, w1, w2, beside, across, core, dz):
    core[1] = beside[...]
    for k, (d, out) in enumerate(((d2, across), (d3, core.at[0]))):
        z = (dot_nt(d[...], w2[...]) * gp_all[2 + k].astype(f32)).astype(bf16)
        dz[k] = z
        out[...] = dot_nt(z, w1[...]).astype(out.dtype)


def feed_grads_body(d0, d1, d2, d3, h0, h1, h2, h3, g_all, dz_near, dz_far, *refs):
    outs, g_in, g_out = refs[:-2], refs[-2], refs[-1]
    d = jnp.concatenate([x[...] for x in (d0, d1, d2, d3)], 0)
    h = jnp.concatenate([x[...] for x in (h0, h1, h2, h3)], 0)
    g = jnp.concatenate([g_all[k] for k in range(RANKS)], 0)
    z = jnp.concatenate([dz_near[0], dz_near[1], dz_far[0], dz_far[1]], 0)
    g_in[...] = dot_tn(h, z).astype(bf16)
    g_out[...] = dot_tn(g, d).astype(bf16)
    cut = g_in.shape[1]
    if len(outs) == 1:
        outs[0][:, :cut] = g_in[...]
        outs[0][:, cut:] = g_out[...]
        return
    for j, out in enumerate(outs):
        seat = ff_seat(j // 2, j % 2)
        rows = out.shape[0]
        for x in (0, 1):
            out[rows // 2 * x : rows // 2 * (x + 1), :cut] = g_in[ff_rows(seat, x, rows // 4)]
        out[:, cut:] = g_out[block(out, seat, rows)]


def norm_one_body(h0, h1, h2, du2, n1, i1, norms, two, wo, c0, c1, c2, c3, *refs):
    d0, d2, d3, core, du1, w_own, w_across, scr = refs
    wide = d0.shape[1]
    dh = du2[...] + (h0[...] + h1[1].astype(f32) + h2[...].astype(f32))
    width = dh.shape[1]
    normed = n1[...]
    d = norm_pull(dh * norms[0:1], normed, i1[...])
    du1[...] = d
    low = d.astype(bf16)
    dc = [dot_nt(low, wo[block(wo, partner(k), wide)]).astype(bf16) for k in range(RANKS)]
    d0[...] = dc[0]
    core[2 * width :, :wide] = dc[1]
    d2[...] = dc[2]
    d3[...] = dc[3]
    sums = jnp.concatenate(
        [jnp.sum(dh * normed, axis=0, keepdims=True), two[0:1]]
        + [jnp.sum(dh, axis=0, keepdims=True), two[1:2], jnp.zeros((124, width), f32)],
        0,
    )
    for k, c in enumerate((c0, c1, c2, c3)):
        g = dot_tn(c[...], low).astype(bf16)
        at = block(scr, partner(k), wide)
        for t in range(RANKS):
            scr[t, at, :wide] = g[:, wide * t : wide * t + wide]
    vec = sums.T.astype(bf16)
    for t in range(RANKS):
        scr[t, :, wide:] = vec[:, :64]
    w_own[...] = scr[partner(0)]
    core[:width] = scr[partner(3)]
    core[width : 2 * width] = scr[partner(1)]
    w_across[...] = scr[partner(2)]


def attend_back_body(factor, d0, core, d2, d3, qw, qe, kk, vv, p_ref, dqkv, dc, dqw, dqe, dk, dv):
    b = lax.axis_index("blk")
    rows, wide = qw.shape
    local = rows * 4 // 5 // RANKS
    words = local * RANKS
    share = (rows - words) // RANKS
    hl = HEADS // RANKS
    dh = wide // hl
    base = core.shape[0] - d0.shape[0]
    for k, d in enumerate((d0[...], core[base:, :wide], d2[...], d3[...])):
        to = jnp.bitwise_xor(b, k)
        dc[block(dc, to, local)] = d[:local]
        dc[pl.ds(pl.multiple_of(words + to * share, share), share)] = d[local:]
    keys_t = kk[...].astype(f32).T.astype(bf16)
    lane_head = lax.broadcasted_iota(jnp.int32, (128, wide), 1) // dh
    dk[...] = jnp.zeros_like(dk)
    dv[...] = jnp.zeros_like(dv)

    def query_block(i, carry):
        at = pl.ds(pl.multiple_of(i * 128, 128), 128)
        zero = jnp.zeros((128, wide), bf16)

        def stacked(x):
            return jnp.concatenate([jnp.where(lane_head == h, x, zero) for h in range(hl)], 0)

        stack_d = stacked(dc[at])
        prob = p_ref[i]
        dp = dot_nt(vv[...], stack_d)
        parts = []
        for h in range(hl):
            lanes = slice(128 * h, 128 * h + 128)
            p = prob[:, lanes].astype(f32)
            g = dp[:, lanes]
            delta = jnp.sum(p * g, axis=0, keepdims=True)
            parts.append((p * (g - delta)).astype(bf16))
        ds = jnp.concatenate(parts, 1)
        dv[...] += dot_nn(prob, stack_d)
        dk[:words] += dot_nn(ds[:words], stacked(qw[at]))
        dk[words:] += dot_nn(ds[words:], stacked(qe[at]))
        for keys, ds_part, out in ((keys_t[:, :words], ds[:words], dqw), (keys_t[:, words:], ds[words:], dqe)):
            t = dot_nn(keys, ds_part)
            t = jnp.concatenate(
                [t[dh * h : dh * h + dh, 128 * h : 128 * h + 128] for h in range(hl)], 0
            )
            out[at] = t.T
        return carry

    lax.fori_loop(0, rows // 128, query_block, 0)
    dqkv[:, :wide] = (dqw[...] * factor).astype(bf16)
    dqkv[:, wide : 2 * wide] = (dqe[...] * factor).astype(bf16)
    dqkv[:, 2 * wide : 3 * wide] = dk[...].astype(bf16)
    dqkv[:, 3 * wide :] = dv[...].astype(bf16)


def proj_grads_body(dqkv, xw, xe, o0, o1, o2, *refs):
    outs, scr = refs[:-1], refs[-1]
    words = xw.shape[0]
    out_rows = o0.shape[0]
    half = dqkv.shape[1] // 2
    w = dot_tn(xw[...], dqkv[:words])
    e = dot_tn(xe[...], dqkv[words:])
    scr[:, :half] = w[:, :half].astype(bf16)
    scr[:, half : 2 * half] = (w[:, half:] + e[:, half:]).astype(bf16)
    scr[:, 2 * half : 3 * half] = e[:, :half].astype(bf16)
    scr[:, 3 * half :] = (o0[...].astype(f32) + o1[out_rows : 2 * out_rows].astype(f32) + o2[...].astype(f32)).astype(bf16)
    for j, out in enumerate(outs):
        to = ring_seat(j // 2, j % 2) if len(outs) > 1 else 0
        out[...] = scr[block(scr, to, out.shape[0])]


def total_of(parts):
    return parts[0][...].astype(f32) + (parts[1][...].astype(f32) + parts[2][...].astype(f32))


def last_ff_body(a0, a1, a2, w_out, c0, c1, c2, c3, scr):
    rows = c0.shape[0]
    width = c0.shape[1]
    t = total_of((a0, a1, a2))
    w_out[...] = t[:, width:]
    scr[...] = t[:, :width]
    for k, c in enumerate((c0, c1, c2, c3)):
        c[...] = scr[block(scr, jnp.bitwise_xor(ff_rank(), k), rows)].astype(bf16)


def spread_ff_body(c0, c1, c2, c3, out, scr):
    part = out.shape[1] // (8 * RANKS)
    for k, c in enumerate((c0, c1, c2, c3)):
        scr[jnp.bitwise_xor(ff_rank(), k)] = c[...].astype(f32)
    for t in range(RANKS):
        for j in range(8):
            at = ff_column(t, j, part)
            out[:, at : at + part] = scr[t, :, part * j : part * j + part]


def last_body(a0, a1, a2, c0, c1, c2, c3, scr):
    rows = c0.shape[0]
    scr[...] = total_of((a0, a1, a2))
    for k, c in enumerate((c0, c1, c2, c3)):
        c[...] = scr[block(scr, partner(k), rows)].astype(bf16)


def finish_body(c0, c1, c2, c3, gq, gkv, go, gg, gb, scr):
    wide = go.shape[1] // RANKS
    for k, c in enumerate((c0, c1, c2, c3)):
        scr[partner(k)] = c[...].astype(f32)
    for t in range(RANKS):
        cut = slice(wide * t, wide * t + wide)
        for j, (out, i) in enumerate(((gq, 0), (gq, 1), (gkv, 0), (gkv, 1), (gq, 2), (gq, 3))):
            out[i, :, cut] = scr[t, :, wide * j : wide * j + wide]
        go[:, cut] = scr[t, :, 6 * wide : 7 * wide]
    at = 7 * wide + 64 - 128
    v = c0[:, at:].astype(f32).T
    gg[...] = v[64:66]
    gb[...] = v[66:68]


def input_body(dqkv, wq, du1, ye, own, across, core, part):
    b = lax.axis_index("blk")
    local, share = own.shape[0], ye.shape[0]
    words = RANKS * local
    half = dqkv.shape[1] // 2
    part[:words] = dot_nt(dqkv[:words], wq[:, : 2 * half])
    part[words:] = dot_nt(dqkv[words:, half:], wq[:, half : 2 * half]) + dot_nt(
        dqkv[words:, :half], wq[:, 2 * half :]
    )
    part[pl.ds(pl.multiple_of(words + b * share, share), share)] += du1[local:]
    own[...] = part[block(part, b, local)] + du1[:local]
    low = part[words:].astype(bf16)
    core[:local] = part[block(part, partner(3), local)].astype(bf16)
    core[local : 2 * local] = part[block(part, partner(1), local)].astype(bf16)
    core[2 * local : -share] = low
    core[-share:] = ye[...]
    across[:local] = part[block(part, partner(2), local)].astype(bf16)
    across[local:-share] = low
    across[-share:] = ye[...]


def input_pair_body(across, came, sent):
    share = sent.shape[0] - across.shape[0]
    local = came.shape[0] - across.shape[0]
    sent[:local] = (across[:local].astype(f32) + came[:local].astype(f32)).astype(bf16)
    pair = across[local:-share].astype(f32) + came[2 * local : -share].astype(f32)
    sent[local : -2 * share] = pair.astype(bf16)
    sent[-2 * share : -share] = across[-share:]
    sent[-share:] = came[-share:]


def input_sum_body(own, core, sent, came, gw, ge, ye):
    local = own.shape[0]
    share = ye.shape[0] // RANKS
    two = 2 * share
    gw[...] = own[...] + core[local : 2 * local].astype(f32) + came[:local].astype(f32)
    ge[...] = sent[local:-two].astype(f32) + came[local:-two].astype(f32)
    for k, rows in enumerate((sent[-two:-share], sent[-share:], came[-two:-share], came[-share:])):
        ye[block(ye, partner(k), share)] = rows


def swap(x, k):
    return lax.ppermute(x, "blk", [(i, i ^ k) for i in range(RANKS)])


def swapped(send):
    return [swap(send[k - 1], k) for k in (1, 2, 3)]


def spread(x):
    across = swap(x, 2)
    beside = swap(x, 1)
    return [beside, across, swap(across, 1)]


def plus(*parts):
    total = parts[0].astype(f32)
    for part in parts[1:]:
        total = total + part.astype(f32)
    return total.astype(bf16)


def over_x(x):
    return lax.ppermute(x, "seq", [(i, i ^ 1) for i in range(8)])


ring = (0, 1, 3, 2)


def swap_ff(x, k, direct):
    if not direct or k == 1:
        return swap(x, k)
    if k == 2:
        return over_x(x)
    return lax.ppermute(x, ("seq", "blk"), [(i, i ^ 5) for i in range(32)])


def along_ring(x, step=1):
    route = [(ring[i], ring[(i + step) % 4]) for i in range(4)]
    return lax.ppermute(x, "seq", [(2 * z + i, 2 * to + i) for z, to in route for i in (0, 1)])


def fence(*groups):
    return lax.optimization_barrier(groups)


def after(x, *before):
    return lax.optimization_barrier((x, before))[0]


def per_device(
    words,
    entities,
    segments,
    entity_counts,
    entity_anchor,
    query_weights,
    kv_weights,
    out_weight,
    ff_in,
    ff_out,
    norm_gain,
    norm_bias,
    grad_words,
    grad_entities,
):
    seqs = lax.axis_size("seq")
    direct = seqs == 8
    _, local, width = words.shape
    ents = entities.shape[1]
    share = ents // RANKS
    total = local * RANKS
    rows = total + ents
    mine = local + share
    wide = width // RANKS
    hl = HEADS // RANKS
    factor = (width // HEADS) ** (-0.5)
    part_rows = query_weights.shape[2]
    ff_part = ff_out.shape[1]
    ff = ff_part * seqs
    shards = 8 if direct else 1
    slab_cols = 7 * wide + 64
    xw_own, xe = words[0], entities[0]

    seg_ents = jnp.take_along_axis(segments, entity_anchor, axis=1)
    live = jnp.arange(ents, dtype=jnp.int32)[None, :] < entity_counts[:, None]
    segq = jnp.concatenate([segments, seg_ents], 1)
    segk = jnp.concatenate([segments, jnp.where(live, seg_ents, -1)], 1).T
    join_rows = call(join_rows_body, "join_rows", [((total, width), bf16)])

    if direct:
        pack = call(
            pack_body,
            "pack",
            [((part_rows, slab_cols), bf16)] * 4 + [((part_rows, ff), bf16)] * 4,
            [pltpu.VMEM((RANKS, part_rows, n), bf16) for n in (slab_cols, ff)]
            + [pltpu.VMEM((n, part_rows, width), bf16) for n in (4, 2)]
            + [pltpu.VMEM((part_rows, width), bf16)]
            + [pltpu.VMEM((2, part_rows), bf16)] * 2
            + [pltpu.VMEM((part_rows, RANKS * ff), bf16), pltpu.SemaphoreType.DMA((6,))],
            held=6,
            vmem=60,
        )
        pieces = pack(
            query_weights[0],
            kv_weights[0],
            out_weight[0],
            norm_gain[0],
            norm_bias[0],
            ff_in[0],
        )
        pieces, ff_pieces = pieces[:4], pieces[4:]
        own = call(
            arrange_own_body, "arrange_own", [((RANKS * part_rows, slab_cols), f32)]
        )(pieces[0])
        pieces = [own[0], *swapped(pieces[1:])]

        arrange = call(
            arrange_body,
            "arrange",
            [((RANKS * part_rows, slab_cols), bf16)],
            [pltpu.VMEM((RANKS * part_rows, slab_cols), f32)],
        )
        arrange_ff = call(
            arrange_ff_body,
            "arrange_ff",
            [((RANKS * part_rows, ff + width), bf16)],
            [pltpu.VMEM((RANKS * part_rows, ff), f32)],
        )
        (slab,) = arrange(*pieces)
        xw_own, slab = fence(xw_own, slab)
        xb, xa = swap(xw_own, 1), swap(xw_own, 2)
        x0, g1 = over_x(slab), along_ring(slab)
        g1, x0, xb, ff_pieces = fence(g1, x0, xb, ff_pieces)
        x1, g2 = over_x(g1), along_ring(g1)
        came = [swap_ff(ff_pieces[k], k, direct) for k in (1, 2, 3)]
        (ff_slab,) = arrange_ff(ff_pieces[0], *came, ff_out[0])
        g2, x1, ff_slab, xa = fence(g2, x1, ff_slab, xa)
        x2, g3 = over_x(g2), along_ring(g2)
        y0, xc = swap(ff_slab, 2), swap(xa, 1)
        g3, x2, xc, segq, segk = fence(g3, x2, xc, segq, segk)
        f1, x3 = along_ring(after(ff_slab, g3)), over_x(g3)
        (xw,) = join_rows(xw_own, xb, xa, xc)
        x3, f1, y0, xw = fence(x3, f1, y0, xw)
        f2 = along_ring(f1)
        slabs = [slab, x0, g1, x1, g2, x2, g3, x3]
    else:
        vec = jnp.concatenate([norm_gain[0], norm_bias[0]], 0).T
        vec = jnp.pad(vec, ((0, 0), (0, 60)))
        six = jnp.concatenate(
            [query_weights[0, :2], kv_weights[0], query_weights[0, 2:], out_weight], 0
        )
        six = six.reshape(7, part_rows, RANKS, wide).transpose(2, 1, 0, 3)
        six = six.reshape(RANKS, part_rows, 7 * wide)
        ff_cols = ff_in[0].reshape(part_rows, seqs, RANKS, ff_part).transpose(2, 0, 1, 3)
        ff_cols = ff_cols.reshape(RANKS, part_rows, ff)
        pack = jnp.concatenate(
            [six, jnp.broadcast_to(vec, (RANKS, part_rows, 64)), ff_cols], 2
        )
        pack = lax.all_to_all(pack, "blk", 0, 0, tiled=True).reshape(RANKS * part_rows, -1)
        pack = jnp.concatenate([pack, ff_out[0]], 1)
        pack = lax.all_gather(pack, "seq", axis=0, tiled=True)
        slabs, ff_slabs = [pack[:, :slab_cols]], [pack[:, slab_cols:]]
        (xw,) = join_rows(xw_own, *spread(xw_own))

    def place(slots, last, *args):
        outs = [((width, 6 * wide), bf16), ((width, 128), bf16), ((width, wide - 64), bf16)]
        if last:
            outs += [((width * 3 // 2, 128), bf16), ((8, width), f32)]
        body = place_last_body if last else place_body
        same = len(args) - len(slots)
        name = "place_last" if last else "place"
        return call(lambda *r: body(slots, *r), name, outs, same=same)(*args)

    if direct:
        ready = place((0, 1, 2, 3, 4), False, *slabs[:5])
        wq, _, _, wo_col, norms = place((5, 6, 7), True, *ready, *slabs[5:])
    else:
        blank = [jnp.zeros((width, n), bf16) for n in (6 * wide, 128, wide - 64)]
        wq, _, _, wo_col, norms = place((0,), True, *blank, slabs[0])
    wa, wb = swap(wo_col, 2), swap(wo_col, 1)
    attend = call(
        lambda *r: attend_body(wide, factor, *r),
        "attend",
        [((mine, wide), bf16)] * 4
        + [((rows, wide), bf16)] * 4
        + [((rows // 128, rows, 128 * hl), bf16)],
        [pltpu.VMEM((rows, wide), bf16)],
        us=7,
        vmem=16,
    )
    *ctx, qw, qe, kk, vv, prob = attend(xw, xe, wq, segq, segk)
    if direct:
        ctx = after(ctx, wb)
    ctx = [ctx[0]] + swapped(ctx[1:])
    wos = [wo_col, wb, wa, swap(after(wa, ctx), 1)]
    if direct:
        f3, y1 = along_ring(f2), swap(after(f1, ctx), 2)
        wos = after(wos, f3)
    join_out = call(
        join_out_body,
        "join_out",
        [((width, width), bf16)],
        [pltpu.VMEM((RANKS, width * 3 // 2, 128), bf16)],
    )
    (wo,) = join_out(*wos)
    mix = call(
        mix_body,
        "mix",
        [((mine, width), bf16), ((mine, width), f32), ((mine, 1), f32)],
        [pltpu.VMEM((mine, width), f32)],
    )
    hr, n1, i1 = mix(*ctx, *wos, norms, xw_own, xe)
    across, beside = swap_ff(hr, 2, direct), swap(hr, 1)
    if direct:
        fb, y2 = along_ring(after(y0, hr), -1), swap(after(f2, hr), 2)
        across = after(across, y1)
        ff_slabs = [ff_slab, y0, f1, y1, f2, y2, f3, fb]
    hs = [hr, beside, across, swap(across, 1)]
    def place_ff(slots, *args):
        outs = [((width, ff), bf16), ((ff, width), bf16)]
        same = len(args) - len(slots)
        return call(lambda *r: place_ff_body(slots, *r), "place_ff", outs, same=same)(*args)

    if direct:
        early = (0, 1, 2, 3, 4)
        ready = place_ff(early, *(ff_slabs[j] for j in early))
        w1, w2 = place_ff((5, 6, 7), *ready, *ff_slabs[5:])
    else:
        w1, w2 = place_ff((0,), ff_slabs[0])
    feed = call(
        feed_body,
        "feed",
        [((mine, width), f32), ((mine, width), bf16), ((2, mine, width), bf16)]
        + [((RANKS, mine, ff), bf16)] * 2,
        us=3,
        vmem=14,
    )
    own, across, core, g_all, gp_all = feed(*hs, w1, w2)
    core = swap(core, 1)
    fs = [own, core, swap_ff(plus(across, core[0]), 2, direct)]
    turn = call(
        turn_body,
        "turn",
        [((local, width), bf16), ((share, width), bf16), ((mine, width), bf16)]
        + [((mine, width), f32), ((8, width), f32)],
    )
    yw, ye, df, du2, sums = turn(*fs, n1, norms, grad_words[0], grad_entities[0])

    across, beside = swap_ff(df, 2, direct), swap(df, 1)
    ds = [df, beside, across, swap(across, 1)]
    half_dz = ((2, mine, ff), bf16)
    feed_back_near = call(
        feed_back_near_body,
        "feed_back_near",
        [((mine, width), f32), ((mine, width), bf16), half_dz],
        vmem=12,
    )
    feed_back_far = call(
        feed_back_far_body,
        "feed_back_far",
        [((mine, width), bf16), ((2, mine, width), bf16), half_dz],
        vmem=12,
    )
    own, beside, dz_near = feed_back_near(*ds[:2], gp_all, w1, w2)
    across, core, dz_far = feed_back_far(*ds[2:], gp_all, w1, w2, beside)
    core = swap(core, 1)
    feed_grads = call(
        feed_grads_body,
        "feed_grads",
        [((width // shards, ff + width), bf16)] * shards,
        [pltpu.VMEM((width, ff), bf16), pltpu.VMEM((ff, width), bf16)],
        us=3,
        vmem=16,
    )
    ff_chunks = feed_grads(*ds, *hs, g_all, dz_near, dz_far)
    sent = plus(across, after(core, ff_chunks)[0])
    dhs = [own, core, swap_ff(sent, 2, direct)]
    if direct:
        fz, fy = along_ring(ff_chunks[2], -1), swap(ff_chunks[5], 2)
        dhs[2] = after(dhs[2], fz, fy)
        fz = along_ring(plus(ff_chunks[4], fz, fy), -1)

    norm_one = call(
        norm_one_body,
        "norm_one",
        [((mine, wide), bf16)] * 3
        + [((2 * width + mine, wide + 64), bf16), ((mine, width), f32)]
        + [((width, wide + 64), bf16)] * 2,
        [pltpu.VMEM((RANKS, width, wide + 64), bf16)],
        vmem=12,
    )
    d0, d2, d3, core, du1, wo_own, across = norm_one(
        *dhs, du2, n1, i1, norms, sums, wo, *ctx
    )
    dcs = [d0, swap(core, 1), swap(d2, 2), swap(d3, 3)]
    sent = plus(across, after(dcs[1], dcs[2], dcs[3])[:width])
    outs = [wo_own, dcs[1], swap(sent, 2)]
    if direct:
        fb = along_ring(after(ff_chunks[3], du1))
    dcs = after(dcs, sent)
    attend_back = call(
        lambda *r: attend_back_body(factor, *r),
        "attend_back",
        [((rows, 4 * wide), bf16)],
        [pltpu.VMEM((rows, wide), bf16)] + [pltpu.VMEM((rows, wide), f32)] * 4,
        us=7,
        vmem=16,
    )
    (dqkv,) = attend_back(*dcs, qw, qe, kk, vv, prob)
    to_input = call(
        input_body,
        "to_input",
        [((local, width), f32)]
        + [((n * local + ents + share, width), bf16) for n in (1, 2)],
        [pltpu.VMEM((rows, width), f32)],
        us=2,
        vmem=12,
    )
    own, across, core = to_input(dqkv, wq, du1, ye)
    if direct:
        own = after(own, fb)
        fz = along_ring(plus(ff_chunks[6], after(fz, dqkv)), -1)
        fc = along_ring(after(ff_chunks[7], dqkv), -1)
    core = swap(core, 1)
    proj_grads = call(
        proj_grads_body,
        "proj_grads",
        [((width // shards, slab_cols), bf16)] * shards,
        [pltpu.VMEM((width, slab_cols), bf16)],
        us=2,
        vmem=14,
    )
    chunks = proj_grads(after(dqkv, own), xw, xe, *outs)
    if direct:
        part = plus(chunks[2], after(over_x(chunks[3]), fz, fc))
        fy = swap(plus(ff_chunks[1], fb, after(fc, part)), 2)
        cx, cz = over_x(after(chunks[5], part)), along_ring(part, -1)
        core = after(core, part)
    (sent,) = call(input_pair_body, "input_pair", [((local + ents + 2 * share, width), bf16)])(across, core)
    came = swap(sent, 2)
    input_sum = call(
        input_sum_body,
        "input_sum",
        [((local, width), f32), ((ents, width), f32), ((ents, width), bf16)],
    )
    if not direct:
        gxw, gxe, ye = input_sum(own, core, sent, came)

    if direct:
        last_ff = call(
            last_ff_body,
            "last_ff",
            [((ff_part, width), f32)] + [((part_rows, ff), bf16)] * 4,
            [pltpu.VMEM((RANKS * part_rows, ff), f32)],
        )
        part = plus(chunks[4], cz, cx)
        cx, cz = over_x(after(chunks[7], part)), along_ring(part, -1)
        grad_ff_out, *back = last_ff(ff_chunks[0], after(fz, part), fy)
        part = plus(chunks[6], after(cz, came), cx)
        cx, cz = over_x(after(chunks[1], part)), along_ring(part, -1)
        back = [back[0]] + [swap_ff(back[k], k, direct) for k in (1, 2, 3)]
        spread_ff = call(
            spread_ff_body,
            "spread_ff",
            [((part_rows, RANKS * ff), f32)],
            [pltpu.VMEM((RANKS, part_rows, ff), f32)],
        )
        (grad_ff_in,) = spread_ff(*back)
        gxw, gxe, ye = input_sum(own, core, sent, after(came, part))
        last = call(
            last_body,
            "last",
            [((part_rows, slab_cols), bf16)] * 4,
            [pltpu.VMEM((RANKS * part_rows, slab_cols), f32)],
        )
        back = last(chunks[0], after(cz, grad_ff_in, gxw), cx)
        back = [back[0]] + swapped(back[1:])
        finish = call(
            finish_body,
            "finish",
            [((4, part_rows, width), f32), ((2, part_rows, width), f32), ((part_rows, width), f32)]
            + [((2, part_rows), f32)] * 2,
            [pltpu.VMEM((RANKS, part_rows, slab_cols), f32)],
        )
        grad_query, grad_kv, grad_out, grad_gain, grad_bias = finish(*back)
    else:
        both = jnp.concatenate([chunks[0], ff_chunks[0]], 1)
        both = lax.psum_scatter(both, "seq", scatter_dimension=0, tiled=True)
        grad_ff_out = both[:, slab_cols + ff :].astype(f32)
        both = both[:, : slab_cols + ff].reshape(RANKS, part_rows, slab_cols + ff)
        both = lax.all_to_all(both, "blk", 0, 0, tiled=True).astype(f32)
        seven = both[:, :, : 7 * wide].reshape(RANKS, part_rows, 7, wide)
        seven = seven.transpose(2, 1, 0, 3).reshape(7, part_rows, width)
        grad_query = jnp.concatenate([seven[:2], seven[4:6]], 0)
        grad_kv, grad_out = seven[2:4], seven[6]
        vecs = both[0, :, 7 * wide : 7 * wide + 4].T
        grad_gain, grad_bias = vecs[:2], vecs[2:]
        grad_ff_in = both[:, :, slab_cols:].reshape(RANKS, part_rows, seqs, ff_part)
        grad_ff_in = grad_ff_in.transpose(1, 2, 0, 3).reshape(part_rows, RANKS * ff)
    return (
        yw[None],
        ye[None],
        gxw[None],
        gxe[None],
        grad_query[None],
        grad_kv[None],
        grad_out[None],
        grad_ff_in[None],
        grad_ff_out[None],
        grad_gain[None],
        grad_bias[None],
    )


def solution(mesh):
    placed = (
        P("seq", "blk", None),
        P("seq", None, None),
        P("seq", None),
        P("seq"),
        P("seq", None),
        P(None, None, ("seq", "blk"), None),
        P(None, None, ("seq", "blk"), None),
        P(None, ("seq", "blk"), None),
        P(None, ("seq", "blk"), None),
        P(None, ("seq", "blk"), None),
        P(None, None, ("seq", "blk")),
        P(None, None, ("seq", "blk")),
        P("seq", "blk", None),
        P("seq", None, None),
    )
    return jax.shard_map(
        per_device,
        mesh=mesh,
        in_specs=placed,
        out_specs=(
            P("seq", "blk", None),
            P("seq", None, None),
            P("seq", "blk", None),
            P("seq", None, None),
            P(None, None, ("seq", "blk"), None),
            P(None, None, ("seq", "blk"), None),
            P(None, ("seq", "blk"), None),
            P(None, ("seq", "blk"), None),
            P(None, ("seq", "blk"), None),
            P(None, None, ("seq", "blk")),
            P(None, None, ("seq", "blk")),
        ),
        check_vma=False,
    )
```

```python
import jax
import jax.numpy as jnp
from jax import lax
from jax.experimental import pallas as pl
from jax.experimental.pallas import tpu as pltpu
from jax.sharding import PartitionSpec as P

HEADS = 12
RANKS = 4
epsilon = 1e-05
masked_score = -1e30
bf16 = jnp.bfloat16
f32 = jnp.float32


def dot_nn(a, b):
    return jnp.dot(a, b, preferred_element_type=f32)


def dot_nt(a, b):
    return lax.dot_general(a, b, (((1,), (1,)), ((), ())), preferred_element_type=f32)


def dot_tn(a, b):
    return lax.dot_general(a, b, (((0,), (0,)), ((), ())), preferred_element_type=f32)


def block(ref, index, size):
    return pl.ds(pl.multiple_of(index * size, size), size)


def call(body, name, outs, scratch=(), vmem=10, us=1, held=0, same=0):
    def run(*args):
        return pl.pallas_call(
            body,
            name=name,
            out_shape=[jax.ShapeDtypeStruct(s, t) for s, t in outs],
            in_specs=[pl.BlockSpec(memory_space=pltpu.HBM)] * held
            + [pl.BlockSpec(memory_space=pltpu.VMEM)] * (len(args) - held),
            out_specs=[pl.BlockSpec(memory_space=pltpu.VMEM)] * len(outs),
            scratch_shapes=list(scratch),
            input_output_aliases={i: i for i in range(same)},
            compiler_params=pltpu.CompilerParams(vmem_limit_bytes=vmem << 20),
            cost_estimate=pl.CostEstimate(
                flops=int(us * 1e6), bytes_accessed=int(us * 1e3), transcendentals=0
            ),
        )(*args)

    return run


def partner(k):
    return jnp.bitwise_xor(lax.axis_index("blk"), k)


def ring_seat(k, e):
    s = lax.axis_index("seq")
    z = lax.div(s, 2)
    at = lax.rem(jnp.bitwise_xor(z, lax.div(z, 2)) + (k + 4), 4)
    return 2 * jnp.bitwise_xor(at, lax.div(at, 2)) + jnp.bitwise_xor(lax.rem(s, 2), e)


def ff_rank():
    return 2 * lax.rem(lax.axis_index("seq"), 2) + lax.rem(lax.axis_index("blk"), 2)


def ff_seat(k, e):
    z = lax.div(lax.axis_index("seq"), 2)
    at = lax.rem(jnp.bitwise_xor(z, lax.div(z, 2)) + (k + 4), 4)
    y = jnp.bitwise_xor(lax.div(lax.axis_index("blk"), 2), e)
    return 2 * jnp.bitwise_xor(at, lax.div(at, 2)) + y


def ff_column(rank, j, part):
    return (8 * (j // 2) + 4 * (rank // 2) + 2 * (j % 2) + rank % 2) * part


def ff_rows(seat, x, rows):
    at = 4 * lax.div(seat, 2) + 2 * x + lax.rem(seat, 2)
    return pl.ds(pl.multiple_of(2 * rows * at, 16), 2 * rows)


def norm_stats(u):
    center = u - jnp.mean(u, axis=-1, keepdims=True)
    inverse = lax.rsqrt(jnp.mean(center * center, axis=-1, keepdims=True) + epsilon)
    return center * inverse, inverse


def norm_pull(scaled, normed, inverse):
    return inverse * (
        scaled
        - jnp.mean(scaled, axis=-1, keepdims=True)
        - normed * jnp.mean(scaled * normed, axis=-1, keepdims=True)
    )


def fetch(refs, sems):
    half = len(refs) // 2
    copies = [
        pltpu.make_async_copy(source, target, sems.at[i])
        for i, (source, target) in enumerate(zip(refs[:half], refs[half:]))
    ]
    for copy in copies:
        copy.start()
    for copy in copies:
        copy.wait()


def pack_body(*refs):
    sources, outs, scr, here, sems = refs[:5], refs[5:9], refs[9], refs[10:15], refs[15]
    fetch((*sources, *here), sems)
    q, kv, wo, gain, bias = here
    rows, wide = q.shape[1], q.shape[2] // RANKS
    eye = lax.broadcasted_iota(jnp.int32, (rows, rows), 0) == lax.broadcasted_iota(
        jnp.int32, (rows, rows), 1
    )
    lane = lax.broadcasted_iota(jnp.int32, (rows, 64), 1)
    vec = jnp.zeros((rows, 64), f32)
    for j, row in enumerate((gain[0:1], gain[1:2], bias[0:1], bias[1:2])):
        column = jnp.sum(jnp.where(eye, row.astype(f32), 0.0), axis=1, keepdims=True)
        vec = jnp.where(lane == j, column, vec)
    for t in range(RANKS):
        cut = slice(wide * t, wide * t + wide)
        for j, piece in enumerate((q[0], q[1], kv[0], kv[1], q[2], q[3], wo[...])):
            scr[t, :, wide * j : wide * j + wide] = piece[:, cut]
        scr[t, :, 7 * wide :] = vec.astype(bf16)
    for k in range(RANKS):
        outs[k][...] = scr[partner(k)]


def pack_ff_body(ff, *refs):
    outs, scr = refs[:RANKS], refs[RANKS]
    part = ff.shape[1] // (8 * RANKS)
    for t in range(RANKS):
        for j in range(8):
            at = ff_column(t, j, part)
            scr[t, :, part * j : part * j + part] = ff[:, at : at + part]
    for k in range(RANKS):
        outs[k][...] = scr[jnp.bitwise_xor(ff_rank(), k)]


def arrange_own_body(p0, out):
    out[block(out, partner(0), p0.shape[0])] = p0[...].astype(f32)


def arrange_body(own, p1, p2, p3, slab, scr):
    rows = p1.shape[0]
    scr[...] = own[...]
    for k, p in ((1, p1), (2, p2), (3, p3)):
        scr[block(scr, partner(k), rows)] = p[...].astype(f32)
    slab[...] = scr[...].astype(bf16)


def arrange_ff_body(p0, p1, p2, p3, ff_out, slab, scr):
    rows, cols = p0.shape
    for k, p in enumerate((p0, p1, p2, p3)):
        scr[block(scr, jnp.bitwise_xor(ff_rank(), k), rows)] = p[...].astype(f32)
    slab[:, :cols] = scr[...].astype(bf16)
    slab[:, cols:] = ff_out[...]


def place_body(slots, *refs):
    shards, (wq, wo_first, rest) = refs[-3 - len(slots) : -3], refs[-3:]
    rows, first = shards[0].shape[0], wq.shape[1]
    for j, shard in zip(slots, shards):
        at = block(shard, ring_seat(-(j // 2), j % 2) if rows < wq.shape[0] else 0, rows)
        wq[at] = shard[:, :first]
        wo_first[at] = shard[:, first : first + 128]
        rest[at] = shard[:, first + 128 :]


def place_last_body(slots, *refs):
    wide = refs[0].shape[1] // 6
    ins, (wq, wo_first, rest, wo_col, norms) = refs[:-5], refs[-5:]
    place_body(slots, *ins, wq, wo_first, rest)
    width = wq.shape[0]
    half = width // 2
    tail = rest[...]
    wo_col[:width] = wo_first[...]
    wo_col[width:] = jnp.concatenate([tail[:half, : wide - 128], tail[half:, : wide - 128]], 1)
    norms[...] = tail.astype(f32).T[wide - 128 : wide - 120]


def place_ff_body(slots, *refs):
    shards, w1, w2 = refs[-2 - len(slots) : -2], refs[-2], refs[-1]
    rows, cut = shards[0].shape[0], w1.shape[1]
    if rows == w1.shape[0]:
        w1[...] = shards[0][:, :cut]
        w2[...] = shards[0][:, cut:]
        return
    for j, shard in zip(slots, shards):
        seat = ff_seat(-(j // 2), j % 2)
        for x in (0, 1):
            w1[ff_rows(seat, x, rows // 4)] = shard[rows // 2 * x : rows // 2 * (x + 1), :cut]
        w2[block(shard, seat, rows)] = shard[:, cut:]


def join_out_body(w0, w1, w2, w3, wo, scr):
    wide = wo.shape[1] // RANKS
    half = wo.shape[0] // 2
    for k, w in enumerate((w0, w1, w2, w3)):
        scr[partner(k)] = w[...]
    for t in range(RANKS):
        wo[:, wide * t : wide * t + 128] = scr[t, : 2 * half]
        tail = scr[t, 2 * half :]
        wo[:half, wide * t + 128 : wide * t + wide] = tail[:, : wide - 128]
        wo[half:, wide * t + 128 : wide * t + wide] = tail[:, wide - 128 :]


def join_rows_body(x0, x1, x2, x3, xw):
    local = x0.shape[0]
    for k, x in enumerate((x0, x1, x2, x3)):
        xw[block(xw, partner(k), local)] = x[...]


def attend_body(wide, factor, xw, xe, wq, segq, segk, c0, c1, c2, c3, qw, qe, kk, vv, p_ref, c_scr):
    words, ents = xw.shape[0], xe.shape[0]
    local = words // RANKS
    share = ents // RANKS
    hl = HEADS // RANKS
    dh = wide // hl
    rows = words + ents
    w = dot_nn(xw[...], wq[:, : 4 * wide])
    e_kv = dot_nn(xe[...], wq[:, 2 * wide : 4 * wide])
    e_q = dot_nn(xe[...], wq[:, 4 * wide :])
    qw[:words] = (w[:, :wide] * factor).astype(bf16)
    qe[:words] = (w[:, wide : 2 * wide] * factor).astype(bf16)
    kk[:words] = w[:, 2 * wide : 3 * wide].astype(bf16)
    vv[:words] = w[:, 3 * wide :].astype(bf16)
    qw[words:] = (e_q[:, :wide] * factor).astype(bf16)
    qe[words:] = (e_q[:, wide:] * factor).astype(bf16)
    kk[words:] = e_kv[:, :wide].astype(bf16)
    vv[words:] = e_kv[:, wide:].astype(bf16)
    values_t = vv[...].astype(f32).T.astype(bf16)
    lane_head = lax.broadcasted_iota(jnp.int32, (128, wide), 1) // dh
    segcol = segk[...]

    def query_block(i, carry):
        at = pl.ds(pl.multiple_of(i * 128, 128), 128)
        q_word, q_ent = qw[at], qe[at]
        zero = jnp.zeros_like(q_word)
        stack_w = jnp.concatenate([jnp.where(lane_head == h, q_word, zero) for h in range(hl)], 0)
        stack_e = jnp.concatenate([jnp.where(lane_head == h, q_ent, zero) for h in range(hl)], 0)
        s_w = dot_nt(kk[:words], stack_w)
        s_e = dot_nt(kk[words:], stack_e)
        allowed = segcol == segq[0:1, at]
        probs = []
        for h in range(hl):
            lanes = slice(128 * h, 128 * h + 128)
            s = jnp.concatenate([s_w[:, lanes], s_e[:, lanes]], 0)
            s = jnp.where(allowed, s, masked_score)
            top = jnp.max(s, axis=0, keepdims=True)
            e = jnp.exp(s - top)
            probs.append((e * (1.0 / jnp.sum(e, axis=0, keepdims=True))).astype(bf16))
        prob = jnp.concatenate(probs, 1)
        p_ref[i] = prob
        ctx = dot_nn(values_t, prob)
        ctx = jnp.concatenate(
            [ctx[dh * h : dh * h + dh, 128 * h : 128 * h + 128] for h in range(hl)], 0
        )
        c_scr[at] = ctx.T.astype(bf16)
        return carry

    lax.fori_loop(0, rows // 128, query_block, 0, unroll=True)
    b = lax.axis_index("blk")
    for k, out in enumerate((c0, c1, c2, c3)):
        to = jnp.bitwise_xor(b, k)
        out[:local] = c_scr[block(c_scr, to, local)]
        out[local:] = c_scr[pl.ds(pl.multiple_of(words + to * share, share), share)]


def mix_body(c0, c1, c2, c3, wo, norms, xw, xe, hr, n1, i1):
    b = lax.axis_index("blk")
    wide = c0.shape[1]
    share = hr.shape[0] - xw.shape[0]
    u = jnp.concatenate([xw[...].astype(f32), xe[block(xe, b, share)].astype(f32)], 0)
    for k, c in enumerate((c0, c1, c2, c3)):
        u = u + dot_nn(c[...], wo[block(wo, partner(k), wide)])
    normed, inverse = norm_stats(u)
    n1[...] = normed
    i1[...] = inverse
    hr[...] = (normed * norms[0:1] + norms[2:3]).astype(bf16)


def feed_body(h0, h1, h2, h3, w1, w2, own, across, core, g_all, gp_all):
    outs = (own, core.at[1], across, core.at[0])
    for k, h in enumerate((h0, h1, h2, h3)):
        z = dot_nn(h[...], w1[...])
        cdf = 0.5 * (1.0 + lax.erf(z * 0.7071067811865476))
        g = (z * cdf).astype(bf16)
        g_all[k] = g
        gp_all[k] = (cdf + z * (0.3989422804014327 * jnp.exp(-0.5 * z * z))).astype(bf16)
        outs[k][...] = dot_nn(g, w2[...]).astype(outs[k].dtype)


def turn_body(f0, f1, f2, n1, norms, gw, ge, yw, ye, df, du2, sums):
    b = lax.axis_index("blk")
    local = gw.shape[0]
    rows = n1.shape[0]
    share = rows - local
    n = norms[...]
    u = n1[...] * n[0:1] + n[2:3]
    u = u + (f0[...] + f1[1].astype(f32) + f2[...].astype(f32))
    normed, inverse = norm_stats(u)
    y = (normed * n[1:2] + n[3:4]).astype(bf16)
    yw[...] = y[:local]
    ye[...] = y[local:]
    dy = jnp.concatenate([gw[...].astype(f32), ge[block(ge, b, share)].astype(f32)], 0)
    sums[...] = jnp.concatenate(
        [jnp.sum(dy * normed, axis=0, keepdims=True), jnp.sum(dy, axis=0, keepdims=True)]
        + [jnp.zeros((6, dy.shape[1]), f32)],
        0,
    )
    d = norm_pull(dy * n[1:2], normed, inverse)
    du2[...] = d
    df[...] = d.astype(bf16)


def feed_back_near_body(d0, d1, gp_all, w1, w2, own, beside, dz):
    for k, (d, out) in enumerate(((d0, own), (d1, beside))):
        z = (dot_nt(d[...], w2[...]) * gp_all[k].astype(f32)).astype(bf16)
        dz[k] = z
        out[...] = dot_nt(z, w1[...]).astype(out.dtype)


def feed_back_far_body(d2, d3, gp_all, w1, w2, beside, across, core, dz):
    core[1] = beside[...]
    for k, (d, out) in enumerate(((d2, across), (d3, core.at[0]))):
        z = (dot_nt(d[...], w2[...]) * gp_all[2 + k].astype(f32)).astype(bf16)
        dz[k] = z
        out[...] = dot_nt(z, w1[...]).astype(out.dtype)


def feed_grads_body(d0, d1, d2, d3, h0, h1, h2, h3, g_all, dz_near, dz_far, *refs):
    outs, g_in, g_out = refs[:-2], refs[-2], refs[-1]
    d = jnp.concatenate([x[...] for x in (d0, d1, d2, d3)], 0)
    h = jnp.concatenate([x[...] for x in (h0, h1, h2, h3)], 0)
    g = jnp.concatenate([g_all[k] for k in range(RANKS)], 0)
    z = jnp.concatenate([dz_near[0], dz_near[1], dz_far[0], dz_far[1]], 0)
    g_in[...] = dot_tn(h, z).astype(bf16)
    g_out[...] = dot_tn(g, d).astype(bf16)
    cut = g_in.shape[1]
    if len(outs) == 1:
        outs[0][:, :cut] = g_in[...]
        outs[0][:, cut:] = g_out[...]
        return
    for j, out in enumerate(outs):
        seat = ff_seat(j // 2, j % 2)
        rows = out.shape[0]
        for x in (0, 1):
            out[rows // 2 * x : rows // 2 * (x + 1), :cut] = g_in[ff_rows(seat, x, rows // 4)]
        out[:, cut:] = g_out[block(out, seat, rows)]


def norm_one_body(h0, h1, h2, du2, n1, i1, norms, two, wo, c0, c1, c2, c3, *refs):
    d0, d2, d3, core, du1, w_own, w_across, scr = refs
    wide = d0.shape[1]
    dh = du2[...] + (h0[...] + h1[1].astype(f32) + h2[...].astype(f32))
    width = dh.shape[1]
    normed = n1[...]
    d = norm_pull(dh * norms[0:1], normed, i1[...])
    du1[...] = d
    low = d.astype(bf16)
    dc = [dot_nt(low, wo[block(wo, partner(k), wide)]).astype(bf16) for k in range(RANKS)]
    d0[...] = dc[0]
    core[2 * width :, :wide] = dc[1]
    d2[...] = dc[2]
    d3[...] = dc[3]
    sums = jnp.concatenate(
        [jnp.sum(dh * normed, axis=0, keepdims=True), two[0:1]]
        + [jnp.sum(dh, axis=0, keepdims=True), two[1:2], jnp.zeros((124, width), f32)],
        0,
    )
    for k, c in enumerate((c0, c1, c2, c3)):
        g = dot_tn(c[...], low).astype(bf16)
        at = block(scr, partner(k), wide)
        for t in range(RANKS):
            scr[t, at, :wide] = g[:, wide * t : wide * t + wide]
    vec = sums.T.astype(bf16)
    for t in range(RANKS):
        scr[t, :, wide:] = vec[:, :64]
    w_own[...] = scr[partner(0)]
    core[:width] = scr[partner(3)]
    core[width : 2 * width] = scr[partner(1)]
    w_across[...] = scr[partner(2)]


def attend_back_body(factor, d0, core, d2, d3, qw, qe, kk, vv, p_ref, dqkv, dc, dqw, dqe, dk, dv):
    b = lax.axis_index("blk")
    rows, wide = qw.shape
    local = rows * 4 // 5 // RANKS
    words = local * RANKS
    share = (rows - words) // RANKS
    hl = HEADS // RANKS
    dh = wide // hl
    base = core.shape[0] - d0.shape[0]
    for k, d in enumerate((d0[...], core[base:, :wide], d2[...], d3[...])):
        to = jnp.bitwise_xor(b, k)
        dc[block(dc, to, local)] = d[:local]
        dc[pl.ds(pl.multiple_of(words + to * share, share), share)] = d[local:]
    keys_t = kk[...].astype(f32).T.astype(bf16)
    lane_head = lax.broadcasted_iota(jnp.int32, (128, wide), 1) // dh
    dk[...] = jnp.zeros_like(dk)
    dv[...] = jnp.zeros_like(dv)

    def query_block(i, carry):
        at = pl.ds(pl.multiple_of(i * 128, 128), 128)
        zero = jnp.zeros((128, wide), bf16)

        def stacked(x):
            return jnp.concatenate([jnp.where(lane_head == h, x, zero) for h in range(hl)], 0)

        stack_d = stacked(dc[at])
        prob = p_ref[i]
        dp = dot_nt(vv[...], stack_d)
        parts = []
        for h in range(hl):
            lanes = slice(128 * h, 128 * h + 128)
            p = prob[:, lanes].astype(f32)
            g = dp[:, lanes]
            delta = jnp.sum(p * g, axis=0, keepdims=True)
            parts.append((p * (g - delta)).astype(bf16))
        ds = jnp.concatenate(parts, 1)
        dv[...] += dot_nn(prob, stack_d)
        dk[:words] += dot_nn(ds[:words], stacked(qw[at]))
        dk[words:] += dot_nn(ds[words:], stacked(qe[at]))
        for keys, ds_part, out in ((keys_t[:, :words], ds[:words], dqw), (keys_t[:, words:], ds[words:], dqe)):
            t = dot_nn(keys, ds_part)
            t = jnp.concatenate(
                [t[dh * h : dh * h + dh, 128 * h : 128 * h + 128] for h in range(hl)], 0
            )
            out[at] = t.T
        return carry

    lax.fori_loop(0, rows // 128, query_block, 0, unroll=True)
    dqkv[:, :wide] = (dqw[...] * factor).astype(bf16)
    dqkv[:, wide : 2 * wide] = (dqe[...] * factor).astype(bf16)
    dqkv[:, 2 * wide : 3 * wide] = dk[...].astype(bf16)
    dqkv[:, 3 * wide :] = dv[...].astype(bf16)


def proj_grads_body(dqkv, xw, xe, o0, o1, o2, *refs):
    outs, scr = refs[:-1], refs[-1]
    words = xw.shape[0]
    out_rows = o0.shape[0]
    half = dqkv.shape[1] // 2
    w = dot_tn(xw[...], dqkv[:words])
    e = dot_tn(xe[...], dqkv[words:])
    scr[:, :half] = w[:, :half].astype(bf16)
    scr[:, half : 2 * half] = (w[:, half:] + e[:, half:]).astype(bf16)
    scr[:, 2 * half : 3 * half] = e[:, :half].astype(bf16)
    scr[:, 3 * half :] = (o0[...].astype(f32) + o1[out_rows : 2 * out_rows].astype(f32) + o2[...].astype(f32)).astype(bf16)
    for j, out in enumerate(outs):
        to = ring_seat(j // 2, j % 2) if len(outs) > 1 else 0
        out[...] = scr[block(scr, to, out.shape[0])]


def total_of(*parts):
    total = parts[0][...].astype(f32)
    for part in parts[1:]:
        total = total + part[...].astype(f32)
    return total


def last_ff_body(a0, a1, a2, a3, w_out, c0, c1, c2, c3, scr):
    rows = c0.shape[0]
    width = c0.shape[1]
    t = total_of(a0, a1, a2, a3)
    w_out[...] = t[:, width:]
    scr[...] = t[:, :width]
    for k, c in enumerate((c0, c1, c2, c3)):
        c[...] = scr[block(scr, jnp.bitwise_xor(ff_rank(), k), rows)].astype(bf16)


def spread_ff_body(c0, c1, c2, c3, out, scr):
    part = out.shape[1] // (8 * RANKS)
    for k, c in enumerate((c0, c1, c2, c3)):
        scr[jnp.bitwise_xor(ff_rank(), k)] = c[...].astype(f32)
    for t in range(RANKS):
        for j in range(8):
            at = ff_column(t, j, part)
            out[:, at : at + part] = scr[t, :, part * j : part * j + part]


def last_body(a0, a1, a2, c0, c1, c2, c3, scr):
    rows = c0.shape[0]
    scr[...] = total_of(a0, a1, a2)
    for k, c in enumerate((c0, c1, c2, c3)):
        c[...] = scr[block(scr, partner(k), rows)].astype(bf16)


def finish_body(c0, c1, c2, c3, gq, gkv, go, gg, gb, scr):
    wide = go.shape[1] // RANKS
    for k, c in enumerate((c0, c1, c2, c3)):
        scr[partner(k)] = c[...].astype(f32)
    for t in range(RANKS):
        cut = slice(wide * t, wide * t + wide)
        for j, (out, i) in enumerate(((gq, 0), (gq, 1), (gkv, 0), (gkv, 1), (gq, 2), (gq, 3))):
            out[i, :, cut] = scr[t, :, wide * j : wide * j + wide]
        go[:, cut] = scr[t, :, 6 * wide : 7 * wide]
    at = 7 * wide + 64 - 128
    v = c0[:, at:].astype(f32).T
    gg[...] = v[64:66]
    gb[...] = v[66:68]


def input_body(dqkv, wq, du1, ye, own, across, core, part):
    b = lax.axis_index("blk")
    local, share = own.shape[0], ye.shape[0]
    words = RANKS * local
    half = dqkv.shape[1] // 2
    part[:words] = dot_nt(dqkv[:words], wq[:, : 2 * half])
    part[words:] = dot_nt(dqkv[words:, half:], wq[:, half : 2 * half]) + dot_nt(
        dqkv[words:, :half], wq[:, 2 * half :]
    )
    part[pl.ds(pl.multiple_of(words + b * share, share), share)] += du1[local:]
    own[...] = part[block(part, b, local)] + du1[:local]
    low = part[words:].astype(bf16)
    core[:local] = part[block(part, partner(3), local)].astype(bf16)
    core[local : 2 * local] = part[block(part, partner(1), local)].astype(bf16)
    core[2 * local : -share] = low
    core[-share:] = ye[...]
    across[:local] = part[block(part, partner(2), local)].astype(bf16)
    across[local:-share] = low
    across[-share:] = ye[...]


def input_pair_body(across, came, sent):
    share = sent.shape[0] - across.shape[0]
    local = came.shape[0] - across.shape[0]
    sent[:local] = (across[:local].astype(f32) + came[:local].astype(f32)).astype(bf16)
    pair = across[local:-share].astype(f32) + came[2 * local : -share].astype(f32)
    sent[local : -2 * share] = pair.astype(bf16)
    sent[-2 * share : -share] = across[-share:]
    sent[-share:] = came[-share:]


def input_sum_body(own, core, sent, came, gw, ge, ye):
    local = own.shape[0]
    share = ye.shape[0] // RANKS
    two = 2 * share
    gw[...] = own[...] + core[local : 2 * local].astype(f32) + came[:local].astype(f32)
    ge[...] = sent[local:-two].astype(f32) + came[local:-two].astype(f32)
    for k, rows in enumerate((sent[-two:-share], sent[-share:], came[-two:-share], came[-share:])):
        ye[block(ye, partner(k), share)] = rows


def swap(x, k):
    return lax.ppermute(x, "blk", [(i, i ^ k) for i in range(RANKS)])


def swapped(send):
    return [swap(send[k - 1], k) for k in (1, 2, 3)]


def spread(x):
    across = swap(x, 2)
    beside = swap(x, 1)
    return [beside, across, swap(across, 1)]


def plus(*parts):
    total = parts[0].astype(f32)
    for part in parts[1:]:
        total = total + part.astype(f32)
    return total.astype(bf16)


def over_x(x):
    return lax.ppermute(x, "seq", [(i, i ^ 1) for i in range(8)])


ring = (0, 1, 3, 2)


def swap_ff(x, k, direct):
    if not direct or k == 1:
        return swap(x, k)
    if k == 2:
        return over_x(x)
    return lax.ppermute(x, ("seq", "blk"), [(i, i ^ 5) for i in range(32)])


def along_ring(x, step=1):
    route = [(ring[i], ring[(i + step) % 4]) for i in range(4)]
    return lax.ppermute(x, "seq", [(2 * z + i, 2 * to + i) for z, to in route for i in (0, 1)])


def fence(*groups):
    return lax.optimization_barrier(groups)


def after(x, *before):
    return lax.optimization_barrier((x, before))[0]


def per_device(
    words,
    entities,
    segments,
    entity_counts,
    entity_anchor,
    query_weights,
    kv_weights,
    out_weight,
    ff_in,
    ff_out,
    norm_gain,
    norm_bias,
    grad_words,
    grad_entities,
):
    seqs = lax.axis_size("seq")
    direct = seqs == 8
    _, local, width = words.shape
    ents = entities.shape[1]
    share = ents // RANKS
    total = local * RANKS
    rows = total + ents
    mine = local + share
    wide = width // RANKS
    hl = HEADS // RANKS
    factor = (width // HEADS) ** (-0.5)
    part_rows = query_weights.shape[2]
    ff_part = ff_out.shape[1]
    ff = ff_part * seqs
    shards = 8 if direct else 1
    slab_cols = 7 * wide + 64
    xw_own, xe = words[0], entities[0]

    seg_ents = jnp.take_along_axis(segments, entity_anchor, axis=1)
    live = jnp.arange(ents, dtype=jnp.int32)[None, :] < entity_counts[:, None]
    segq = jnp.concatenate([segments, seg_ents], 1)
    segk = jnp.concatenate([segments, jnp.where(live, seg_ents, -1)], 1).T
    join_rows = call(join_rows_body, "join_rows", [((total, width), bf16)])

    if direct:
        pack = call(
            pack_body,
            "pack",
            [((part_rows, slab_cols), bf16)] * 4,
            [pltpu.VMEM((RANKS, part_rows, slab_cols), bf16)]
            + [pltpu.VMEM((n, part_rows, width), bf16) for n in (4, 2)]
            + [pltpu.VMEM((part_rows, width), bf16)]
            + [pltpu.VMEM((2, part_rows), bf16)] * 2
            + [pltpu.SemaphoreType.DMA((5,))],
            held=5,
            vmem=60,
        )
        pieces = pack(
            query_weights[0], kv_weights[0], out_weight[0], norm_gain[0], norm_bias[0]
        )
        pack_ff = call(
            pack_ff_body,
            "pack_ff",
            [((part_rows, ff), bf16)] * 4,
            [pltpu.VMEM((RANKS, part_rows, ff), bf16)],
        )
        ff_pieces = pack_ff(after(ff_in[0], pieces[0]))
        own = call(
            arrange_own_body, "arrange_own", [((RANKS * part_rows, slab_cols), f32)]
        )(pieces[0])
        pieces = [own[0], *swapped(pieces[1:])]

        arrange = call(
            arrange_body,
            "arrange",
            [((RANKS * part_rows, slab_cols), bf16)],
            [pltpu.VMEM((RANKS * part_rows, slab_cols), f32)],
        )
        arrange_ff = call(
            arrange_ff_body,
            "arrange_ff",
            [((RANKS * part_rows, ff + width), bf16)],
            [pltpu.VMEM((RANKS * part_rows, ff), f32)],
        )
        (slab,) = arrange(*pieces)
        xw_own, slab = fence(xw_own, slab)
        xb, xa = swap(xw_own, 1), swap(xw_own, 2)
        x0, g1 = over_x(slab), along_ring(slab)
        g1, x0, xb, ff_pieces = fence(g1, x0, xb, ff_pieces)
        x1, g2 = over_x(g1), along_ring(g1)
        came = [swap_ff(ff_pieces[k], k, direct) for k in (1, 2, 3)]
        (ff_slab,) = arrange_ff(ff_pieces[0], *came, ff_out[0])
        g2, x1, ff_slab, xa = fence(g2, x1, ff_slab, xa)
        x2, g3 = over_x(g2), along_ring(g2)
        y0, xc = swap(ff_slab, 2), swap(xa, 1)
        g3, x2, xc, segq, segk = fence(g3, x2, xc, segq, segk)
        f1, x3 = along_ring(after(ff_slab, g3)), over_x(g3)
        (xw,) = join_rows(xw_own, xb, xa, xc)
        x3, f1, y0, xw = fence(x3, f1, y0, xw)
        f2 = along_ring(f1)
        slabs = [slab, x0, g1, x1, g2, x2, g3, x3]
    else:
        vec = jnp.concatenate([norm_gain[0], norm_bias[0]], 0).T
        vec = jnp.pad(vec, ((0, 0), (0, 60)))
        six = jnp.concatenate(
            [query_weights[0, :2], kv_weights[0], query_weights[0, 2:], out_weight], 0
        )
        six = six.reshape(7, part_rows, RANKS, wide).transpose(2, 1, 0, 3)
        six = six.reshape(RANKS, part_rows, 7 * wide)
        ff_cols = ff_in[0].reshape(part_rows, seqs, RANKS, ff_part).transpose(2, 0, 1, 3)
        ff_cols = ff_cols.reshape(RANKS, part_rows, ff)
        pack = jnp.concatenate(
            [six, jnp.broadcast_to(vec, (RANKS, part_rows, 64)), ff_cols], 2
        )
        pack = lax.all_to_all(pack, "blk", 0, 0, tiled=True).reshape(RANKS * part_rows, -1)
        pack = jnp.concatenate([pack, ff_out[0]], 1)
        pack = lax.all_gather(pack, "seq", axis=0, tiled=True)
        slabs, ff_slabs = [pack[:, :slab_cols]], [pack[:, slab_cols:]]
        (xw,) = join_rows(xw_own, *spread(xw_own))

    def place(slots, last, *args):
        outs = [((width, 6 * wide), bf16), ((width, 128), bf16), ((width, wide - 64), bf16)]
        if last:
            outs += [((width * 3 // 2, 128), bf16), ((8, width), f32)]
        body = place_last_body if last else place_body
        same = len(args) - len(slots)
        name = "place_last" if last else "place"
        return call(lambda *r: body(slots, *r), name, outs, same=same)(*args)

    if direct:
        ready = place((0, 1, 2, 3, 4), False, *slabs[:5])
        wq, _, _, wo_col, norms = place((5, 6, 7), True, *ready, *slabs[5:])
    else:
        blank = [jnp.zeros((width, n), bf16) for n in (6 * wide, 128, wide - 64)]
        wq, _, _, wo_col, norms = place((0,), True, *blank, slabs[0])
    wa, wb = swap(wo_col, 2), swap(wo_col, 1)
    attend = call(
        lambda *r: attend_body(wide, factor, *r),
        "attend",
        [((mine, wide), bf16)] * 4
        + [((rows, wide), bf16)] * 4
        + [((rows // 128, rows, 128 * hl), bf16)],
        [pltpu.VMEM((rows, wide), bf16)],
        us=7,
        vmem=16,
    )
    *ctx, qw, qe, kk, vv, prob = attend(xw, xe, wq, segq, segk)
    if direct:
        ctx = after(ctx, wb)
    ctx = [ctx[0]] + swapped(ctx[1:])
    wos = [wo_col, wb, wa, swap(after(wa, ctx), 1)]
    if direct:
        f3, y1 = along_ring(f2), swap(after(f1, ctx), 2)
    join_out = call(
        join_out_body,
        "join_out",
        [((width, width), bf16)],
        [pltpu.VMEM((RANKS, width * 3 // 2, 128), bf16)],
    )
    (wo,) = join_out(*wos)
    mix = call(
        mix_body,
        "mix",
        [((mine, width), bf16), ((mine, width), f32), ((mine, 1), f32)],
    )
    hr, n1, i1 = mix(*ctx, after(wo, f3) if direct else wo, norms, xw_own, xe)

    def place_ff(slots, *args):
        outs = [((width, ff), bf16), ((ff, width), bf16)]
        same = len(args) - len(slots)
        return call(lambda *r: place_ff_body(slots, *r), "place_ff", outs, same=same)(*args)

    across, beside = swap_ff(hr, 2, direct), swap(hr, 1)
    if direct:
        fb, y2 = along_ring(after(y0, hr), -1), swap(after(f2, hr), 2)
        ready = place_ff((0, 1, 2, 3, 4, 6), ff_slab, y0, f1, y1, f2, f3)
        across = after(across, ready)
        ff_slabs = [ff_slab, y0, f1, y1, f2, y2, f3, fb]
    hs = [hr, beside, across, swap(across, 1)]
    if direct:
        w1, w2 = place_ff((5, 7), *ready, ff_slabs[5], ff_slabs[7])
    else:
        w1, w2 = place_ff((0,), ff_slabs[0])
    feed = call(
        feed_body,
        "feed",
        [((mine, width), f32), ((mine, width), bf16), ((2, mine, width), bf16)]
        + [((RANKS, mine, ff), bf16)] * 2,
        us=3,
        vmem=14,
    )
    own, across, core, g_all, gp_all = feed(*hs, w1, w2)
    core = swap(core, 1)
    fs = [own, core, swap_ff(plus(across, core[0]), 2, direct)]
    turn = call(
        turn_body,
        "turn",
        [((local, width), bf16), ((share, width), bf16), ((mine, width), bf16)]
        + [((mine, width), f32), ((8, width), f32)],
    )
    yw, ye, df, du2, sums = turn(*fs, n1, norms, grad_words[0], grad_entities[0])

    across, beside = swap_ff(df, 2, direct), swap(df, 1)
    ds = [df, beside, across, swap(across, 1)]
    half_dz = ((2, mine, ff), bf16)
    feed_back_near = call(
        feed_back_near_body,
        "feed_back_near",
        [((mine, width), f32), ((mine, width), bf16), half_dz],
        vmem=12,
    )
    feed_back_far = call(
        feed_back_far_body,
        "feed_back_far",
        [((mine, width), bf16), ((2, mine, width), bf16), half_dz],
        vmem=12,
    )
    own, beside, dz_near = feed_back_near(*ds[:2], gp_all, w1, w2)
    across, core, dz_far = feed_back_far(*ds[2:], gp_all, w1, w2, beside)
    core = swap(core, 1)
    feed_grads = call(
        feed_grads_body,
        "feed_grads",
        [((width // shards, ff + width), bf16)] * shards,
        [pltpu.VMEM((width, ff), bf16), pltpu.VMEM((ff, width), bf16)],
        us=3,
        vmem=16,
    )
    ff_chunks = feed_grads(*ds, *hs, g_all, dz_near, dz_far)
    sent = plus(across, after(core, ff_chunks)[0])
    dhs = [own, core, swap_ff(sent, 2, direct)]
    if direct:
        ff0, ff1, ff2, ff3, ff4, ff5, ff6, ff7 = ff_chunks
        fy, fz = swap(ff5, 2), along_ring(ff2)
        part = plus(ff4, fy)
        dhs[2] = after(dhs[2], part, fz)
        fl = along_ring(part, -1)

    norm_one = call(
        norm_one_body,
        "norm_one",
        [((mine, wide), bf16)] * 3
        + [((2 * width + mine, wide + 64), bf16), ((mine, width), f32)]
        + [((width, wide + 64), bf16)] * 2,
        [pltpu.VMEM((RANKS, width, wide + 64), bf16)],
        vmem=12,
    )
    d0, d2, d3, core, du1, wo_own, across = norm_one(
        *dhs, du2, n1, i1, norms, sums, wo, *ctx
    )
    dcs = [d0, swap(core, 1), swap(d2, 2), swap(d3, 3)]
    sent = plus(across, after(dcs[1], dcs[2], dcs[3])[:width])
    outs = [wo_own, dcs[1], swap(sent, 2)]
    if direct:
        fb, fc = along_ring(after(ff3, du1)), along_ring(after(ff7, du1), -1)
    dcs = after(dcs, sent)
    attend_back = call(
        lambda *r: attend_back_body(factor, *r),
        "attend_back",
        [((rows, 4 * wide), bf16)],
        [pltpu.VMEM((rows, wide), bf16)] + [pltpu.VMEM((rows, wide), f32)] * 4,
        us=7,
        vmem=16,
    )
    (dqkv,) = attend_back(*dcs, qw, qe, kk, vv, prob)
    to_input = call(
        input_body,
        "to_input",
        [((local, width), f32)]
        + [((n * local + ents + share, width), bf16) for n in (1, 2)],
        [pltpu.VMEM((rows, width), f32)],
        us=2,
        vmem=12,
    )
    own, across, core = to_input(dqkv, wq, du1, ye)
    if direct:
        own = after(own, fl)
        fl = along_ring(plus(ff6, after(fl, dqkv)), -1)
    core = swap(core, 1)
    proj_grads = call(
        proj_grads_body,
        "proj_grads",
        [((width // shards, slab_cols), bf16)] * shards,
        [pltpu.VMEM((width, slab_cols), bf16)],
        us=2,
        vmem=14,
    )
    chunks = proj_grads(after(dqkv, own), xw, xe, *outs)
    if direct:
        part = plus(chunks[2], after(over_x(chunks[3]), fl, fb, fc))
        fy = swap(plus(ff1, fb, after(fc, part)), 2)
        cx, cz = over_x(after(chunks[5], part)), along_ring(part, -1)
        core = after(core, part)
    (sent,) = call(input_pair_body, "input_pair", [((local + ents + 2 * share, width), bf16)])(across, core)
    came = swap(sent, 2)
    input_sum = call(
        input_sum_body,
        "input_sum",
        [((local, width), f32), ((ents, width), f32), ((ents, width), bf16)],
    )
    if not direct:
        gxw, gxe, ye = input_sum(own, core, sent, came)

    if direct:
        last_ff = call(
            last_ff_body,
            "last_ff",
            [((ff_part, width), f32)] + [((part_rows, ff), bf16)] * 4,
            [pltpu.VMEM((RANKS * part_rows, ff), f32)],
        )
        part = plus(chunks[4], cz, cx)
        cx, cz = over_x(after(chunks[7], part)), along_ring(part, -1)
        grad_ff_out, *back = last_ff(ff0, fz, fl, after(fy, part))
        part = plus(chunks[6], after(cz, came), cx)
        cx, cz = over_x(after(chunks[1], part)), along_ring(part, -1)
        back = [back[0]] + [swap_ff(back[k], k, direct) for k in (1, 2, 3)]
        spread_ff = call(
            spread_ff_body,
            "spread_ff",
            [((part_rows, RANKS * ff), f32)],
            [pltpu.VMEM((RANKS, part_rows, ff), f32)],
        )
        (grad_ff_in,) = spread_ff(*back)
        gxw, gxe, ye = input_sum(own, core, sent, after(came, part))
        last = call(
            last_body,
            "last",
            [((part_rows, slab_cols), bf16)] * 4,
            [pltpu.VMEM((RANKS * part_rows, slab_cols), f32)],
        )
        back = last(chunks[0], after(cz, grad_ff_in, gxw), cx)
        back = [back[0]] + swapped(back[1:])
        finish = call(
            finish_body,
            "finish",
            [((4, part_rows, width), f32), ((2, part_rows, width), f32), ((part_rows, width), f32)]
            + [((2, part_rows), f32)] * 2,
            [pltpu.VMEM((RANKS, part_rows, slab_cols), f32)],
        )
        grad_query, grad_kv, grad_out, grad_gain, grad_bias = finish(*back)
    else:
        both = jnp.concatenate([chunks[0], ff_chunks[0]], 1)
        both = lax.psum_scatter(both, "seq", scatter_dimension=0, tiled=True)
        grad_ff_out = both[:, slab_cols + ff :].astype(f32)
        both = both[:, : slab_cols + ff].reshape(RANKS, part_rows, slab_cols + ff)
        both = lax.all_to_all(both, "blk", 0, 0, tiled=True).astype(f32)
        seven = both[:, :, : 7 * wide].reshape(RANKS, part_rows, 7, wide)
        seven = seven.transpose(2, 1, 0, 3).reshape(7, part_rows, width)
        grad_query = jnp.concatenate([seven[:2], seven[4:6]], 0)
        grad_kv, grad_out = seven[2:4], seven[6]
        vecs = both[0, :, 7 * wide : 7 * wide + 4].T
        grad_gain, grad_bias = vecs[:2], vecs[2:]
        grad_ff_in = both[:, :, slab_cols:].reshape(RANKS, part_rows, seqs, ff_part)
        grad_ff_in = grad_ff_in.transpose(1, 2, 0, 3).reshape(part_rows, RANKS * ff)
    return (
        yw[None],
        ye[None],
        gxw[None],
        gxe[None],
        grad_query[None],
        grad_kv[None],
        grad_out[None],
        grad_ff_in[None],
        grad_ff_out[None],
        grad_gain[None],
        grad_bias[None],
    )


def solution(mesh):
    placed = (
        P("seq", "blk", None),
        P("seq", None, None),
        P("seq", None),
        P("seq"),
        P("seq", None),
        P(None, None, ("seq", "blk"), None),
        P(None, None, ("seq", "blk"), None),
        P(None, ("seq", "blk"), None),
        P(None, ("seq", "blk"), None),
        P(None, ("seq", "blk"), None),
        P(None, None, ("seq", "blk")),
        P(None, None, ("seq", "blk")),
        P("seq", "blk", None),
        P("seq", None, None),
    )
    return jax.shard_map(
        per_device,
        mesh=mesh,
        in_specs=placed,
        out_specs=(
            P("seq", "blk", None),
            P("seq", None, None),
            P("seq", "blk", None),
            P("seq", None, None),
            P(None, None, ("seq", "blk"), None),
            P(None, None, ("seq", "blk"), None),
            P(None, ("seq", "blk"), None),
            P(None, ("seq", "blk"), None),
            P(None, ("seq", "blk"), None),
            P(None, None, ("seq", "blk")),
            P(None, None, ("seq", "blk")),
        ),
        check_vma=False,
    )
```

```python
import jax
import jax.numpy as jnp
from jax import lax
from jax.experimental import pallas as pl
from jax.experimental.pallas import tpu as pltpu
from jax.sharding import PartitionSpec as P

HEADS = 12
RANKS = 4
epsilon = 1e-05
masked_score = -1e30
bf16 = jnp.bfloat16
f32 = jnp.float32


def dot_nn(a, b):
    return jnp.dot(a, b, preferred_element_type=f32)


def dot_nt(a, b):
    return lax.dot_general(a, b, (((1,), (1,)), ((), ())), preferred_element_type=f32)


def dot_tn(a, b):
    return lax.dot_general(a, b, (((0,), (0,)), ((), ())), preferred_element_type=f32)


def block(ref, index, size):
    return pl.ds(pl.multiple_of(index * size, size), size)


def call(body, name, outs, scratch=(), vmem=10, us=1, held=0, same=0):
    def run(*args):
        return pl.pallas_call(
            body,
            name=name,
            out_shape=[jax.ShapeDtypeStruct(s, t) for s, t in outs],
            in_specs=[pl.BlockSpec(memory_space=pltpu.HBM)] * held
            + [pl.BlockSpec(memory_space=pltpu.VMEM)] * (len(args) - held),
            out_specs=[pl.BlockSpec(memory_space=pltpu.VMEM)] * len(outs),
            scratch_shapes=list(scratch),
            input_output_aliases={i: i for i in range(same)},
            compiler_params=pltpu.CompilerParams(vmem_limit_bytes=vmem << 20),
            cost_estimate=pl.CostEstimate(
                flops=int(us * 1e6), bytes_accessed=int(us * 1e3), transcendentals=0
            ),
        )(*args)

    return run


def partner(k):
    return jnp.bitwise_xor(lax.axis_index("blk"), k)


def ring_seat(k, e):
    s = lax.axis_index("seq")
    z = lax.div(s, 2)
    at = lax.rem(jnp.bitwise_xor(z, lax.div(z, 2)) + (k + 4), 4)
    return 2 * jnp.bitwise_xor(at, lax.div(at, 2)) + jnp.bitwise_xor(lax.rem(s, 2), e)


def ff_rank():
    return 2 * lax.rem(lax.axis_index("seq"), 2) + lax.rem(lax.axis_index("blk"), 2)


def ff_seat(k, e):
    z = lax.div(lax.axis_index("seq"), 2)
    at = lax.rem(jnp.bitwise_xor(z, lax.div(z, 2)) + (k + 4), 4)
    y = jnp.bitwise_xor(lax.div(lax.axis_index("blk"), 2), e)
    return 2 * jnp.bitwise_xor(at, lax.div(at, 2)) + y


def ff_column(rank, j, part):
    return (8 * (j // 2) + 4 * (rank // 2) + 2 * (j % 2) + rank % 2) * part


def ff_rows(seat, x, rows):
    at = 4 * lax.div(seat, 2) + 2 * x + lax.rem(seat, 2)
    return pl.ds(pl.multiple_of(2 * rows * at, 16), 2 * rows)


def norm_stats(u):
    center = u - jnp.mean(u, axis=-1, keepdims=True)
    inverse = lax.rsqrt(jnp.mean(center * center, axis=-1, keepdims=True) + epsilon)
    return center * inverse, inverse


def norm_pull(scaled, normed, inverse):
    return inverse * (
        scaled
        - jnp.mean(scaled, axis=-1, keepdims=True)
        - normed * jnp.mean(scaled * normed, axis=-1, keepdims=True)
    )


def fetch(refs, sems):
    half = len(refs) // 2
    copies = [
        pltpu.make_async_copy(source, target, sems.at[i])
        for i, (source, target) in enumerate(zip(refs[:half], refs[half:]))
    ]
    for copy in copies:
        copy.start()
    for copy in copies:
        copy.wait()


def pack_body(*refs):
    sources, outs, scr, here, sems = refs[:5], refs[5:9], refs[9], refs[10:15], refs[15]
    fetch((*sources, *here), sems)
    q, kv, wo, gain, bias = here
    rows, wide = q.shape[1], q.shape[2] // RANKS
    eye = lax.broadcasted_iota(jnp.int32, (rows, rows), 0) == lax.broadcasted_iota(
        jnp.int32, (rows, rows), 1
    )
    lane = lax.broadcasted_iota(jnp.int32, (rows, 64), 1)
    vec = jnp.zeros((rows, 64), f32)
    for j, row in enumerate((gain[0:1], gain[1:2], bias[0:1], bias[1:2])):
        column = jnp.sum(jnp.where(eye, row.astype(f32), 0.0), axis=1, keepdims=True)
        vec = jnp.where(lane == j, column, vec)
    for t in range(RANKS):
        cut = slice(wide * t, wide * t + wide)
        for j, piece in enumerate((q[0], q[1], kv[0], kv[1], q[2], q[3], wo[...])):
            scr[t, :, wide * j : wide * j + wide] = piece[:, cut]
        scr[t, :, 7 * wide :] = vec.astype(bf16)
    for k in range(RANKS):
        outs[k][...] = scr[partner(k)]


def pack_ff_body(ff, *refs):
    outs, scr = refs[:RANKS], refs[RANKS]
    part = ff.shape[1] // (8 * RANKS)
    for t in range(RANKS):
        for j in range(8):
            at = ff_column(t, j, part)
            scr[t, :, part * j : part * j + part] = ff[:, at : at + part]
    for k in range(RANKS):
        outs[k][...] = scr[jnp.bitwise_xor(ff_rank(), k)]


def arrange_own_body(p0, out):
    out[block(out, partner(0), p0.shape[0])] = p0[...].astype(f32)


def arrange_body(own, p1, p2, p3, slab, scr):
    rows = p1.shape[0]
    scr[...] = own[...]
    for k, p in ((1, p1), (2, p2), (3, p3)):
        scr[block(scr, partner(k), rows)] = p[...].astype(f32)
    slab[...] = scr[...].astype(bf16)


def arrange_ff_body(p0, p1, p2, p3, ff_out, slab, scr):
    rows, cols = p0.shape
    for k, p in enumerate((p0, p1, p2, p3)):
        scr[block(scr, jnp.bitwise_xor(ff_rank(), k), rows)] = p[...].astype(f32)
    slab[:, :cols] = scr[...].astype(bf16)
    slab[:, cols:] = ff_out[...]


def place_body(slots, *refs):
    shards, (wq, wo_first, rest) = refs[-3 - len(slots) : -3], refs[-3:]
    rows, first = shards[0].shape[0], wq.shape[1]
    for j, shard in zip(slots, shards):
        at = block(shard, ring_seat(-(j // 2), j % 2) if rows < wq.shape[0] else 0, rows)
        wq[at] = shard[:, :first]
        wo_first[at] = shard[:, first : first + 128]
        rest[at] = shard[:, first + 128 :]


def place_last_body(slots, *refs):
    wide = refs[0].shape[1] // 6
    ins, (wq, wo_first, rest, wo_col, norms) = refs[:-5], refs[-5:]
    place_body(slots, *ins, wq, wo_first, rest)
    width = wq.shape[0]
    half = width // 2
    tail = rest[...]
    wo_col[:width] = wo_first[...]
    wo_col[width:] = jnp.concatenate([tail[:half, : wide - 128], tail[half:, : wide - 128]], 1)
    norms[...] = tail.astype(f32).T[wide - 128 : wide - 120]


def place_ff_body(slots, *refs):
    shards, w1, w2 = refs[-2 - len(slots) : -2], refs[-2], refs[-1]
    rows, cut = shards[0].shape[0], w1.shape[1]
    if rows == w1.shape[0]:
        w1[...] = shards[0][:, :cut]
        w2[...] = shards[0][:, cut:]
        return
    for j, shard in zip(slots, shards):
        seat = ff_seat(-(j // 2), j % 2)
        for x in (0, 1):
            w1[ff_rows(seat, x, rows // 4)] = shard[rows // 2 * x : rows // 2 * (x + 1), :cut]
        w2[block(shard, seat, rows)] = shard[:, cut:]


def join_out_body(w0, w1, w2, w3, wo, scr):
    wide = wo.shape[1] // RANKS
    half = wo.shape[0] // 2
    for k, w in enumerate((w0, w1, w2, w3)):
        scr[partner(k)] = w[...]
    for t in range(RANKS):
        wo[:, wide * t : wide * t + 128] = scr[t, : 2 * half]
        tail = scr[t, 2 * half :]
        wo[:half, wide * t + 128 : wide * t + wide] = tail[:, : wide - 128]
        wo[half:, wide * t + 128 : wide * t + wide] = tail[:, wide - 128 :]


def join_rows_body(x0, x1, x2, x3, xw):
    local = x0.shape[0]
    for k, x in enumerate((x0, x1, x2, x3)):
        xw[block(xw, partner(k), local)] = x[...]


def attend_body(wide, factor, xw, xe, wq, segq, segk, c0, c1, c2, c3, qw, qe, kk, vv, p_ref, c_scr):
    words, ents = xw.shape[0], xe.shape[0]
    local = words // RANKS
    share = ents // RANKS
    hl = HEADS // RANKS
    dh = wide // hl
    rows = words + ents
    w = dot_nn(xw[...], wq[:, : 4 * wide])
    e_kv = dot_nn(xe[...], wq[:, 2 * wide : 4 * wide])
    e_q = dot_nn(xe[...], wq[:, 4 * wide :])
    qw[:words] = (w[:, :wide] * factor).astype(bf16)
    qe[:words] = (w[:, wide : 2 * wide] * factor).astype(bf16)
    kk[:words] = w[:, 2 * wide : 3 * wide].astype(bf16)
    vv[:words] = w[:, 3 * wide :].astype(bf16)
    qw[words:] = (e_q[:, :wide] * factor).astype(bf16)
    qe[words:] = (e_q[:, wide:] * factor).astype(bf16)
    kk[words:] = e_kv[:, :wide].astype(bf16)
    vv[words:] = e_kv[:, wide:].astype(bf16)
    values_t = vv[...].astype(f32).T.astype(bf16)
    lane_head = lax.broadcasted_iota(jnp.int32, (128, wide), 1) // dh
    segcol = segk[...]

    def query_block(i, carry):
        at = pl.ds(pl.multiple_of(i * 128, 128), 128)
        q_word, q_ent = qw[at], qe[at]
        zero = jnp.zeros_like(q_word)
        stack_w = jnp.concatenate([jnp.where(lane_head == h, q_word, zero) for h in range(hl)], 0)
        stack_e = jnp.concatenate([jnp.where(lane_head == h, q_ent, zero) for h in range(hl)], 0)
        s_w = dot_nt(kk[:words], stack_w)
        s_e = dot_nt(kk[words:], stack_e)
        allowed = segcol == segq[0:1, at]
        probs = []
        for h in range(hl):
            lanes = slice(128 * h, 128 * h + 128)
            s = jnp.concatenate([s_w[:, lanes], s_e[:, lanes]], 0)
            s = jnp.where(allowed, s, masked_score)
            top = jnp.max(s, axis=0, keepdims=True)
            e = jnp.exp(s - top)
            probs.append((e * (1.0 / jnp.sum(e, axis=0, keepdims=True))).astype(bf16))
        prob = jnp.concatenate(probs, 1)
        p_ref[i] = prob
        ctx = dot_nn(values_t, prob)
        ctx = jnp.concatenate(
            [ctx[dh * h : dh * h + dh, 128 * h : 128 * h + 128] for h in range(hl)], 0
        )
        c_scr[at] = ctx.T.astype(bf16)
        return carry

    lax.fori_loop(0, rows // 128, query_block, 0, unroll=True)
    b = lax.axis_index("blk")
    for k, out in enumerate((c0, c1, c2, c3)):
        to = jnp.bitwise_xor(b, k)
        out[:local] = c_scr[block(c_scr, to, local)]
        out[local:] = c_scr[pl.ds(pl.multiple_of(words + to * share, share), share)]


def mix_body(c0, c1, c2, c3, wo, norms, xw, xe, hr, n1, i1):
    b = lax.axis_index("blk")
    wide = c0.shape[1]
    share = hr.shape[0] - xw.shape[0]
    u = jnp.concatenate([xw[...].astype(f32), xe[block(xe, b, share)].astype(f32)], 0)
    for k, c in enumerate((c0, c1, c2, c3)):
        u = u + dot_nn(c[...], wo[block(wo, partner(k), wide)])
    normed, inverse = norm_stats(u)
    n1[...] = normed
    i1[...] = inverse
    hr[...] = (normed * norms[0:1] + norms[2:3]).astype(bf16)


def feed_body(h0, h1, h2, h3, w1, w2, own, across, core, g_all, gp_all):
    outs = (own, core.at[1], across, core.at[0])
    for k, h in enumerate((h0, h1, h2, h3)):
        z = dot_nn(h[...], w1[...])
        cdf = 0.5 * (1.0 + lax.erf(z * 0.7071067811865476))
        g = (z * cdf).astype(bf16)
        g_all[k] = g
        gp_all[k] = (cdf + z * (0.3989422804014327 * jnp.exp(-0.5 * z * z))).astype(bf16)
        outs[k][...] = dot_nn(g, w2[...]).astype(outs[k].dtype)


def turn_body(f0, f1, f2, n1, norms, gw, ge, yw, ye, df, du2, sums):
    b = lax.axis_index("blk")
    local = gw.shape[0]
    rows = n1.shape[0]
    share = rows - local
    n = norms[...]
    u = n1[...] * n[0:1] + n[2:3]
    u = u + (f0[...] + f1[1].astype(f32) + f2[...].astype(f32))
    normed, inverse = norm_stats(u)
    y = (normed * n[1:2] + n[3:4]).astype(bf16)
    yw[...] = y[:local]
    ye[...] = y[local:]
    dy = jnp.concatenate([gw[...].astype(f32), ge[block(ge, b, share)].astype(f32)], 0)
    sums[...] = jnp.concatenate(
        [jnp.sum(dy * normed, axis=0, keepdims=True), jnp.sum(dy, axis=0, keepdims=True)]
        + [jnp.zeros((6, dy.shape[1]), f32)],
        0,
    )
    d = norm_pull(dy * n[1:2], normed, inverse)
    du2[...] = d
    df[...] = d.astype(bf16)


def feed_back_near_body(d0, d1, gp_all, w1, w2, own, beside, dz):
    for k, (d, out) in enumerate(((d0, own), (d1, beside))):
        z = (dot_nt(d[...], w2[...]) * gp_all[k].astype(f32)).astype(bf16)
        dz[k] = z
        out[...] = dot_nt(z, w1[...]).astype(out.dtype)


def feed_back_far_body(d2, d3, gp_all, w1, w2, beside, across, core, dz):
    core[1] = beside[...]
    for k, (d, out) in enumerate(((d2, across), (d3, core.at[0]))):
        z = (dot_nt(d[...], w2[...]) * gp_all[2 + k].astype(f32)).astype(bf16)
        dz[k] = z
        out[...] = dot_nt(z, w1[...]).astype(out.dtype)


def feed_grads_body(d0, d1, d2, d3, h0, h1, h2, h3, g_all, dz_near, dz_far, *refs):
    outs, g_in, g_out = refs[:-2], refs[-2], refs[-1]
    d = jnp.concatenate([x[...] for x in (d0, d1, d2, d3)], 0)
    h = jnp.concatenate([x[...] for x in (h0, h1, h2, h3)], 0)
    g = jnp.concatenate([g_all[k] for k in range(RANKS)], 0)
    z = jnp.concatenate([dz_near[0], dz_near[1], dz_far[0], dz_far[1]], 0)
    g_in[...] = dot_tn(h, z).astype(bf16)
    g_out[...] = dot_tn(g, d).astype(bf16)
    cut = g_in.shape[1]
    if len(outs) == 1:
        outs[0][:, :cut] = g_in[...]
        outs[0][:, cut:] = g_out[...]
        return
    for j, out in enumerate(outs):
        seat = ff_seat(j // 2, j % 2)
        rows = out.shape[0]
        for x in (0, 1):
            out[rows // 2 * x : rows // 2 * (x + 1), :cut] = g_in[ff_rows(seat, x, rows // 4)]
        out[:, cut:] = g_out[block(out, seat, rows)]


def norm_one_body(h0, h1, h2, du2, n1, i1, norms, two, wo, c0, c1, c2, c3, *refs):
    d0, d2, d3, core, du1, w_own, w_across, scr = refs
    wide = d0.shape[1]
    dh = du2[...] + (h0[...] + h1[1].astype(f32) + h2[...].astype(f32))
    width = dh.shape[1]
    normed = n1[...]
    d = norm_pull(dh * norms[0:1], normed, i1[...])
    du1[...] = d
    low = d.astype(bf16)
    dc = [dot_nt(low, wo[block(wo, partner(k), wide)]).astype(bf16) for k in range(RANKS)]
    d0[...] = dc[0]
    base = 2 * scr.shape[1]
    mine = dc[1].shape[0]
    core[base : base + mine] = dc[1][:, :128]
    core[base + mine :] = jnp.concatenate([dc[1][: mine // 2, 128:], dc[1][mine // 2 :, 128:]], 1)
    d2[...] = dc[2]
    d3[...] = dc[3]
    sums = jnp.concatenate(
        [jnp.sum(dh * normed, axis=0, keepdims=True), two[0:1]]
        + [jnp.sum(dh, axis=0, keepdims=True), two[1:2], jnp.zeros((124, width), f32)],
        0,
    )
    half = width // 2
    for k, c in enumerate((c0, c1, c2, c3)):
        g = dot_tn(c[...], low).astype(bf16)
        q = partner(k)
        tail = pl.ds(pl.multiple_of(width + lax.rem(q, 2) * wide, 64), wide)
        for t in range(RANKS):
            scr[t, block(scr, q, wide)] = g[:, wide * t : wide * t + 128]
        for side in (0, 1):

            @pl.when(lax.div(q, 2) == side)
            def _():
                for t in range(RANKS):
                    rest = g[:, wide * t + 128 : wide * t + wide]
                    scr[t, tail, 64 * side : 64 * side + 64] = rest

    low_sums = sums[:8].astype(bf16)
    for t in range(RANKS):
        for j in range(width // 128):
            at = width + half + 8 * j
            scr[t, at : at + 8] = low_sums[:, 128 * j : 128 * j + 128]
    rows = scr.shape[1]
    w_own[...] = scr[partner(0)]
    core[:rows] = scr[partner(3)]
    core[rows : 2 * rows] = scr[partner(1)]
    w_across[...] = scr[partner(2)]


def attend_back_body(factor, d0, core, d2, d3, qw, qe, kk, vv, p_ref, dqkv, dc, dqw, dqe, dk, dv):
    b = lax.axis_index("blk")
    rows, wide = qw.shape
    local = rows * 4 // 5 // RANKS
    words = local * RANKS
    share = (rows - words) // RANKS
    hl = HEADS // RANKS
    dh = wide // hl
    mine = d0.shape[0]
    base = core.shape[0] - mine * 3 // 2
    tail = core[base + mine :]
    d1 = jnp.concatenate(
        [core[base : base + mine], jnp.concatenate([tail[:, :64], tail[:, 64:]], 0)], 1
    )
    for k, d in enumerate((d0[...], d1, d2[...], d3[...])):
        to = jnp.bitwise_xor(b, k)
        dc[block(dc, to, local)] = d[:local]
        dc[pl.ds(pl.multiple_of(words + to * share, share), share)] = d[local:]
    keys_t = kk[...].astype(f32).T.astype(bf16)
    lane_head = lax.broadcasted_iota(jnp.int32, (128, wide), 1) // dh
    dk[...] = jnp.zeros_like(dk)
    dv[...] = jnp.zeros_like(dv)

    def query_block(i, carry):
        at = pl.ds(pl.multiple_of(i * 128, 128), 128)
        zero = jnp.zeros((128, wide), bf16)

        def stacked(x):
            return jnp.concatenate([jnp.where(lane_head == h, x, zero) for h in range(hl)], 0)

        stack_d = stacked(dc[at])
        prob = p_ref[i]
        dp = dot_nt(vv[...], stack_d)
        parts = []
        for h in range(hl):
            lanes = slice(128 * h, 128 * h + 128)
            p = prob[:, lanes].astype(f32)
            g = dp[:, lanes]
            delta = jnp.sum(p * g, axis=0, keepdims=True)
            parts.append((p * (g - delta)).astype(bf16))
        ds = jnp.concatenate(parts, 1)
        dv[...] += dot_nn(prob, stack_d)
        dk[:words] += dot_nn(ds[:words], stacked(qw[at]))
        dk[words:] += dot_nn(ds[words:], stacked(qe[at]))
        for keys, ds_part, out in ((keys_t[:, :words], ds[:words], dqw), (keys_t[:, words:], ds[words:], dqe)):
            t = dot_nn(keys, ds_part)
            t = jnp.concatenate(
                [t[dh * h : dh * h + dh, 128 * h : 128 * h + 128] for h in range(hl)], 0
            )
            out[at] = t.T
        return carry

    lax.fori_loop(0, rows // 128, query_block, 0, unroll=True)
    dqkv[:, :wide] = (dqw[...] * factor).astype(bf16)
    dqkv[:, wide : 2 * wide] = (dqe[...] * factor).astype(bf16)
    dqkv[:, 2 * wide : 3 * wide] = dk[...].astype(bf16)
    dqkv[:, 3 * wide :] = dv[...].astype(bf16)


def proj_grads_body(dqkv, xw, xe, o0, o1, o2, *refs):
    outs, scr = refs[:-1], refs[-1]
    words = xw.shape[0]
    out_rows = o0.shape[0]
    half = dqkv.shape[1] // 2
    w = dot_tn(xw[...], dqkv[:words])
    e = dot_tn(xe[...], dqkv[words:])
    scr[:, :half] = w[:, :half].astype(bf16)
    scr[:, half : 2 * half] = (w[:, half:] + e[:, half:]).astype(bf16)
    scr[:, 2 * half : 3 * half] = e[:, :half].astype(bf16)
    o = o0[...].astype(f32) + o1[out_rows : 2 * out_rows].astype(f32) + o2[...].astype(f32)
    width = scr.shape[0]
    middle = width // 2
    tail = o[width : width + middle]
    scr[:, 3 * half : 3 * half + 128] = o[:width].astype(bf16)
    scr[:middle, 3 * half + 128 : 3 * half + 192] = tail[:, :64].astype(bf16)
    scr[middle:, 3 * half + 128 : 3 * half + 192] = tail[:, 64:].astype(bf16)
    vec = o[width + middle :]
    sums = jnp.concatenate([vec[8 * j : 8 * j + 8] for j in range(width // 128)], 1)
    sums = jnp.concatenate([sums, jnp.zeros((120, width), f32)], 0).T
    scr[:, 3 * half + 192 :] = sums[:, :64].astype(bf16)
    for j, out in enumerate(outs):
        to = ring_seat(j // 2, j % 2) if len(outs) > 1 else 0
        out[...] = scr[block(scr, to, out.shape[0])]


def total_of(*parts):
    total = parts[0][...].astype(f32)
    for part in parts[1:]:
        total = total + part[...].astype(f32)
    return total


def last_ff_body(a0, a1, a2, a3, w_out, c0, c1, c2, c3, scr):
    rows = c0.shape[0]
    width = c0.shape[1]
    t = total_of(a0, a1, a2, a3)
    w_out[...] = t[:, width:]
    scr[...] = t[:, :width]
    for k, c in enumerate((c0, c1, c2, c3)):
        c[...] = scr[block(scr, jnp.bitwise_xor(ff_rank(), k), rows)].astype(bf16)


def spread_ff_body(c0, c1, c2, c3, out, scr):
    part = out.shape[1] // (8 * RANKS)
    for k, c in enumerate((c0, c1, c2, c3)):
        scr[jnp.bitwise_xor(ff_rank(), k)] = c[...].astype(f32)
    for t in range(RANKS):
        for j in range(8):
            at = ff_column(t, j, part)
            out[:, at : at + part] = scr[t, :, part * j : part * j + part]


def last_body(a0, a1, a2, c0, c1, c2, c3, scr):
    rows = c0.shape[0]
    scr[...] = total_of(a0, a1, a2)
    for k, c in enumerate((c0, c1, c2, c3)):
        c[...] = scr[block(scr, partner(k), rows)].astype(bf16)


def finish_body(c0, c1, c2, c3, gq, gkv, go, gg, gb, scr):
    wide = go.shape[1] // RANKS
    for k, c in enumerate((c0, c1, c2, c3)):
        scr[partner(k)] = c[...].astype(f32)
    for t in range(RANKS):
        cut = slice(wide * t, wide * t + wide)
        for j, (out, i) in enumerate(((gq, 0), (gq, 1), (gkv, 0), (gkv, 1), (gq, 2), (gq, 3))):
            out[i, :, cut] = scr[t, :, wide * j : wide * j + wide]
        go[:, cut] = scr[t, :, 6 * wide : 7 * wide]
    at = 7 * wide + 64 - 128
    v = c0[:, at:].astype(f32).T
    gg[...] = v[64:66]
    gb[...] = v[66:68]


def input_body(dqkv, wq, du1, ye, own, across, core, part):
    b = lax.axis_index("blk")
    local, share = own.shape[0], ye.shape[0]
    words = RANKS * local
    half = dqkv.shape[1] // 2
    part[:words] = dot_nt(dqkv[:words], wq[:, : 2 * half])
    part[words:] = dot_nt(dqkv[words:, half:], wq[:, half : 2 * half]) + dot_nt(
        dqkv[words:, :half], wq[:, 2 * half :]
    )
    part[pl.ds(pl.multiple_of(words + b * share, share), share)] += du1[local:]
    own[...] = part[block(part, b, local)] + du1[:local]
    low = part[words:].astype(bf16)
    core[:local] = part[block(part, partner(3), local)].astype(bf16)
    core[local : 2 * local] = part[block(part, partner(1), local)].astype(bf16)
    core[2 * local : -share] = low
    core[-share:] = ye[...]
    across[:local] = part[block(part, partner(2), local)].astype(bf16)
    across[local:-share] = low
    across[-share:] = ye[...]


def input_pair_body(across, came, sent):
    share = sent.shape[0] - across.shape[0]
    local = came.shape[0] - across.shape[0]
    sent[:local] = (across[:local].astype(f32) + came[:local].astype(f32)).astype(bf16)
    pair = across[local:-share].astype(f32) + came[2 * local : -share].astype(f32)
    sent[local : -2 * share] = pair.astype(bf16)
    sent[-2 * share : -share] = across[-share:]
    sent[-share:] = came[-share:]


def input_sum_body(own, core, sent, came, gw, ge, ye):
    local = own.shape[0]
    share = ye.shape[0] // RANKS
    two = 2 * share
    gw[...] = own[...] + core[local : 2 * local].astype(f32) + came[:local].astype(f32)
    ge[...] = sent[local:-two].astype(f32) + came[local:-two].astype(f32)
    for k, rows in enumerate((sent[-two:-share], sent[-share:], came[-two:-share], came[-share:])):
        ye[block(ye, partner(k), share)] = rows


def swap(x, k):
    return lax.ppermute(x, "blk", [(i, i ^ k) for i in range(RANKS)])


def swapped(send):
    return [swap(send[k - 1], k) for k in (1, 2, 3)]


def spread(x):
    across = swap(x, 2)
    beside = swap(x, 1)
    return [beside, across, swap(across, 1)]


def plus(*parts):
    total = parts[0].astype(f32)
    for part in parts[1:]:
        total = total + part.astype(f32)
    return total.astype(bf16)


def over_x(x):
    return lax.ppermute(x, "seq", [(i, i ^ 1) for i in range(8)])


ring = (0, 1, 3, 2)


def swap_ff(x, k, direct):
    if not direct or k == 1:
        return swap(x, k)
    if k == 2:
        return over_x(x)
    return lax.ppermute(x, ("seq", "blk"), [(i, i ^ 5) for i in range(32)])


def along_ring(x, step=1):
    route = [(ring[i], ring[(i + step) % 4]) for i in range(4)]
    return lax.ppermute(x, "seq", [(2 * z + i, 2 * to + i) for z, to in route for i in (0, 1)])


def fence(*groups):
    return lax.optimization_barrier(groups)


def after(x, *before):
    return lax.optimization_barrier((x, before))[0]


def per_device(
    words,
    entities,
    segments,
    entity_counts,
    entity_anchor,
    query_weights,
    kv_weights,
    out_weight,
    ff_in,
    ff_out,
    norm_gain,
    norm_bias,
    grad_words,
    grad_entities,
):
    seqs = lax.axis_size("seq")
    direct = seqs == 8
    _, local, width = words.shape
    ents = entities.shape[1]
    share = ents // RANKS
    total = local * RANKS
    rows = total + ents
    mine = local + share
    wide = width // RANKS
    hl = HEADS // RANKS
    factor = (width // HEADS) ** (-0.5)
    part_rows = query_weights.shape[2]
    ff_part = ff_out.shape[1]
    ff = ff_part * seqs
    shards = 8 if direct else 1
    slab_cols = 7 * wide + 64
    xw_own, xe = words[0], entities[0]

    seg_ents = jnp.take_along_axis(segments, entity_anchor, axis=1)
    live = jnp.arange(ents, dtype=jnp.int32)[None, :] < entity_counts[:, None]
    segq = jnp.concatenate([segments, seg_ents], 1)
    segk = jnp.concatenate([segments, jnp.where(live, seg_ents, -1)], 1).T
    join_rows = call(join_rows_body, "join_rows", [((total, width), bf16)])

    if direct:
        pack = call(
            pack_body,
            "pack",
            [((part_rows, slab_cols), bf16)] * 4,
            [pltpu.VMEM((RANKS, part_rows, slab_cols), bf16)]
            + [pltpu.VMEM((n, part_rows, width), bf16) for n in (4, 2)]
            + [pltpu.VMEM((part_rows, width), bf16)]
            + [pltpu.VMEM((2, part_rows), bf16)] * 2
            + [pltpu.SemaphoreType.DMA((5,))],
            held=5,
            vmem=60,
        )
        pieces = pack(
            query_weights[0], kv_weights[0], out_weight[0], norm_gain[0], norm_bias[0]
        )
        pack_ff = call(
            pack_ff_body,
            "pack_ff",
            [((part_rows, ff), bf16)] * 4,
            [pltpu.VMEM((RANKS, part_rows, ff), bf16)],
        )
        ff_pieces = pack_ff(after(ff_in[0], pieces[0]))
        own = call(
            arrange_own_body, "arrange_own", [((RANKS * part_rows, slab_cols), f32)]
        )(pieces[0])
        pieces = [own[0], *swapped(pieces[1:])]

        arrange = call(
            arrange_body,
            "arrange",
            [((RANKS * part_rows, slab_cols), bf16)],
            [pltpu.VMEM((RANKS * part_rows, slab_cols), f32)],
        )
        arrange_ff = call(
            arrange_ff_body,
            "arrange_ff",
            [((RANKS * part_rows, ff + width), bf16)],
            [pltpu.VMEM((RANKS * part_rows, ff), f32)],
        )
        (slab,) = arrange(*pieces)
        xw_own, slab = fence(xw_own, slab)
        xb, xa = swap(xw_own, 1), swap(xw_own, 2)
        x0, g1 = over_x(slab), along_ring(slab)
        g1, x0, xb, ff_pieces = fence(g1, x0, xb, ff_pieces)
        x1, g2 = over_x(g1), along_ring(g1)
        came = [swap_ff(ff_pieces[k], k, direct) for k in (1, 2, 3)]
        (ff_slab,) = arrange_ff(ff_pieces[0], *came, ff_out[0])
        g2, x1, ff_slab, xa = fence(g2, x1, ff_slab, xa)
        x2, g3 = over_x(g2), along_ring(g2)
        y0, xc = swap(ff_slab, 2), swap(xa, 1)
        g3, x2, xc, segq, segk = fence(g3, x2, xc, segq, segk)
        f1, x3 = along_ring(after(ff_slab, g3)), over_x(g3)
        (xw,) = join_rows(xw_own, xb, xa, xc)
        x3, f1, y0, xw = fence(x3, f1, y0, xw)
        f2 = along_ring(f1)
        slabs = [slab, x0, g1, x1, g2, x2, g3, x3]
    else:
        vec = jnp.concatenate([norm_gain[0], norm_bias[0]], 0).T
        vec = jnp.pad(vec, ((0, 0), (0, 60)))
        six = jnp.concatenate(
            [query_weights[0, :2], kv_weights[0], query_weights[0, 2:], out_weight], 0
        )
        six = six.reshape(7, part_rows, RANKS, wide).transpose(2, 1, 0, 3)
        six = six.reshape(RANKS, part_rows, 7 * wide)
        ff_cols = ff_in[0].reshape(part_rows, seqs, RANKS, ff_part).transpose(2, 0, 1, 3)
        ff_cols = ff_cols.reshape(RANKS, part_rows, ff)
        pack = jnp.concatenate(
            [six, jnp.broadcast_to(vec, (RANKS, part_rows, 64)), ff_cols], 2
        )
        pack = lax.all_to_all(pack, "blk", 0, 0, tiled=True).reshape(RANKS * part_rows, -1)
        pack = jnp.concatenate([pack, ff_out[0]], 1)
        pack = lax.all_gather(pack, "seq", axis=0, tiled=True)
        slabs, ff_slabs = [pack[:, :slab_cols]], [pack[:, slab_cols:]]
        (xw,) = join_rows(xw_own, *spread(xw_own))

    def place(slots, last, *args):
        outs = [((width, 6 * wide), bf16), ((width, 128), bf16), ((width, wide - 64), bf16)]
        if last:
            outs += [((width * 3 // 2, 128), bf16), ((8, width), f32)]
        body = place_last_body if last else place_body
        same = len(args) - len(slots)
        name = "place_last" if last else "place"
        return call(lambda *r: body(slots, *r), name, outs, same=same)(*args)

    if direct:
        ready = place((0, 1, 2, 3, 4), False, *slabs[:5])
        wq, _, _, wo_col, norms = place((5, 6, 7), True, *ready, *slabs[5:])
    else:
        blank = [jnp.zeros((width, n), bf16) for n in (6 * wide, 128, wide - 64)]
        wq, _, _, wo_col, norms = place((0,), True, *blank, slabs[0])
    wa, wb = swap(wo_col, 2), swap(wo_col, 1)
    attend = call(
        lambda *r: attend_body(wide, factor, *r),
        "attend",
        [((mine, wide), bf16)] * 4
        + [((rows, wide), bf16)] * 4
        + [((rows // 128, rows, 128 * hl), bf16)],
        [pltpu.VMEM((rows, wide), bf16)],
        us=7,
        vmem=16,
    )
    *ctx, qw, qe, kk, vv, prob = attend(xw, xe, wq, segq, segk)
    if direct:
        ctx = after(ctx, wb)
    ctx = [ctx[0]] + swapped(ctx[1:])
    wos = [wo_col, wb, wa, swap(after(wa, ctx), 1)]
    if direct:
        f3, y1 = along_ring(f2), swap(after(f1, ctx), 2)
    join_out = call(
        join_out_body,
        "join_out",
        [((width, width), bf16)],
        [pltpu.VMEM((RANKS, width * 3 // 2, 128), bf16)],
    )
    (wo,) = join_out(*(after(wos, f3) if direct else wos))
    mix = call(
        mix_body,
        "mix",
        [((mine, width), bf16), ((mine, width), f32), ((mine, 1), f32)],
    )
    hr, n1, i1 = mix(*ctx, wo, norms, xw_own, xe)

    def place_ff(slots, *args):
        outs = [((width, ff), bf16), ((ff, width), bf16)]
        same = len(args) - len(slots)
        return call(lambda *r: place_ff_body(slots, *r), "place_ff", outs, same=same)(*args)

    across, beside = swap_ff(hr, 2, direct), swap(hr, 1)
    if direct:
        fb, y2 = along_ring(after(y0, hr), -1), swap(after(f2, hr), 2)
        ready = place_ff((0, 1, 2, 3, 4, 6), ff_slab, y0, f1, y1, f2, f3)
        across = after(across, ready)
        ff_slabs = [ff_slab, y0, f1, y1, f2, y2, f3, fb]
    hs = [hr, beside, across, swap(across, 1)]
    if direct:
        w1, w2 = place_ff((5, 7), *ready, ff_slabs[5], ff_slabs[7])
    else:
        w1, w2 = place_ff((0,), ff_slabs[0])
    feed = call(
        feed_body,
        "feed",
        [((mine, width), f32), ((mine, width), bf16), ((2, mine, width), bf16)]
        + [((RANKS, mine, ff), bf16)] * 2,
        us=3,
        vmem=14,
    )
    own, across, core, g_all, gp_all = feed(*hs, w1, w2)
    core = swap(core, 1)
    fs = [own, core, swap_ff(plus(across, core[0]), 2, direct)]
    turn = call(
        turn_body,
        "turn",
        [((local, width), bf16), ((share, width), bf16), ((mine, width), bf16)]
        + [((mine, width), f32), ((8, width), f32)],
    )
    yw, ye, df, du2, sums = turn(*fs, n1, norms, grad_words[0], grad_entities[0])

    across, beside = swap_ff(df, 2, direct), swap(df, 1)
    ds = [df, beside, across, swap(across, 1)]
    half_dz = ((2, mine, ff), bf16)
    feed_back_near = call(
        feed_back_near_body,
        "feed_back_near",
        [((mine, width), f32), ((mine, width), bf16), half_dz],
        vmem=12,
    )
    feed_back_far = call(
        feed_back_far_body,
        "feed_back_far",
        [((mine, width), bf16), ((2, mine, width), bf16), half_dz],
        vmem=12,
    )
    own, beside, dz_near = feed_back_near(*ds[:2], gp_all, w1, w2)
    across, core, dz_far = feed_back_far(*ds[2:], gp_all, w1, w2, beside)
    core = swap(core, 1)
    feed_grads = call(
        feed_grads_body,
        "feed_grads",
        [((width // shards, ff + width), bf16)] * shards,
        [pltpu.VMEM((width, ff), bf16), pltpu.VMEM((ff, width), bf16)],
        us=3,
        vmem=16,
    )
    sent = plus(across, core[0])
    ff_chunks = feed_grads(*ds, *hs, g_all, dz_near, after(dz_far, sent))
    dhs = [own, core, swap_ff(sent, 2, direct)]
    if direct:
        ff0, ff1, ff2, ff3, ff4, ff5, ff6, ff7 = ff_chunks
        fy, fz = swap(ff5, 2), along_ring(ff2)
        part = plus(ff4, after(fy, fz))
        dhs[2] = after(dhs[2], ff_chunks)
        fl = along_ring(part, -1)

    packed = width * 3 // 2 + 8 * (width // 128)
    norm_one = call(
        norm_one_body,
        "norm_one",
        [((mine, wide), bf16)] * 3
        + [((2 * packed + mine * 3 // 2, 128), bf16), ((mine, width), f32)]
        + [((packed, 128), bf16)] * 2,
        [pltpu.VMEM((RANKS, packed, 128), bf16)],
        vmem=12,
    )
    d0, d2, d3, core, du1, wo_own, across = norm_one(
        *dhs, du2, n1, i1, norms, sums, wo, *ctx
    )
    dcs = [d0, swap(core, 1), swap(d2, 2), swap(d3, 3)]
    sent = plus(across, after(dcs[1], dcs[2], dcs[3])[:packed])
    outs = [wo_own, dcs[1], swap(sent, 2)]
    dcs = after(dcs, sent)
    attend_back = call(
        lambda *r: attend_back_body(factor, *r),
        "attend_back",
        [((rows, 4 * wide), bf16)],
        [pltpu.VMEM((rows, wide), bf16)] + [pltpu.VMEM((rows, wide), f32)] * 4,
        us=7,
        vmem=16,
    )
    (dqkv,) = attend_back(*dcs, qw, qe, kk, vv, prob)
    to_input = call(
        input_body,
        "to_input",
        [((local, width), f32)]
        + [((n * local + ents + share, width), bf16) for n in (1, 2)],
        [pltpu.VMEM((rows, width), f32)],
        us=2,
        vmem=12,
    )
    own, across, core = to_input(dqkv, wq, du1, ye)
    if direct:
        own = after(own, fl)
    core = swap(core, 1)
    proj_grads = call(
        proj_grads_body,
        "proj_grads",
        [((width // shards, slab_cols), bf16)] * shards,
        [pltpu.VMEM((width, slab_cols), bf16)],
        us=2,
        vmem=14,
    )
    chunks = proj_grads(after(dqkv, own), xw, xe, *outs)
    if direct:
        fl = along_ring(plus(ff6, after(fl, dqkv)), -1)
        fb, fc = along_ring(after(ff3, chunks)), along_ring(after(ff7, chunks), -1)
        part = plus(chunks[2], after(over_x(chunks[3]), fl, fb))
        cx, cz = over_x(after(chunks[5], part)), along_ring(part, -1)
        core = after(core, part)
    (sent,) = call(input_pair_body, "input_pair", [((local + ents + 2 * share, width), bf16)])(across, core)
    came = swap(sent, 2)
    input_sum = call(
        input_sum_body,
        "input_sum",
        [((local, width), f32), ((ents, width), f32), ((ents, width), bf16)],
    )
    if not direct:
        gxw, gxe, ye = input_sum(own, core, sent, came)

    if direct:
        last_ff = call(
            last_ff_body,
            "last_ff",
            [((ff_part, width), f32)] + [((part_rows, ff), bf16)] * 4,
            [pltpu.VMEM((RANKS * part_rows, ff), f32)],
        )
        part = plus(chunks[4], cz, cx)
        cx, cz = over_x(after(chunks[7], part)), along_ring(part, -1)
        fy_last = swap(plus(ff1, fb, after(fc, part)), 2)
        part = plus(chunks[6], after(cz, came), cx)
        cx, cz = over_x(after(chunks[1], part)), along_ring(part, -1)
        grad_ff_out, *back = last_ff(ff0, fz, fl, after(fy_last, part))
        back = [back[0]] + [swap_ff(back[k], k, direct) for k in (1, 2, 3)]
        spread_ff = call(
            spread_ff_body,
            "spread_ff",
            [((part_rows, RANKS * ff), f32)],
            [pltpu.VMEM((RANKS, part_rows, ff), f32)],
        )
        (grad_ff_in,) = spread_ff(*back)
        gxw, gxe, ye = input_sum(own, core, sent, after(came, part))
        last = call(
            last_body,
            "last",
            [((part_rows, slab_cols), bf16)] * 4,
            [pltpu.VMEM((RANKS * part_rows, slab_cols), f32)],
        )
        back = last(chunks[0], after(cz, grad_ff_in, gxw), cx)
        back = [back[0]] + swapped(back[1:])
        finish = call(
            finish_body,
            "finish",
            [((4, part_rows, width), f32), ((2, part_rows, width), f32), ((part_rows, width), f32)]
            + [((2, part_rows), f32)] * 2,
            [pltpu.VMEM((RANKS, part_rows, slab_cols), f32)],
        )
        grad_query, grad_kv, grad_out, grad_gain, grad_bias = finish(*back)
    else:
        both = jnp.concatenate([chunks[0], ff_chunks[0]], 1)
        both = lax.psum_scatter(both, "seq", scatter_dimension=0, tiled=True)
        grad_ff_out = both[:, slab_cols + ff :].astype(f32)
        both = both[:, : slab_cols + ff].reshape(RANKS, part_rows, slab_cols + ff)
        both = lax.all_to_all(both, "blk", 0, 0, tiled=True).astype(f32)
        seven = both[:, :, : 7 * wide].reshape(RANKS, part_rows, 7, wide)
        seven = seven.transpose(2, 1, 0, 3).reshape(7, part_rows, width)
        grad_query = jnp.concatenate([seven[:2], seven[4:6]], 0)
        grad_kv, grad_out = seven[2:4], seven[6]
        vecs = both[0, :, 7 * wide : 7 * wide + 4].T
        grad_gain, grad_bias = vecs[:2], vecs[2:]
        grad_ff_in = both[:, :, slab_cols:].reshape(RANKS, part_rows, seqs, ff_part)
        grad_ff_in = grad_ff_in.transpose(1, 2, 0, 3).reshape(part_rows, RANKS * ff)
    return (
        yw[None],
        ye[None],
        gxw[None],
        gxe[None],
        grad_query[None],
        grad_kv[None],
        grad_out[None],
        grad_ff_in[None],
        grad_ff_out[None],
        grad_gain[None],
        grad_bias[None],
    )


def solution(mesh):
    placed = (
        P("seq", "blk", None),
        P("seq", None, None),
        P("seq", None),
        P("seq"),
        P("seq", None),
        P(None, None, ("seq", "blk"), None),
        P(None, None, ("seq", "blk"), None),
        P(None, ("seq", "blk"), None),
        P(None, ("seq", "blk"), None),
        P(None, ("seq", "blk"), None),
        P(None, None, ("seq", "blk")),
        P(None, None, ("seq", "blk")),
        P("seq", "blk", None),
        P("seq", None, None),
    )
    return jax.shard_map(
        per_device,
        mesh=mesh,
        in_specs=placed,
        out_specs=(
            P("seq", "blk", None),
            P("seq", None, None),
            P("seq", "blk", None),
            P("seq", None, None),
            P(None, None, ("seq", "blk"), None),
            P(None, None, ("seq", "blk"), None),
            P(None, ("seq", "blk"), None),
            P(None, ("seq", "blk"), None),
            P(None, ("seq", "blk"), None),
            P(None, None, ("seq", "blk")),
            P(None, None, ("seq", "blk")),
        ),
        check_vma=False,
    )
```

```python
import jax
import jax.numpy as jnp
from jax import lax
from jax.experimental import pallas as pl
from jax.experimental.pallas import tpu as pltpu
from jax.sharding import PartitionSpec as P

HEADS = 12
RANKS = 4
epsilon = 1e-05
masked_score = -1e30
bf16 = jnp.bfloat16
f32 = jnp.float32


def dot_nn(a, b):
    return jnp.dot(a, b, preferred_element_type=f32)


def dot_nt(a, b):
    return lax.dot_general(a, b, (((1,), (1,)), ((), ())), preferred_element_type=f32)


def dot_tn(a, b):
    return lax.dot_general(a, b, (((0,), (0,)), ((), ())), preferred_element_type=f32)


def block(ref, index, size):
    return pl.ds(pl.multiple_of(index * size, size), size)


def call(body, name, outs, scratch=(), vmem=10, us=1, held=0, same=0):
    def run(*args):
        return pl.pallas_call(
            body,
            name=name,
            out_shape=[jax.ShapeDtypeStruct(s, t) for s, t in outs],
            in_specs=[pl.BlockSpec(memory_space=pltpu.HBM)] * held
            + [pl.BlockSpec(memory_space=pltpu.VMEM)] * (len(args) - held),
            out_specs=[pl.BlockSpec(memory_space=pltpu.VMEM)] * len(outs),
            scratch_shapes=list(scratch),
            input_output_aliases={i: i for i in range(same)},
            compiler_params=pltpu.CompilerParams(vmem_limit_bytes=vmem << 20),
            cost_estimate=pl.CostEstimate(
                flops=int(us * 1e6), bytes_accessed=int(us * 1e3), transcendentals=0
            ),
        )(*args)

    return run


def partner(k):
    return jnp.bitwise_xor(lax.axis_index("blk"), k)


def ring_seat(k, e):
    s = lax.axis_index("seq")
    z = lax.div(s, 2)
    at = lax.rem(jnp.bitwise_xor(z, lax.div(z, 2)) + (k + 4), 4)
    return 2 * jnp.bitwise_xor(at, lax.div(at, 2)) + jnp.bitwise_xor(lax.rem(s, 2), e)


def ff_rank():
    return 2 * lax.rem(lax.axis_index("seq"), 2) + lax.rem(lax.axis_index("blk"), 2)


def ff_seat(k, e):
    z = lax.div(lax.axis_index("seq"), 2)
    at = lax.rem(jnp.bitwise_xor(z, lax.div(z, 2)) + (k + 4), 4)
    y = jnp.bitwise_xor(lax.div(lax.axis_index("blk"), 2), e)
    return 2 * jnp.bitwise_xor(at, lax.div(at, 2)) + y


def ff_column(rank, j, part):
    return (8 * (j // 2) + 4 * (rank // 2) + 2 * (j % 2) + rank % 2) * part


def ff_rows(seat, x, rows):
    at = 4 * lax.div(seat, 2) + 2 * x + lax.rem(seat, 2)
    return pl.ds(pl.multiple_of(2 * rows * at, 16), 2 * rows)


def norm_stats(u):
    center = u - jnp.mean(u, axis=-1, keepdims=True)
    inverse = lax.rsqrt(jnp.mean(center * center, axis=-1, keepdims=True) + epsilon)
    return center * inverse, inverse


def norm_pull(scaled, normed, inverse):
    return inverse * (
        scaled
        - jnp.mean(scaled, axis=-1, keepdims=True)
        - normed * jnp.mean(scaled * normed, axis=-1, keepdims=True)
    )


def fetch(refs, sems):
    half = len(refs) // 2
    copies = [
        pltpu.make_async_copy(source, target, sems.at[i])
        for i, (source, target) in enumerate(zip(refs[:half], refs[half:]))
    ]
    for copy in copies:
        copy.start()
    for copy in copies:
        copy.wait()


def pack_body(*refs):
    sources, outs, scr, here, sems = refs[:5], refs[5:9], refs[9], refs[10:15], refs[15]
    fetch((*sources, *here), sems)
    q, kv, wo, gain, bias = here
    rows, wide = q.shape[1], q.shape[2] // RANKS
    eye = lax.broadcasted_iota(jnp.int32, (rows, rows), 0) == lax.broadcasted_iota(
        jnp.int32, (rows, rows), 1
    )
    lane = lax.broadcasted_iota(jnp.int32, (rows, 64), 1)
    vec = jnp.zeros((rows, 64), f32)
    for j, row in enumerate((gain[0:1], gain[1:2], bias[0:1], bias[1:2])):
        column = jnp.sum(jnp.where(eye, row.astype(f32), 0.0), axis=1, keepdims=True)
        vec = jnp.where(lane == j, column, vec)
    for t in range(RANKS):
        cut = slice(wide * t, wide * t + wide)
        for j, piece in enumerate((q[0], q[1], kv[0], kv[1], q[2], q[3], wo[...])):
            scr[t, :, wide * j : wide * j + wide] = piece[:, cut]
        scr[t, :, 7 * wide :] = vec.astype(bf16)
    for k in range(RANKS):
        outs[k][...] = scr[partner(k)]


def pack_ff_body(ff, *refs):
    outs, scr = refs[:RANKS], refs[RANKS]
    part = ff.shape[1] // (8 * RANKS)
    for t in range(RANKS):
        for j in range(8):
            at = ff_column(t, j, part)
            scr[t, :, part * j : part * j + part] = ff[:, at : at + part]
    for k in range(RANKS):
        outs[k][...] = scr[jnp.bitwise_xor(ff_rank(), k)]


def arrange_own_body(p0, out):
    out[block(out, partner(0), p0.shape[0])] = p0[...].astype(f32)


def arrange_body(own, p1, p2, p3, slab, scr):
    rows = p1.shape[0]
    scr[...] = own[...]
    for k, p in ((1, p1), (2, p2), (3, p3)):
        scr[block(scr, partner(k), rows)] = p[...].astype(f32)
    slab[...] = scr[...].astype(bf16)


def arrange_ff_body(p0, p1, p2, p3, ff_out, slab, scr):
    rows, cols = p0.shape
    for k, p in enumerate((p0, p1, p2, p3)):
        scr[block(scr, jnp.bitwise_xor(ff_rank(), k), rows)] = p[...].astype(f32)
    slab[:, :cols] = scr[...].astype(bf16)
    slab[:, cols:] = ff_out[...]


def place_body(slots, *refs):
    shards, (wq, wo_first, rest) = refs[-3 - len(slots) : -3], refs[-3:]
    rows, first = shards[0].shape[0], wq.shape[1]
    for j, shard in zip(slots, shards):
        at = block(shard, ring_seat(-(j // 2), j % 2) if rows < wq.shape[0] else 0, rows)
        wq[at] = shard[:, :first]
        wo_first[at] = shard[:, first : first + 128]
        rest[at] = shard[:, first + 128 :]


def place_last_body(slots, *refs):
    wide = refs[0].shape[1] // 6
    ins, (wq, wo_first, rest, wo_col, norms) = refs[:-5], refs[-5:]
    place_body(slots, *ins, wq, wo_first, rest)
    width = wq.shape[0]
    half = width // 2
    tail = rest[...]
    wo_col[:width] = wo_first[...]
    wo_col[width:] = jnp.concatenate([tail[:half, : wide - 128], tail[half:, : wide - 128]], 1)
    norms[...] = tail.astype(f32).T[wide - 128 : wide - 120]


def place_ff_body(slots, *refs):
    shards, w1, w2 = refs[-2 - len(slots) : -2], refs[-2], refs[-1]
    rows, cut = shards[0].shape[0], w1.shape[1]
    if rows == w1.shape[0]:
        w1[...] = shards[0][:, :cut]
        w2[...] = shards[0][:, cut:]
        return
    for j, shard in zip(slots, shards):
        seat = ff_seat(-(j // 2), j % 2)
        for x in (0, 1):
            w1[ff_rows(seat, x, rows // 4)] = shard[rows // 2 * x : rows // 2 * (x + 1), :cut]
        w2[block(shard, seat, rows)] = shard[:, cut:]


def join_out_body(w0, w1, w2, w3, wo, scr):
    wide = wo.shape[1] // RANKS
    half = wo.shape[0] // 2
    for k, w in enumerate((w0, w1, w2, w3)):
        scr[partner(k)] = w[...]
    for t in range(RANKS):
        wo[:, wide * t : wide * t + 128] = scr[t, : 2 * half]
        tail = scr[t, 2 * half :]
        wo[:half, wide * t + 128 : wide * t + wide] = tail[:, : wide - 128]
        wo[half:, wide * t + 128 : wide * t + wide] = tail[:, wide - 128 :]


def join_rows_body(x0, x1, x2, x3, xw):
    local = x0.shape[0]
    for k, x in enumerate((x0, x1, x2, x3)):
        xw[block(xw, partner(k), local)] = x[...]


def attend_body(wide, factor, xw, xe, wq, segq, segk, c0, c1, c2, c3, qw, qe, kk, vv, p_ref, c_scr):
    words, ents = xw.shape[0], xe.shape[0]
    local = words // RANKS
    share = ents // RANKS
    hl = HEADS // RANKS
    dh = wide // hl
    rows = words + ents
    w = dot_nn(xw[...], wq[:, : 4 * wide])
    e_kv = dot_nn(xe[...], wq[:, 2 * wide : 4 * wide])
    e_q = dot_nn(xe[...], wq[:, 4 * wide :])
    qw[:words] = (w[:, :wide] * factor).astype(bf16)
    qe[:words] = (w[:, wide : 2 * wide] * factor).astype(bf16)
    kk[:words] = w[:, 2 * wide : 3 * wide].astype(bf16)
    vv[:words] = w[:, 3 * wide :].astype(bf16)
    qw[words:] = (e_q[:, :wide] * factor).astype(bf16)
    qe[words:] = (e_q[:, wide:] * factor).astype(bf16)
    kk[words:] = e_kv[:, :wide].astype(bf16)
    vv[words:] = e_kv[:, wide:].astype(bf16)
    values_t = vv[...].astype(f32).T.astype(bf16)
    lane_head = lax.broadcasted_iota(jnp.int32, (128, wide), 1) // dh
    segcol = segk[...]

    def query_block(i, carry):
        at = pl.ds(pl.multiple_of(i * 128, 128), 128)
        q_word, q_ent = qw[at], qe[at]
        zero = jnp.zeros_like(q_word)
        stack_w = jnp.concatenate([jnp.where(lane_head == h, q_word, zero) for h in range(hl)], 0)
        stack_e = jnp.concatenate([jnp.where(lane_head == h, q_ent, zero) for h in range(hl)], 0)
        s_w = dot_nt(kk[:words], stack_w)
        s_e = dot_nt(kk[words:], stack_e)
        allowed = segcol == segq[0:1, at]
        probs = []
        for h in range(hl):
            lanes = slice(128 * h, 128 * h + 128)
            s = jnp.concatenate([s_w[:, lanes], s_e[:, lanes]], 0)
            s = jnp.where(allowed, s, masked_score)
            top = jnp.max(s, axis=0, keepdims=True)
            e = jnp.exp(s - top)
            probs.append((e * (1.0 / jnp.sum(e, axis=0, keepdims=True))).astype(bf16))
        prob = jnp.concatenate(probs, 1)
        p_ref[i] = prob
        ctx = dot_nn(values_t, prob)
        ctx = jnp.concatenate(
            [ctx[dh * h : dh * h + dh, 128 * h : 128 * h + 128] for h in range(hl)], 0
        )
        c_scr[at] = ctx.T.astype(bf16)
        return carry

    lax.fori_loop(0, rows // 128, query_block, 0, unroll=True)
    b = lax.axis_index("blk")
    for k, out in enumerate((c0, c1, c2, c3)):
        to = jnp.bitwise_xor(b, k)
        out[:local] = c_scr[block(c_scr, to, local)]
        out[local:] = c_scr[pl.ds(pl.multiple_of(words + to * share, share), share)]


def mix_body(c0, c1, c2, c3, wo, norms, xw, xe, hr, n1, i1):
    b = lax.axis_index("blk")
    wide = c0.shape[1]
    share = hr.shape[0] - xw.shape[0]
    u = jnp.concatenate([xw[...].astype(f32), xe[block(xe, b, share)].astype(f32)], 0)
    for k, c in enumerate((c0, c1, c2, c3)):
        u = u + dot_nn(c[...], wo[block(wo, partner(k), wide)])
    normed, inverse = norm_stats(u)
    n1[...] = normed
    i1[...] = inverse
    hr[...] = (normed * norms[0:1] + norms[2:3]).astype(bf16)


def feed_body(h0, h1, h2, h3, w1, w2, own, across, core, g_all, gp_all):
    outs = (own, core.at[1], across, core.at[0])
    for k, h in enumerate((h0, h1, h2, h3)):
        z = dot_nn(h[...], w1[...])
        cdf = 0.5 * (1.0 + lax.erf(z * 0.7071067811865476))
        g = (z * cdf).astype(bf16)
        g_all[k] = g
        gp_all[k] = (cdf + z * (0.3989422804014327 * jnp.exp(-0.5 * z * z))).astype(bf16)
        outs[k][...] = dot_nn(g, w2[...]).astype(outs[k].dtype)


def turn_body(f0, f1, f2, n1, norms, gw, ge, yw, ye, df, du2, sums):
    b = lax.axis_index("blk")
    local = gw.shape[0]
    rows = n1.shape[0]
    share = rows - local
    n = norms[...]
    u = n1[...] * n[0:1] + n[2:3]
    u = u + (f0[...] + f1[1].astype(f32) + f2[...].astype(f32))
    normed, inverse = norm_stats(u)
    y = (normed * n[1:2] + n[3:4]).astype(bf16)
    yw[...] = y[:local]
    ye[...] = y[local:]
    dy = jnp.concatenate([gw[...].astype(f32), ge[block(ge, b, share)].astype(f32)], 0)
    sums[...] = jnp.concatenate(
        [jnp.sum(dy * normed, axis=0, keepdims=True), jnp.sum(dy, axis=0, keepdims=True)]
        + [jnp.zeros((6, dy.shape[1]), f32)],
        0,
    )
    d = norm_pull(dy * n[1:2], normed, inverse)
    du2[...] = d
    df[...] = d.astype(bf16)


def feed_back_near_body(d0, d1, gp_all, w1, w2, own, beside, dz):
    for k, (d, out) in enumerate(((d0, own), (d1, beside))):
        z = (dot_nt(d[...], w2[...]) * gp_all[k].astype(f32)).astype(bf16)
        dz[k] = z
        out[...] = dot_nt(z, w1[...]).astype(out.dtype)


def feed_back_far_body(d2, d3, gp_all, w1, w2, beside, across, core, dz):
    core[1] = beside[...]
    for k, (d, out) in enumerate(((d2, across), (d3, core.at[0]))):
        z = (dot_nt(d[...], w2[...]) * gp_all[2 + k].astype(f32)).astype(bf16)
        dz[k] = z
        out[...] = dot_nt(z, w1[...]).astype(out.dtype)


def feed_grads_body(d0, d1, d2, d3, h0, h1, h2, h3, g_all, dz_near, dz_far, *refs):
    outs, g_in, g_out = refs[:-2], refs[-2], refs[-1]
    d = jnp.concatenate([x[...] for x in (d0, d1, d2, d3)], 0)
    h = jnp.concatenate([x[...] for x in (h0, h1, h2, h3)], 0)
    g = jnp.concatenate([g_all[k] for k in range(RANKS)], 0)
    z = jnp.concatenate([dz_near[0], dz_near[1], dz_far[0], dz_far[1]], 0)
    g_in[...] = dot_tn(h, z).astype(bf16)
    g_out[...] = dot_tn(g, d).astype(bf16)
    cut = g_in.shape[1]
    if len(outs) == 1:
        outs[0][:, :cut] = g_in[...]
        outs[0][:, cut:] = g_out[...]
        return
    for j, out in enumerate(outs):
        seat = ff_seat(j // 2, j % 2)
        rows = out.shape[0]
        for x in (0, 1):
            out[rows // 2 * x : rows // 2 * (x + 1), :cut] = g_in[ff_rows(seat, x, rows // 4)]
        out[:, cut:] = g_out[block(out, seat, rows)]


def norm_one_body(h0, h1, h2, du2, n1, i1, norms, two, wo, c0, c1, c2, c3, *refs):
    d0, d2, d3, core, du1, w_own, w_across, scr = refs
    wide = d0.shape[1]
    dh = du2[...] + (h0[...] + h1[1].astype(f32) + h2[...].astype(f32))
    width = dh.shape[1]
    normed = n1[...]
    d = norm_pull(dh * norms[0:1], normed, i1[...])
    du1[...] = d
    low = d.astype(bf16)
    dc = [dot_nt(low, wo[block(wo, partner(k), wide)]).astype(bf16) for k in range(RANKS)]
    d0[...] = dc[0]
    base = 2 * scr.shape[1]
    mine = dc[1].shape[0]
    core[base : base + mine] = dc[1][:, :128]
    core[base + mine :] = jnp.concatenate([dc[1][: mine // 2, 128:], dc[1][mine // 2 :, 128:]], 1)
    d2[...] = dc[2]
    d3[...] = dc[3]
    sums = jnp.concatenate(
        [jnp.sum(dh * normed, axis=0, keepdims=True), two[0:1]]
        + [jnp.sum(dh, axis=0, keepdims=True), two[1:2], jnp.zeros((124, width), f32)],
        0,
    )
    half = width // 2
    for k, c in enumerate((c0, c1, c2, c3)):
        g = dot_tn(c[...], low).astype(bf16)
        q = partner(k)
        tail = pl.ds(pl.multiple_of(width + lax.rem(q, 2) * wide, 64), wide)
        for t in range(RANKS):
            scr[t, block(scr, q, wide)] = g[:, wide * t : wide * t + 128]
        for side in (0, 1):

            @pl.when(lax.div(q, 2) == side)
            def _():
                for t in range(RANKS):
                    rest = g[:, wide * t + 128 : wide * t + wide]
                    scr[t, tail, 64 * side : 64 * side + 64] = rest

    low_sums = sums[:8].astype(bf16)
    for t in range(RANKS):
        for j in range(width // 128):
            at = width + half + 8 * j
            scr[t, at : at + 8] = low_sums[:, 128 * j : 128 * j + 128]
    rows = scr.shape[1]
    w_own[...] = scr[partner(0)]
    core[:rows] = scr[partner(3)]
    core[rows : 2 * rows] = scr[partner(1)]
    w_across[...] = scr[partner(2)]


def attend_back_body(factor, d0, core, d2, d3, qw, qe, kk, vv, p_ref, dqkv, dc, dqw, dqe, dk, dv):
    b = lax.axis_index("blk")
    rows, wide = qw.shape
    local = rows * 4 // 5 // RANKS
    words = local * RANKS
    share = (rows - words) // RANKS
    hl = HEADS // RANKS
    dh = wide // hl
    mine = d0.shape[0]
    base = core.shape[0] - mine * 3 // 2
    tail = core[base + mine :]
    d1 = jnp.concatenate(
        [core[base : base + mine], jnp.concatenate([tail[:, :64], tail[:, 64:]], 0)], 1
    )
    for k, d in enumerate((d0[...], d1, d2[...], d3[...])):
        to = jnp.bitwise_xor(b, k)
        dc[block(dc, to, local)] = d[:local]
        dc[pl.ds(pl.multiple_of(words + to * share, share), share)] = d[local:]
    keys_t = kk[...].astype(f32).T.astype(bf16)
    lane_head = lax.broadcasted_iota(jnp.int32, (128, wide), 1) // dh
    dk[...] = jnp.zeros_like(dk)
    dv[...] = jnp.zeros_like(dv)

    def query_block(i, carry):
        at = pl.ds(pl.multiple_of(i * 128, 128), 128)
        zero = jnp.zeros((128, wide), bf16)

        def stacked(x):
            return jnp.concatenate([jnp.where(lane_head == h, x, zero) for h in range(hl)], 0)

        stack_d = stacked(dc[at])
        prob = p_ref[i]
        dp = dot_nt(vv[...], stack_d)
        parts = []
        for h in range(hl):
            lanes = slice(128 * h, 128 * h + 128)
            p = prob[:, lanes].astype(f32)
            g = dp[:, lanes]
            delta = jnp.sum(p * g, axis=0, keepdims=True)
            parts.append((p * (g - delta)).astype(bf16))
        ds = jnp.concatenate(parts, 1)
        dv[...] += dot_nn(prob, stack_d)
        dk[:words] += dot_nn(ds[:words], stacked(qw[at]))
        dk[words:] += dot_nn(ds[words:], stacked(qe[at]))
        for keys, ds_part, out in ((keys_t[:, :words], ds[:words], dqw), (keys_t[:, words:], ds[words:], dqe)):
            t = dot_nn(keys, ds_part)
            t = jnp.concatenate(
                [t[dh * h : dh * h + dh, 128 * h : 128 * h + 128] for h in range(hl)], 0
            )
            out[at] = t.T
        return carry

    lax.fori_loop(0, rows // 128, query_block, 0, unroll=True)
    dqkv[:, :wide] = (dqw[...] * factor).astype(bf16)
    dqkv[:, wide : 2 * wide] = (dqe[...] * factor).astype(bf16)
    dqkv[:, 2 * wide : 3 * wide] = dk[...].astype(bf16)
    dqkv[:, 3 * wide :] = dv[...].astype(bf16)


def proj_grads_body(dqkv, xw, xe, o0, o1, o2, *refs):
    outs, scr = refs[:-1], refs[-1]
    words = xw.shape[0]
    out_rows = o0.shape[0]
    half = dqkv.shape[1] // 2
    w = dot_tn(xw[...], dqkv[:words])
    e = dot_tn(xe[...], dqkv[words:])
    scr[:, :half] = w[:, :half].astype(bf16)
    scr[:, half : 2 * half] = (w[:, half:] + e[:, half:]).astype(bf16)
    scr[:, 2 * half : 3 * half] = e[:, :half].astype(bf16)
    o = o0[...].astype(f32) + o1[out_rows : 2 * out_rows].astype(f32) + o2[...].astype(f32)
    width = scr.shape[0]
    middle = width // 2
    tail = o[width : width + middle]
    scr[:, 3 * half : 3 * half + 128] = o[:width].astype(bf16)
    scr[:middle, 3 * half + 128 : 3 * half + 192] = tail[:, :64].astype(bf16)
    scr[middle:, 3 * half + 128 : 3 * half + 192] = tail[:, 64:].astype(bf16)
    vec = o[width + middle :]
    sums = jnp.concatenate([vec[8 * j : 8 * j + 8] for j in range(width // 128)], 1)
    sums = jnp.concatenate([sums, jnp.zeros((120, width), f32)], 0).T
    scr[:, 3 * half + 192 :] = sums[:, :64].astype(bf16)
    for j, out in enumerate(outs):
        to = ring_seat(j // 2, j % 2) if len(outs) > 1 else 0
        out[...] = scr[block(scr, to, out.shape[0])]


def total_of(*parts):
    total = parts[0][...].astype(f32)
    for part in parts[1:]:
        total = total + part[...].astype(f32)
    return total


def last_ff_body(a0, a1, a2, a3, w_out, c0, c1, c2, c3, scr):
    rows = c0.shape[0]
    width = c0.shape[1]
    t = total_of(a0, a1, a2, a3)
    w_out[...] = t[:, width:]
    scr[...] = t[:, :width]
    for k, c in enumerate((c0, c1, c2, c3)):
        c[...] = scr[block(scr, jnp.bitwise_xor(ff_rank(), k), rows)].astype(bf16)


def spread_ff_body(c0, c1, c2, c3, out, scr):
    part = out.shape[1] // (8 * RANKS)
    for k, c in enumerate((c0, c1, c2, c3)):
        scr[jnp.bitwise_xor(ff_rank(), k)] = c[...].astype(f32)
    for t in range(RANKS):
        for j in range(8):
            at = ff_column(t, j, part)
            out[:, at : at + part] = scr[t, :, part * j : part * j + part]


def last_body(a0, a1, a2, c0, c1, c2, c3, scr):
    rows = c0.shape[0]
    scr[...] = total_of(a0, a1, a2)
    for k, c in enumerate((c0, c1, c2, c3)):
        c[...] = scr[block(scr, partner(k), rows)].astype(bf16)


def finish_body(c0, c1, c2, c3, gq, gkv, go, gg, gb, scr):
    wide = go.shape[1] // RANKS
    for k, c in enumerate((c0, c1, c2, c3)):
        scr[partner(k)] = c[...].astype(f32)
    for t in range(RANKS):
        cut = slice(wide * t, wide * t + wide)
        for j, (out, i) in enumerate(((gq, 0), (gq, 1), (gkv, 0), (gkv, 1), (gq, 2), (gq, 3))):
            out[i, :, cut] = scr[t, :, wide * j : wide * j + wide]
        go[:, cut] = scr[t, :, 6 * wide : 7 * wide]
    at = 7 * wide + 64 - 128
    v = c0[:, at:].astype(f32).T
    gg[...] = v[64:66]
    gb[...] = v[66:68]


def input_body(dqkv, wq, du1, ye, own, across, core, part):
    b = lax.axis_index("blk")
    local, share = own.shape[0], ye.shape[0]
    words = RANKS * local
    half = dqkv.shape[1] // 2
    part[:words] = dot_nt(dqkv[:words], wq[:, : 2 * half])
    part[words:] = dot_nt(dqkv[words:, half:], wq[:, half : 2 * half]) + dot_nt(
        dqkv[words:, :half], wq[:, 2 * half :]
    )
    part[pl.ds(pl.multiple_of(words + b * share, share), share)] += du1[local:]
    own[...] = part[block(part, b, local)] + du1[:local]
    low = part[words:].astype(bf16)
    core[:local] = part[block(part, partner(3), local)].astype(bf16)
    core[local : 2 * local] = part[block(part, partner(1), local)].astype(bf16)
    core[2 * local : -share] = low
    core[-share:] = ye[...]
    across[:local] = part[block(part, partner(2), local)].astype(bf16)
    across[local:-share] = low
    across[-share:] = ye[...]


def input_pair_body(across, came, sent):
    share = sent.shape[0] - across.shape[0]
    local = came.shape[0] - across.shape[0]
    sent[:local] = (across[:local].astype(f32) + came[:local].astype(f32)).astype(bf16)
    pair = across[local:-share].astype(f32) + came[2 * local : -share].astype(f32)
    sent[local : -2 * share] = pair.astype(bf16)
    sent[-2 * share : -share] = across[-share:]
    sent[-share:] = came[-share:]


def input_sum_body(own, core, sent, came, gw, ge, ye):
    local = own.shape[0]
    share = ye.shape[0] // RANKS
    two = 2 * share
    gw[...] = own[...] + core[local : 2 * local].astype(f32) + came[:local].astype(f32)
    ge[...] = sent[local:-two].astype(f32) + came[local:-two].astype(f32)
    for k, rows in enumerate((sent[-two:-share], sent[-share:], came[-two:-share], came[-share:])):
        ye[block(ye, partner(k), share)] = rows


def swap(x, k):
    return lax.ppermute(x, "blk", [(i, i ^ k) for i in range(RANKS)])


def swapped(send):
    return [swap(send[k - 1], k) for k in (1, 2, 3)]


def spread(x):
    across = swap(x, 2)
    beside = swap(x, 1)
    return [beside, across, swap(across, 1)]


def plus(*parts):
    total = parts[0].astype(f32)
    for part in parts[1:]:
        total = total + part.astype(f32)
    return total.astype(bf16)


def over_x(x):
    return lax.ppermute(x, "seq", [(i, i ^ 1) for i in range(8)])


ring = (0, 1, 3, 2)


def swap_ff(x, k, direct):
    if not direct or k == 1:
        return swap(x, k)
    if k == 2:
        return over_x(x)
    return lax.ppermute(x, ("seq", "blk"), [(i, i ^ 5) for i in range(32)])


def along_ring(x, step=1):
    route = [(ring[i], ring[(i + step) % 4]) for i in range(4)]
    return lax.ppermute(x, "seq", [(2 * z + i, 2 * to + i) for z, to in route for i in (0, 1)])


def fence(*groups):
    return lax.optimization_barrier(groups)


def after(x, *before):
    return lax.optimization_barrier((x, before))[0]


def per_device(
    words,
    entities,
    segments,
    entity_counts,
    entity_anchor,
    query_weights,
    kv_weights,
    out_weight,
    ff_in,
    ff_out,
    norm_gain,
    norm_bias,
    grad_words,
    grad_entities,
):
    seqs = lax.axis_size("seq")
    direct = seqs == 8
    _, local, width = words.shape
    ents = entities.shape[1]
    share = ents // RANKS
    total = local * RANKS
    rows = total + ents
    mine = local + share
    wide = width // RANKS
    hl = HEADS // RANKS
    factor = (width // HEADS) ** (-0.5)
    part_rows = query_weights.shape[2]
    ff_part = ff_out.shape[1]
    ff = ff_part * seqs
    shards = 8 if direct else 1
    slab_cols = 7 * wide + 64
    xw_own, xe = words[0], entities[0]

    seg_ents = jnp.take_along_axis(segments, entity_anchor, axis=1)
    live = jnp.arange(ents, dtype=jnp.int32)[None, :] < entity_counts[:, None]
    segq = jnp.concatenate([segments, seg_ents], 1)
    segk = jnp.concatenate([segments, jnp.where(live, seg_ents, -1)], 1).T
    join_rows = call(join_rows_body, "join_rows", [((total, width), bf16)])

    if direct:
        pack = call(
            pack_body,
            "pack",
            [((part_rows, slab_cols), bf16)] * 4,
            [pltpu.VMEM((RANKS, part_rows, slab_cols), bf16)]
            + [pltpu.VMEM((n, part_rows, width), bf16) for n in (4, 2)]
            + [pltpu.VMEM((part_rows, width), bf16)]
            + [pltpu.VMEM((2, part_rows), bf16)] * 2
            + [pltpu.SemaphoreType.DMA((5,))],
            held=5,
            vmem=60,
        )
        pieces = pack(
            query_weights[0], kv_weights[0], out_weight[0], norm_gain[0], norm_bias[0]
        )
        pack_ff = call(
            pack_ff_body,
            "pack_ff",
            [((part_rows, ff), bf16)] * 4,
            [pltpu.VMEM((RANKS, part_rows, ff), bf16)],
        )
        ff_pieces = pack_ff(after(ff_in[0], pieces[0]))
        own = call(
            arrange_own_body, "arrange_own", [((RANKS * part_rows, slab_cols), f32)]
        )(pieces[0])
        pieces = [own[0], *swapped(pieces[1:])]

        arrange = call(
            arrange_body,
            "arrange",
            [((RANKS * part_rows, slab_cols), bf16)],
            [pltpu.VMEM((RANKS * part_rows, slab_cols), f32)],
        )
        arrange_ff = call(
            arrange_ff_body,
            "arrange_ff",
            [((RANKS * part_rows, ff + width), bf16)],
            [pltpu.VMEM((RANKS * part_rows, ff), f32)],
        )
        (slab,) = arrange(*pieces)
        xw_own, slab = fence(xw_own, slab)
        xb, xa = swap(xw_own, 1), swap(xw_own, 2)
        x0, g1 = over_x(slab), along_ring(slab)
        g1, x0, xb, ff_pieces = fence(g1, x0, xb, ff_pieces)
        x1, g2 = over_x(g1), along_ring(g1)
        came = [swap_ff(ff_pieces[k], k, direct) for k in (1, 2, 3)]
        (ff_slab,) = arrange_ff(ff_pieces[0], *came, ff_out[0])
        g2, x1, ff_slab, xa = fence(g2, x1, ff_slab, xa)
        x2, g3 = over_x(g2), along_ring(g2)
        y0, xc = swap(ff_slab, 2), swap(xa, 1)
        g3, x2, xc, segq, segk = fence(g3, x2, xc, segq, segk)
        f1, x3 = along_ring(after(ff_slab, g3)), over_x(g3)
        (xw,) = join_rows(xw_own, xb, xa, xc)
        x3, f1, y0, xw = fence(x3, f1, y0, xw)
        f2 = along_ring(f1)
        slabs = [slab, x0, g1, x1, g2, x2, g3, x3]
    else:
        vec = jnp.concatenate([norm_gain[0], norm_bias[0]], 0).T
        vec = jnp.pad(vec, ((0, 0), (0, 60)))
        six = jnp.concatenate(
            [query_weights[0, :2], kv_weights[0], query_weights[0, 2:], out_weight], 0
        )
        six = six.reshape(7, part_rows, RANKS, wide).transpose(2, 1, 0, 3)
        six = six.reshape(RANKS, part_rows, 7 * wide)
        ff_cols = ff_in[0].reshape(part_rows, seqs, RANKS, ff_part).transpose(2, 0, 1, 3)
        ff_cols = ff_cols.reshape(RANKS, part_rows, ff)
        pack = jnp.concatenate(
            [six, jnp.broadcast_to(vec, (RANKS, part_rows, 64)), ff_cols], 2
        )
        pack = lax.all_to_all(pack, "blk", 0, 0, tiled=True).reshape(RANKS * part_rows, -1)
        pack = jnp.concatenate([pack, ff_out[0]], 1)
        pack = lax.all_gather(pack, "seq", axis=0, tiled=True)
        slabs, ff_slabs = [pack[:, :slab_cols]], [pack[:, slab_cols:]]
        (xw,) = join_rows(xw_own, *spread(xw_own))

    def place(slots, last, *args):
        outs = [((width, 6 * wide), bf16), ((width, 128), bf16), ((width, wide - 64), bf16)]
        if last:
            outs += [((width * 3 // 2, 128), bf16), ((8, width), f32)]
        body = place_last_body if last else place_body
        same = len(args) - len(slots)
        name = "place_last" if last else "place"
        return call(lambda *r: body(slots, *r), name, outs, same=same)(*args)

    if direct:
        ready = place((0, 1, 2, 3, 4), False, *slabs[:5])
        wq, _, _, wo_col, norms = place((5, 6, 7), True, *ready, *slabs[5:])
    else:
        blank = [jnp.zeros((width, n), bf16) for n in (6 * wide, 128, wide - 64)]
        wq, _, _, wo_col, norms = place((0,), True, *blank, slabs[0])
    wa, wb = swap(wo_col, 2), swap(wo_col, 1)
    attend = call(
        lambda *r: attend_body(wide, factor, *r),
        "attend",
        [((mine, wide), bf16)] * 4
        + [((rows, wide), bf16)] * 4
        + [((rows // 128, rows, 128 * hl), bf16)],
        [pltpu.VMEM((rows, wide), bf16)],
        us=7,
        vmem=16,
    )
    *ctx, qw, qe, kk, vv, prob = attend(xw, xe, wq, segq, segk)
    if direct:
        ctx = after(ctx, wb)
    ctx = [ctx[0]] + swapped(ctx[1:])
    wos = [wo_col, wb, wa, swap(after(wa, ctx), 1)]
    if direct:
        f3, y1 = along_ring(f2), swap(after(f1, ctx), 2)
    join_out = call(
        join_out_body,
        "join_out",
        [((width, width), bf16)],
        [pltpu.VMEM((RANKS, width * 3 // 2, 128), bf16)],
    )
    (wo,) = join_out(*(after(wos, f3) if direct else wos))
    mix = call(
        mix_body,
        "mix",
        [((mine, width), bf16), ((mine, width), f32), ((mine, 1), f32)],
    )
    hr, n1, i1 = mix(*ctx, wo, norms, xw_own, xe)

    def place_ff(slots, *args):
        outs = [((width, ff), bf16), ((ff, width), bf16)]
        same = len(args) - len(slots)
        return call(lambda *r: place_ff_body(slots, *r), "place_ff", outs, same=same)(*args)

    across, beside = swap_ff(hr, 2, direct), swap(hr, 1)
    if direct:
        fb, y2 = along_ring(after(y0, hr), -1), swap(after(f2, hr), 2)
        ready = place_ff((0, 1, 2, 3, 4, 6), ff_slab, y0, f1, y1, f2, f3)
        across = after(across, ready)
        ff_slabs = [ff_slab, y0, f1, y1, f2, y2, f3, fb]
    hs = [hr, beside, across, swap(across, 1)]
    if direct:
        w1, w2 = place_ff((5, 7), *ready, ff_slabs[5], ff_slabs[7])
    else:
        w1, w2 = place_ff((0,), ff_slabs[0])
    feed = call(
        feed_body,
        "feed",
        [((mine, width), f32), ((mine, width), bf16), ((2, mine, width), bf16)]
        + [((RANKS, mine, ff), bf16)] * 2,
        us=3,
        vmem=14,
    )
    own, across, core, g_all, gp_all = feed(*hs, w1, w2)
    core = swap(core, 1)
    fs = [own, core, swap_ff(plus(across, core[0]), 2, direct)]
    turn = call(
        turn_body,
        "turn",
        [((local, width), bf16), ((share, width), bf16), ((mine, width), bf16)]
        + [((mine, width), f32), ((8, width), f32)],
    )
    yw, ye, df, du2, sums = turn(*fs, n1, norms, grad_words[0], grad_entities[0])

    across, beside = swap_ff(df, 2, direct), swap(df, 1)
    ds = [df, beside, across, swap(across, 1)]
    half_dz = ((2, mine, ff), bf16)
    feed_back_near = call(
        feed_back_near_body,
        "feed_back_near",
        [((mine, width), f32), ((mine, width), bf16), half_dz],
        vmem=12,
    )
    feed_back_far = call(
        feed_back_far_body,
        "feed_back_far",
        [((mine, width), bf16), ((2, mine, width), bf16), half_dz],
        vmem=12,
    )
    own, beside, dz_near = feed_back_near(*ds[:2], gp_all, w1, w2)
    across, core, dz_far = feed_back_far(*ds[2:], gp_all, w1, w2, beside)
    core = swap(core, 1)
    feed_grads = call(
        feed_grads_body,
        "feed_grads",
        [((width // shards, ff + width), bf16)] * shards,
        [pltpu.VMEM((width, ff), bf16), pltpu.VMEM((ff, width), bf16)],
        us=3,
        vmem=16,
    )
    sent = plus(across, core[0])
    ff_chunks = feed_grads(*ds, *hs, g_all, dz_near, after(dz_far, sent))
    dhs = [own, core, swap_ff(sent, 2, direct)]
    if direct:
        ff0, ff1, ff2, ff3, ff4, ff5, ff6, ff7 = ff_chunks
        fy, fz = swap(ff5, 2), along_ring(ff2)
        part = plus(ff4, after(fy, fz))
        dhs[2] = after(dhs[2], ff_chunks)
        fl = along_ring(part, -1)

    packed = width * 3 // 2 + 8 * (width // 128)
    norm_one = call(
        norm_one_body,
        "norm_one",
        [((mine, wide), bf16)] * 3
        + [((2 * packed + mine * 3 // 2, 128), bf16), ((mine, width), f32)]
        + [((packed, 128), bf16)] * 2,
        [pltpu.VMEM((RANKS, packed, 128), bf16)],
        vmem=12,
    )
    d0, d2, d3, core, du1, wo_own, across = norm_one(
        *dhs, du2, n1, i1, norms, sums, wo, *ctx
    )
    dcs = [d0, swap(core, 1), swap(d2, 2), swap(d3, 3)]
    sent = plus(across, after(dcs[1], dcs[2], dcs[3])[:packed])
    outs = [wo_own, dcs[1], swap(sent, 2)]
    dcs = after(dcs, sent)
    attend_back = call(
        lambda *r: attend_back_body(factor, *r),
        "attend_back",
        [((rows, 4 * wide), bf16)],
        [pltpu.VMEM((rows, wide), bf16)] + [pltpu.VMEM((rows, wide), f32)] * 4,
        us=7,
        vmem=16,
    )
    (dqkv,) = attend_back(*dcs, qw, qe, kk, vv, prob)
    to_input = call(
        input_body,
        "to_input",
        [((local, width), f32)]
        + [((n * local + ents + share, width), bf16) for n in (1, 2)],
        [pltpu.VMEM((rows, width), f32)],
        us=2,
        vmem=12,
    )
    own, across, core = to_input(dqkv, wq, du1, ye)
    if direct:
        own = after(own, fl)
    core = swap(core, 1)
    proj_grads = call(
        proj_grads_body,
        "proj_grads",
        [((width // shards, slab_cols), bf16)] * shards,
        [pltpu.VMEM((width, slab_cols), bf16)],
        us=2,
        vmem=14,
    )
    chunks = proj_grads(after(dqkv, own), xw, xe, *outs)
    if direct:
        fl = along_ring(plus(ff6, after(fl, dqkv)), -1)
        fb = along_ring(after(ff3, chunks))
        part = plus(chunks[2], after(over_x(chunks[3]), fl))
        fc = along_ring(after(ff7, fb), -1)
        cx, cz = over_x(after(chunks[5], part)), along_ring(part, -1)
        core = after(core, part)
    (sent,) = call(input_pair_body, "input_pair", [((local + ents + 2 * share, width), bf16)])(across, core)
    came = swap(sent, 2)
    input_sum = call(
        input_sum_body,
        "input_sum",
        [((local, width), f32), ((ents, width), f32), ((ents, width), bf16)],
    )
    if not direct:
        gxw, gxe, ye = input_sum(own, core, sent, came)

    if direct:
        last_ff = call(
            last_ff_body,
            "last_ff",
            [((ff_part, width), f32)] + [((part_rows, ff), bf16)] * 4,
            [pltpu.VMEM((RANKS * part_rows, ff), f32)],
        )
        part = plus(chunks[4], cz, after(cx, fb))
        cx, cz = over_x(after(chunks[7], part)), along_ring(part, -1)
        fy_last = swap(plus(ff1, fb, after(fc, part)), 2)
        part = plus(chunks[6], after(cz, came), cx)
        cx, cz = over_x(after(chunks[1], part)), along_ring(part, -1)
        grad_ff_out, *back = last_ff(ff0, fz, fl, after(fy_last, part))
        back = [back[0]] + [swap_ff(back[k], k, direct) for k in (1, 2, 3)]
        spread_ff = call(
            spread_ff_body,
            "spread_ff",
            [((part_rows, RANKS * ff), f32)],
            [pltpu.VMEM((RANKS, part_rows, ff), f32)],
        )
        (grad_ff_in,) = spread_ff(*back)
        gxw, gxe, ye = input_sum(own, core, sent, after(came, part))
        last = call(
            last_body,
            "last",
            [((part_rows, slab_cols), bf16)] * 4,
            [pltpu.VMEM((RANKS * part_rows, slab_cols), f32)],
        )
        back = last(chunks[0], after(cz, grad_ff_in, gxw), cx)
        back = [back[0]] + swapped(back[1:])
        finish = call(
            finish_body,
            "finish",
            [((4, part_rows, width), f32), ((2, part_rows, width), f32), ((part_rows, width), f32)]
            + [((2, part_rows), f32)] * 2,
            [pltpu.VMEM((RANKS, part_rows, slab_cols), f32)],
        )
        grad_query, grad_kv, grad_out, grad_gain, grad_bias = finish(*back)
    else:
        both = jnp.concatenate([chunks[0], ff_chunks[0]], 1)
        both = lax.psum_scatter(both, "seq", scatter_dimension=0, tiled=True)
        grad_ff_out = both[:, slab_cols + ff :].astype(f32)
        both = both[:, : slab_cols + ff].reshape(RANKS, part_rows, slab_cols + ff)
        both = lax.all_to_all(both, "blk", 0, 0, tiled=True).astype(f32)
        seven = both[:, :, : 7 * wide].reshape(RANKS, part_rows, 7, wide)
        seven = seven.transpose(2, 1, 0, 3).reshape(7, part_rows, width)
        grad_query = jnp.concatenate([seven[:2], seven[4:6]], 0)
        grad_kv, grad_out = seven[2:4], seven[6]
        vecs = both[0, :, 7 * wide : 7 * wide + 4].T
        grad_gain, grad_bias = vecs[:2], vecs[2:]
        grad_ff_in = both[:, :, slab_cols:].reshape(RANKS, part_rows, seqs, ff_part)
        grad_ff_in = grad_ff_in.transpose(1, 2, 0, 3).reshape(part_rows, RANKS * ff)
    return (
        yw[None],
        ye[None],
        gxw[None],
        gxe[None],
        grad_query[None],
        grad_kv[None],
        grad_out[None],
        grad_ff_in[None],
        grad_ff_out[None],
        grad_gain[None],
        grad_bias[None],
    )


def solution(mesh):
    placed = (
        P("seq", "blk", None),
        P("seq", None, None),
        P("seq", None),
        P("seq"),
        P("seq", None),
        P(None, None, ("seq", "blk"), None),
        P(None, None, ("seq", "blk"), None),
        P(None, ("seq", "blk"), None),
        P(None, ("seq", "blk"), None),
        P(None, ("seq", "blk"), None),
        P(None, None, ("seq", "blk")),
        P(None, None, ("seq", "blk")),
        P("seq", "blk", None),
        P("seq", None, None),
    )
    return jax.shard_map(
        per_device,
        mesh=mesh,
        in_specs=placed,
        out_specs=(
            P("seq", "blk", None),
            P("seq", None, None),
            P("seq", "blk", None),
            P("seq", None, None),
            P(None, None, ("seq", "blk"), None),
            P(None, None, ("seq", "blk"), None),
            P(None, ("seq", "blk"), None),
            P(None, ("seq", "blk"), None),
            P(None, ("seq", "blk"), None),
            P(None, None, ("seq", "blk")),
            P(None, None, ("seq", "blk")),
        ),
        check_vma=False,
    )
```

```python
import jax
import jax.numpy as jnp
from jax import lax
from jax.experimental import pallas as pl
from jax.experimental.pallas import tpu as pltpu
from jax.sharding import PartitionSpec as P

HEADS = 12
RANKS = 4
epsilon = 1e-05
masked_score = -1e30
bf16 = jnp.bfloat16
f32 = jnp.float32


def dot_nn(a, b):
    return jnp.dot(a, b, preferred_element_type=f32)


def dot_nt(a, b):
    return lax.dot_general(a, b, (((1,), (1,)), ((), ())), preferred_element_type=f32)


def dot_tn(a, b):
    return lax.dot_general(a, b, (((0,), (0,)), ((), ())), preferred_element_type=f32)


def block(ref, index, size):
    return pl.ds(pl.multiple_of(index * size, size), size)


def call(body, name, outs, scratch=(), vmem=10, us=1, held=0, same=0):
    def run(*args):
        return pl.pallas_call(
            body,
            name=name,
            out_shape=[jax.ShapeDtypeStruct(s, t) for s, t in outs],
            in_specs=[pl.BlockSpec(memory_space=pltpu.HBM)] * held
            + [pl.BlockSpec(memory_space=pltpu.VMEM)] * (len(args) - held),
            out_specs=[pl.BlockSpec(memory_space=pltpu.VMEM)] * len(outs),
            scratch_shapes=list(scratch),
            input_output_aliases={i: i for i in range(same)},
            compiler_params=pltpu.CompilerParams(vmem_limit_bytes=vmem << 20),
            cost_estimate=pl.CostEstimate(
                flops=int(us * 1e6), bytes_accessed=int(us * 1e3), transcendentals=0
            ),
        )(*args)

    return run


def partner(k):
    return jnp.bitwise_xor(lax.axis_index("blk"), k)


def ring_seat(k, e):
    s = lax.axis_index("seq")
    z = lax.div(s, 2)
    at = lax.rem(jnp.bitwise_xor(z, lax.div(z, 2)) + (k + 4), 4)
    return 2 * jnp.bitwise_xor(at, lax.div(at, 2)) + jnp.bitwise_xor(lax.rem(s, 2), e)


def ff_rank():
    return 2 * lax.rem(lax.axis_index("seq"), 2) + lax.rem(lax.axis_index("blk"), 2)


def ff_seat(k, e):
    z = lax.div(lax.axis_index("seq"), 2)
    at = lax.rem(jnp.bitwise_xor(z, lax.div(z, 2)) + (k + 4), 4)
    y = jnp.bitwise_xor(lax.div(lax.axis_index("blk"), 2), e)
    return 2 * jnp.bitwise_xor(at, lax.div(at, 2)) + y


def ff_column(rank, j, part):
    return (8 * (j // 2) + 4 * (rank // 2) + 2 * (j % 2) + rank % 2) * part


def ff_rows(seat, x, rows):
    at = 4 * lax.div(seat, 2) + 2 * x + lax.rem(seat, 2)
    return pl.ds(pl.multiple_of(2 * rows * at, 16), 2 * rows)


def norm_stats(u):
    center = u - jnp.mean(u, axis=-1, keepdims=True)
    inverse = lax.rsqrt(jnp.mean(center * center, axis=-1, keepdims=True) + epsilon)
    return center * inverse, inverse


def norm_pull(scaled, normed, inverse):
    return inverse * (
        scaled
        - jnp.mean(scaled, axis=-1, keepdims=True)
        - normed * jnp.mean(scaled * normed, axis=-1, keepdims=True)
    )


def fetch(refs, sems):
    half = len(refs) // 2
    copies = [
        pltpu.make_async_copy(source, target, sems.at[i])
        for i, (source, target) in enumerate(zip(refs[:half], refs[half:]))
    ]
    for copy in copies:
        copy.start()
    for copy in copies:
        copy.wait()


def pack_body(*refs):
    sources, outs, scr, here, sems = refs[:5], refs[5:9], refs[9], refs[10:15], refs[15]
    fetch((*sources, *here), sems)
    q, kv, wo, gain, bias = here
    rows, wide = q.shape[1], q.shape[2] // RANKS
    eye = lax.broadcasted_iota(jnp.int32, (rows, rows), 0) == lax.broadcasted_iota(
        jnp.int32, (rows, rows), 1
    )
    lane = lax.broadcasted_iota(jnp.int32, (rows, 64), 1)
    vec = jnp.zeros((rows, 64), f32)
    for j, row in enumerate((gain[0:1], gain[1:2], bias[0:1], bias[1:2])):
        column = jnp.sum(jnp.where(eye, row.astype(f32), 0.0), axis=1, keepdims=True)
        vec = jnp.where(lane == j, column, vec)
    for t in range(RANKS):
        cut = slice(wide * t, wide * t + wide)
        for j, piece in enumerate((q[0], q[1], kv[0], kv[1], q[2], q[3], wo[...])):
            scr[t, :, wide * j : wide * j + wide] = piece[:, cut]
        scr[t, :, 7 * wide :] = vec.astype(bf16)
    for k in range(RANKS):
        outs[k][...] = scr[partner(k)]


def pack_ff_body(ff, *refs):
    outs, scr = refs[:RANKS], refs[RANKS]
    part = ff.shape[1] // (8 * RANKS)
    for t in range(RANKS):
        for j in range(8):
            at = ff_column(t, j, part)
            scr[t, :, part * j : part * j + part] = ff[:, at : at + part]
    for k in range(RANKS):
        outs[k][...] = scr[jnp.bitwise_xor(ff_rank(), k)]


def arrange_own_body(p0, out):
    out[block(out, partner(0), p0.shape[0])] = p0[...].astype(f32)


def arrange_body(own, p1, p2, p3, slab, scr):
    rows = p1.shape[0]
    scr[...] = own[...]
    for k, p in ((1, p1), (2, p2), (3, p3)):
        scr[block(scr, partner(k), rows)] = p[...].astype(f32)
    slab[...] = scr[...].astype(bf16)


def arrange_ff_body(p0, p1, p2, p3, ff_out, slab, scr):
    rows, cols = p0.shape
    for k, p in enumerate((p0, p1, p2, p3)):
        scr[block(scr, jnp.bitwise_xor(ff_rank(), k), rows)] = p[...].astype(f32)
    slab[:, :cols] = scr[...].astype(bf16)
    slab[:, cols:] = ff_out[...]


def place_body(slots, *refs):
    shards, (wq, wo_first, rest) = refs[-3 - len(slots) : -3], refs[-3:]
    rows, first = shards[0].shape[0], wq.shape[1]
    for j, shard in zip(slots, shards):
        at = block(shard, ring_seat(-(j // 2), j % 2) if rows < wq.shape[0] else 0, rows)
        wq[at] = shard[:, :first]
        wo_first[at] = shard[:, first : first + 128]
        rest[at] = shard[:, first + 128 :]


def place_last_body(slots, *refs):
    wide = refs[0].shape[1] // 6
    ins, (wq, wo_first, rest, wo_col, norms) = refs[:-5], refs[-5:]
    place_body(slots, *ins, wq, wo_first, rest)
    width = wq.shape[0]
    half = width // 2
    tail = rest[...]
    wo_col[:width] = wo_first[...]
    wo_col[width:] = jnp.concatenate([tail[:half, : wide - 128], tail[half:, : wide - 128]], 1)
    norms[...] = tail.astype(f32).T[wide - 128 : wide - 120]


def place_ff_body(slots, *refs):
    shards, w1, w2 = refs[-2 - len(slots) : -2], refs[-2], refs[-1]
    rows, cut = shards[0].shape[0], w1.shape[1]
    if rows == w1.shape[0]:
        w1[...] = shards[0][:, :cut]
        w2[...] = shards[0][:, cut:]
        return
    for j, shard in zip(slots, shards):
        seat = ff_seat(-(j // 2), j % 2)
        for x in (0, 1):
            w1[ff_rows(seat, x, rows // 4)] = shard[rows // 2 * x : rows // 2 * (x + 1), :cut]
        w2[block(shard, seat, rows)] = shard[:, cut:]


def join_out_body(w0, w1, w2, w3, wo, scr):
    wide = wo.shape[1] // RANKS
    half = wo.shape[0] // 2
    for k, w in enumerate((w0, w1, w2, w3)):
        scr[partner(k)] = w[...]
    for t in range(RANKS):
        wo[:, wide * t : wide * t + 128] = scr[t, : 2 * half]
        tail = scr[t, 2 * half :]
        wo[:half, wide * t + 128 : wide * t + wide] = tail[:, : wide - 128]
        wo[half:, wide * t + 128 : wide * t + wide] = tail[:, wide - 128 :]


def join_rows_body(x0, x1, x2, x3, xw):
    local = x0.shape[0]
    for k, x in enumerate((x0, x1, x2, x3)):
        xw[block(xw, partner(k), local)] = x[...]


def attend_body(wide, factor, xw, xe, wq, segq, segk, c0, c1, c2, c3, qw, qe, kk, vv, p_ref, c_scr):
    words, ents = xw.shape[0], xe.shape[0]
    local = words // RANKS
    share = ents // RANKS
    hl = HEADS // RANKS
    dh = wide // hl
    rows = words + ents
    w = dot_nn(xw[...], wq[:, : 4 * wide])
    e_kv = dot_nn(xe[...], wq[:, 2 * wide : 4 * wide])
    e_q = dot_nn(xe[...], wq[:, 4 * wide :])
    qw[:words] = (w[:, :wide] * factor).astype(bf16)
    qe[:words] = (w[:, wide : 2 * wide] * factor).astype(bf16)
    kk[:words] = w[:, 2 * wide : 3 * wide].astype(bf16)
    vv[:words] = w[:, 3 * wide :].astype(bf16)
    qw[words:] = (e_q[:, :wide] * factor).astype(bf16)
    qe[words:] = (e_q[:, wide:] * factor).astype(bf16)
    kk[words:] = e_kv[:, :wide].astype(bf16)
    vv[words:] = e_kv[:, wide:].astype(bf16)
    values_t = vv[...].astype(f32).T.astype(bf16)
    lane_head = lax.broadcasted_iota(jnp.int32, (128, wide), 1) // dh
    segcol = segk[...]

    def query_block(i, carry):
        at = pl.ds(pl.multiple_of(i * 128, 128), 128)
        q_word, q_ent = qw[at], qe[at]
        zero = jnp.zeros_like(q_word)
        stack_w = jnp.concatenate([jnp.where(lane_head == h, q_word, zero) for h in range(hl)], 0)
        stack_e = jnp.concatenate([jnp.where(lane_head == h, q_ent, zero) for h in range(hl)], 0)
        s_w = dot_nt(kk[:words], stack_w)
        s_e = dot_nt(kk[words:], stack_e)
        allowed = segcol == segq[0:1, at]
        probs = []
        for h in range(hl):
            lanes = slice(128 * h, 128 * h + 128)
            s = jnp.concatenate([s_w[:, lanes], s_e[:, lanes]], 0)
            s = jnp.where(allowed, s, masked_score)
            top = jnp.max(s, axis=0, keepdims=True)
            e = jnp.exp(s - top)
            probs.append((e * (1.0 / jnp.sum(e, axis=0, keepdims=True))).astype(bf16))
        prob = jnp.concatenate(probs, 1)
        p_ref[i] = prob
        ctx = dot_nn(values_t, prob)
        ctx = jnp.concatenate(
            [ctx[dh * h : dh * h + dh, 128 * h : 128 * h + 128] for h in range(hl)], 0
        )
        c_scr[at] = ctx.T.astype(bf16)
        return carry

    lax.fori_loop(0, rows // 128, query_block, 0, unroll=True)
    b = lax.axis_index("blk")
    for k, out in enumerate((c0, c1, c2, c3)):
        to = jnp.bitwise_xor(b, k)
        out[:local] = c_scr[block(c_scr, to, local)]
        out[local:] = c_scr[pl.ds(pl.multiple_of(words + to * share, share), share)]


def mix_body(c0, c1, c2, c3, wo, norms, xw, xe, hr, n1, i1):
    b = lax.axis_index("blk")
    wide = c0.shape[1]
    share = hr.shape[0] - xw.shape[0]
    u = jnp.concatenate([xw[...].astype(f32), xe[block(xe, b, share)].astype(f32)], 0)
    for k, c in enumerate((c0, c1, c2, c3)):
        u = u + dot_nn(c[...], wo[block(wo, partner(k), wide)])
    normed, inverse = norm_stats(u)
    n1[...] = normed
    i1[...] = inverse
    hr[...] = (normed * norms[0:1] + norms[2:3]).astype(bf16)


def feed_body(h0, h1, h2, h3, w1, w2, own, across, core, g_all, gp_all):
    outs = (own, core.at[1], across, core.at[0])
    for k, h in enumerate((h0, h1, h2, h3)):
        z = dot_nn(h[...], w1[...])
        cdf = 0.5 * (1.0 + lax.erf(z * 0.7071067811865476))
        g = (z * cdf).astype(bf16)
        g_all[k] = g
        gp_all[k] = (cdf + z * (0.3989422804014327 * jnp.exp(-0.5 * z * z))).astype(bf16)
        outs[k][...] = dot_nn(g, w2[...]).astype(outs[k].dtype)


def turn_body(f0, f1, f2, n1, norms, gw, ge, yw, ye, df, du2, sums):
    b = lax.axis_index("blk")
    local = gw.shape[0]
    rows = n1.shape[0]
    share = rows - local
    n = norms[...]
    u = n1[...] * n[0:1] + n[2:3]
    u = u + (f0[...] + f1[1].astype(f32) + f2[...].astype(f32))
    normed, inverse = norm_stats(u)
    y = (normed * n[1:2] + n[3:4]).astype(bf16)
    yw[...] = y[:local]
    ye[...] = y[local:]
    dy = jnp.concatenate([gw[...].astype(f32), ge[block(ge, b, share)].astype(f32)], 0)
    sums[...] = jnp.concatenate(
        [jnp.sum(dy * normed, axis=0, keepdims=True), jnp.sum(dy, axis=0, keepdims=True)]
        + [jnp.zeros((6, dy.shape[1]), f32)],
        0,
    )
    d = norm_pull(dy * n[1:2], normed, inverse)
    du2[...] = d
    df[...] = d.astype(bf16)


def feed_back_near_body(d0, d1, gp_all, w1, w2, own, beside, dz):
    for k, (d, out) in enumerate(((d0, own), (d1, beside))):
        z = (dot_nt(d[...], w2[...]) * gp_all[k].astype(f32)).astype(bf16)
        dz[k] = z
        out[...] = dot_nt(z, w1[...]).astype(out.dtype)


def feed_back_far_body(d2, d3, gp_all, w1, w2, beside, across, core, dz):
    core[1] = beside[...]
    for k, (d, out) in enumerate(((d2, across), (d3, core.at[0]))):
        z = (dot_nt(d[...], w2[...]) * gp_all[2 + k].astype(f32)).astype(bf16)
        dz[k] = z
        out[...] = dot_nt(z, w1[...]).astype(out.dtype)


def feed_grads_body(d0, d1, d2, d3, h0, h1, h2, h3, g_all, dz_near, dz_far, *refs):
    outs, g_in, g_out = refs[:-2], refs[-2], refs[-1]
    d = jnp.concatenate([x[...] for x in (d0, d1, d2, d3)], 0)
    h = jnp.concatenate([x[...] for x in (h0, h1, h2, h3)], 0)
    g = jnp.concatenate([g_all[k] for k in range(RANKS)], 0)
    z = jnp.concatenate([dz_near[0], dz_near[1], dz_far[0], dz_far[1]], 0)
    g_in[...] = dot_tn(h, z).astype(bf16)
    g_out[...] = dot_tn(g, d).astype(bf16)
    cut = g_in.shape[1]
    if len(outs) == 1:
        outs[0][:, :cut] = g_in[...]
        outs[0][:, cut:] = g_out[...]
        return
    for j, out in enumerate(outs):
        seat = ff_seat(j // 2, j % 2)
        rows = out.shape[0]
        for x in (0, 1):
            out[rows // 2 * x : rows // 2 * (x + 1), :cut] = g_in[ff_rows(seat, x, rows // 4)]
        out[:, cut:] = g_out[block(out, seat, rows)]


def norm_one_body(h0, h1, h2, du2, n1, i1, norms, two, wo, c0, c1, c2, c3, *refs):
    d0, d2, d3, core, du1, w_own, w_across, scr = refs
    wide = d0.shape[1]
    dh = du2[...] + (h0[...] + h1[1].astype(f32) + h2[...].astype(f32))
    width = dh.shape[1]
    normed = n1[...]
    d = norm_pull(dh * norms[0:1], normed, i1[...])
    du1[...] = d
    low = d.astype(bf16)
    dc = [dot_nt(low, wo[block(wo, partner(k), wide)]).astype(bf16) for k in range(RANKS)]
    d0[...] = dc[0]
    base = 2 * scr.shape[1]
    mine = dc[1].shape[0]
    core[base : base + mine] = dc[1][:, :128]
    core[base + mine :] = jnp.concatenate([dc[1][: mine // 2, 128:], dc[1][mine // 2 :, 128:]], 1)
    d2[...] = dc[2]
    d3[...] = dc[3]
    sums = jnp.concatenate(
        [jnp.sum(dh * normed, axis=0, keepdims=True), two[0:1]]
        + [jnp.sum(dh, axis=0, keepdims=True), two[1:2], jnp.zeros((124, width), f32)],
        0,
    )
    half = width // 2
    for k, c in enumerate((c0, c1, c2, c3)):
        g = dot_tn(c[...], low).astype(bf16)
        q = partner(k)
        tail = pl.ds(pl.multiple_of(width + lax.rem(q, 2) * wide, 64), wide)
        for t in range(RANKS):
            scr[t, block(scr, q, wide)] = g[:, wide * t : wide * t + 128]
        for side in (0, 1):

            @pl.when(lax.div(q, 2) == side)
            def _():
                for t in range(RANKS):
                    rest = g[:, wide * t + 128 : wide * t + wide]
                    scr[t, tail, 64 * side : 64 * side + 64] = rest

    low_sums = sums[:8].astype(bf16)
    for t in range(RANKS):
        for j in range(width // 128):
            at = width + half + 8 * j
            scr[t, at : at + 8] = low_sums[:, 128 * j : 128 * j + 128]
    rows = scr.shape[1]
    w_own[...] = scr[partner(0)]
    core[:rows] = scr[partner(3)]
    core[rows : 2 * rows] = scr[partner(1)]
    w_across[...] = scr[partner(2)]


def attend_back_body(factor, d0, core, d2, d3, qw, qe, kk, vv, p_ref, dqkv, dc, dqw, dqe, dk, dv):
    b = lax.axis_index("blk")
    rows, wide = qw.shape
    local = rows * 4 // 5 // RANKS
    words = local * RANKS
    share = (rows - words) // RANKS
    hl = HEADS // RANKS
    dh = wide // hl
    mine = d0.shape[0]
    base = core.shape[0] - mine * 3 // 2
    tail = core[base + mine :]
    d1 = jnp.concatenate(
        [core[base : base + mine], jnp.concatenate([tail[:, :64], tail[:, 64:]], 0)], 1
    )
    for k, d in enumerate((d0[...], d1, d2[...], d3[...])):
        to = jnp.bitwise_xor(b, k)
        dc[block(dc, to, local)] = d[:local]
        dc[pl.ds(pl.multiple_of(words + to * share, share), share)] = d[local:]
    keys_t = kk[...].astype(f32).T.astype(bf16)
    lane_head = lax.broadcasted_iota(jnp.int32, (128, wide), 1) // dh
    dk[...] = jnp.zeros_like(dk)
    dv[...] = jnp.zeros_like(dv)

    def query_block(i, carry):
        at = pl.ds(pl.multiple_of(i * 128, 128), 128)
        zero = jnp.zeros((128, wide), bf16)

        def stacked(x):
            return jnp.concatenate([jnp.where(lane_head == h, x, zero) for h in range(hl)], 0)

        stack_d = stacked(dc[at])
        prob = p_ref[i]
        dp = dot_nt(vv[...], stack_d)
        parts = []
        for h in range(hl):
            lanes = slice(128 * h, 128 * h + 128)
            p = prob[:, lanes].astype(f32)
            g = dp[:, lanes]
            delta = jnp.sum(p * g, axis=0, keepdims=True)
            parts.append((p * (g - delta)).astype(bf16))
        ds = jnp.concatenate(parts, 1)
        dv[...] += dot_nn(prob, stack_d)
        dk[:words] += dot_nn(ds[:words], stacked(qw[at]))
        dk[words:] += dot_nn(ds[words:], stacked(qe[at]))
        for keys, ds_part, out in ((keys_t[:, :words], ds[:words], dqw), (keys_t[:, words:], ds[words:], dqe)):
            t = dot_nn(keys, ds_part)
            t = jnp.concatenate(
                [t[dh * h : dh * h + dh, 128 * h : 128 * h + 128] for h in range(hl)], 0
            )
            out[at] = t.T
        return carry

    lax.fori_loop(0, rows // 128, query_block, 0, unroll=True)
    dqkv[:, :wide] = (dqw[...] * factor).astype(bf16)
    dqkv[:, wide : 2 * wide] = (dqe[...] * factor).astype(bf16)
    dqkv[:, 2 * wide : 3 * wide] = dk[...].astype(bf16)
    dqkv[:, 3 * wide :] = dv[...].astype(bf16)


def proj_grads_body(dqkv, xw, xe, o0, o1, o2, *refs):
    outs, scr = refs[:-1], refs[-1]
    words = xw.shape[0]
    out_rows = o0.shape[0]
    half = dqkv.shape[1] // 2
    w = dot_tn(xw[...], dqkv[:words])
    e = dot_tn(xe[...], dqkv[words:])
    scr[:, :half] = w[:, :half].astype(bf16)
    scr[:, half : 2 * half] = (w[:, half:] + e[:, half:]).astype(bf16)
    scr[:, 2 * half : 3 * half] = e[:, :half].astype(bf16)
    o = o0[...].astype(f32) + o1[out_rows : 2 * out_rows].astype(f32) + o2[...].astype(f32)
    width = scr.shape[0]
    middle = width // 2
    tail = o[width : width + middle]
    scr[:, 3 * half : 3 * half + 128] = o[:width].astype(bf16)
    scr[:middle, 3 * half + 128 : 3 * half + 192] = tail[:, :64].astype(bf16)
    scr[middle:, 3 * half + 128 : 3 * half + 192] = tail[:, 64:].astype(bf16)
    vec = o[width + middle :]
    sums = jnp.concatenate([vec[8 * j : 8 * j + 8] for j in range(width // 128)], 1)
    sums = jnp.concatenate([sums, jnp.zeros((120, width), f32)], 0).T
    scr[:, 3 * half + 192 :] = sums[:, :64].astype(bf16)
    for j, out in enumerate(outs):
        to = ring_seat(j // 2, j % 2) if len(outs) > 1 else 0
        out[...] = scr[block(scr, to, out.shape[0])]


def total_of(*parts):
    total = parts[0][...].astype(f32)
    for part in parts[1:]:
        total = total + part[...].astype(f32)
    return total


def last_ff_body(a0, a1, a2, a3, w_out, c0, c1, c2, c3, scr):
    rows = c0.shape[0]
    width = c0.shape[1]
    t = total_of(a0, a1, a2, a3)
    w_out[...] = t[:, width:]
    scr[...] = t[:, :width]
    for k, c in enumerate((c0, c1, c2, c3)):
        c[...] = scr[block(scr, jnp.bitwise_xor(ff_rank(), k), rows)].astype(bf16)


def spread_ff_body(c0, c1, c2, c3, out, scr):
    part = out.shape[1] // (8 * RANKS)
    for k, c in enumerate((c0, c1, c2, c3)):
        scr[jnp.bitwise_xor(ff_rank(), k)] = c[...].astype(f32)
    for t in range(RANKS):
        for j in range(8):
            at = ff_column(t, j, part)
            out[:, at : at + part] = scr[t, :, part * j : part * j + part]


def last_body(a0, a1, a2, c0, c1, c2, c3, scr):
    rows = c0.shape[0]
    scr[...] = total_of(a0, a1, a2)
    for k, c in enumerate((c0, c1, c2, c3)):
        c[...] = scr[block(scr, partner(k), rows)].astype(bf16)


def finish_body(c0, c1, c2, c3, gq, gkv, go, gg, gb, scr):
    wide = go.shape[1] // RANKS
    for k, c in enumerate((c0, c1, c2, c3)):
        scr[partner(k)] = c[...].astype(f32)
    for t in range(RANKS):
        cut = slice(wide * t, wide * t + wide)
        for j, (out, i) in enumerate(((gq, 0), (gq, 1), (gkv, 0), (gkv, 1), (gq, 2), (gq, 3))):
            out[i, :, cut] = scr[t, :, wide * j : wide * j + wide]
        go[:, cut] = scr[t, :, 6 * wide : 7 * wide]
    at = 7 * wide + 64 - 128
    v = c0[:, at:].astype(f32).T
    gg[...] = v[64:66]
    gb[...] = v[66:68]


def input_body(dqkv, wq, du1, ye, own, across, core, part):
    b = lax.axis_index("blk")
    local, share = own.shape[0], ye.shape[0]
    words = RANKS * local
    half = dqkv.shape[1] // 2
    part[:words] = dot_nt(dqkv[:words], wq[:, : 2 * half])
    part[words:] = dot_nt(dqkv[words:, half:], wq[:, half : 2 * half]) + dot_nt(
        dqkv[words:, :half], wq[:, 2 * half :]
    )
    part[pl.ds(pl.multiple_of(words + b * share, share), share)] += du1[local:]
    own[...] = part[block(part, b, local)] + du1[:local]
    low = part[words:].astype(bf16)
    core[:local] = part[block(part, partner(3), local)].astype(bf16)
    core[local : 2 * local] = part[block(part, partner(1), local)].astype(bf16)
    core[2 * local : -share] = low
    core[-share:] = ye[...]
    across[:local] = part[block(part, partner(2), local)].astype(bf16)
    across[local:-share] = low
    across[-share:] = ye[...]


def input_pair_body(across, came, sent):
    share = sent.shape[0] - across.shape[0]
    local = came.shape[0] - across.shape[0]
    sent[:local] = (across[:local].astype(f32) + came[:local].astype(f32)).astype(bf16)
    pair = across[local:-share].astype(f32) + came[2 * local : -share].astype(f32)
    sent[local : -2 * share] = pair.astype(bf16)
    sent[-2 * share : -share] = across[-share:]
    sent[-share:] = came[-share:]


def input_sum_body(own, core, sent, came, gw, ge, ye):
    local = own.shape[0]
    share = ye.shape[0] // RANKS
    two = 2 * share
    gw[...] = own[...] + core[local : 2 * local].astype(f32) + came[:local].astype(f32)
    ge[...] = sent[local:-two].astype(f32) + came[local:-two].astype(f32)
    for k, rows in enumerate((sent[-two:-share], sent[-share:], came[-two:-share], came[-share:])):
        ye[block(ye, partner(k), share)] = rows


def swap(x, k):
    return lax.ppermute(x, "blk", [(i, i ^ k) for i in range(RANKS)])


def swapped(send):
    return [swap(send[k - 1], k) for k in (1, 2, 3)]


def spread(x):
    across = swap(x, 2)
    beside = swap(x, 1)
    return [beside, across, swap(across, 1)]


def plus(*parts):
    total = parts[0].astype(f32)
    for part in parts[1:]:
        total = total + part.astype(f32)
    return total.astype(bf16)


def over_x(x):
    return lax.ppermute(x, "seq", [(i, i ^ 1) for i in range(8)])


ring = (0, 1, 3, 2)


def swap_ff(x, k, direct):
    if not direct or k == 1:
        return swap(x, k)
    if k == 2:
        return over_x(x)
    return lax.ppermute(x, ("seq", "blk"), [(i, i ^ 5) for i in range(32)])


def along_ring(x, step=1):
    route = [(ring[i], ring[(i + step) % 4]) for i in range(4)]
    return lax.ppermute(x, "seq", [(2 * z + i, 2 * to + i) for z, to in route for i in (0, 1)])


def fence(*groups):
    return lax.optimization_barrier(groups)


def after(x, *before):
    return lax.optimization_barrier((x, before))[0]


def per_device(
    words,
    entities,
    segments,
    entity_counts,
    entity_anchor,
    query_weights,
    kv_weights,
    out_weight,
    ff_in,
    ff_out,
    norm_gain,
    norm_bias,
    grad_words,
    grad_entities,
):
    seqs = lax.axis_size("seq")
    direct = seqs == 8
    _, local, width = words.shape
    ents = entities.shape[1]
    share = ents // RANKS
    total = local * RANKS
    rows = total + ents
    mine = local + share
    wide = width // RANKS
    hl = HEADS // RANKS
    factor = (width // HEADS) ** (-0.5)
    part_rows = query_weights.shape[2]
    ff_part = ff_out.shape[1]
    ff = ff_part * seqs
    shards = 8 if direct else 1
    slab_cols = 7 * wide + 64
    xw_own, xe = words[0], entities[0]

    seg_ents = jnp.take_along_axis(segments, entity_anchor, axis=1)
    live = jnp.arange(ents, dtype=jnp.int32)[None, :] < entity_counts[:, None]
    segq = jnp.concatenate([segments, seg_ents], 1)
    segk = jnp.concatenate([segments, jnp.where(live, seg_ents, -1)], 1).T
    join_rows = call(join_rows_body, "join_rows", [((total, width), bf16)])

    if direct:
        pack = call(
            pack_body,
            "pack",
            [((part_rows, slab_cols), bf16)] * 4,
            [pltpu.VMEM((RANKS, part_rows, slab_cols), bf16)]
            + [pltpu.VMEM((n, part_rows, width), bf16) for n in (4, 2)]
            + [pltpu.VMEM((part_rows, width), bf16)]
            + [pltpu.VMEM((2, part_rows), bf16)] * 2
            + [pltpu.SemaphoreType.DMA((5,))],
            held=5,
            vmem=60,
        )
        pieces = pack(
            query_weights[0], kv_weights[0], out_weight[0], norm_gain[0], norm_bias[0]
        )
        pack_ff = call(
            pack_ff_body,
            "pack_ff",
            [((part_rows, ff), bf16)] * 4,
            [pltpu.VMEM((RANKS, part_rows, ff), bf16)],
        )
        ff_pieces = pack_ff(after(ff_in[0], pieces[0]))
        own = call(
            arrange_own_body, "arrange_own", [((RANKS * part_rows, slab_cols), f32)]
        )(pieces[0])
        pieces = [own[0], *swapped(pieces[1:])]

        arrange = call(
            arrange_body,
            "arrange",
            [((RANKS * part_rows, slab_cols), bf16)],
            [pltpu.VMEM((RANKS * part_rows, slab_cols), f32)],
        )
        arrange_ff = call(
            arrange_ff_body,
            "arrange_ff",
            [((RANKS * part_rows, ff + width), bf16)],
            [pltpu.VMEM((RANKS * part_rows, ff), f32)],
        )
        (slab,) = arrange(*pieces)
        xw_own, slab = fence(xw_own, slab)
        xb, xa = swap(xw_own, 1), swap(xw_own, 2)
        x0, g1 = over_x(slab), along_ring(slab)
        g1, x0, xb, ff_pieces = fence(g1, x0, xb, ff_pieces)
        x1, g2 = over_x(g1), along_ring(g1)
        came = [swap_ff(ff_pieces[k], k, direct) for k in (1, 2, 3)]
        (ff_slab,) = arrange_ff(ff_pieces[0], *came, ff_out[0])
        g2, x1, ff_slab, xa = fence(g2, x1, ff_slab, xa)
        x2, g3 = over_x(g2), along_ring(g2)
        y0, xc = swap(ff_slab, 2), swap(xa, 1)
        g3, x2, xc, segq, segk = fence(g3, x2, xc, segq, segk)
        f1, x3 = along_ring(after(ff_slab, g3)), over_x(g3)
        (xw,) = join_rows(xw_own, xb, xa, xc)
        x3, f1, y0, xw = fence(x3, f1, y0, xw)
        f2 = along_ring(f1)
        slabs = [slab, x0, g1, x1, g2, x2, g3, x3]
    else:
        vec = jnp.concatenate([norm_gain[0], norm_bias[0]], 0).T
        vec = jnp.pad(vec, ((0, 0), (0, 60)))
        six = jnp.concatenate(
            [query_weights[0, :2], kv_weights[0], query_weights[0, 2:], out_weight], 0
        )
        six = six.reshape(7, part_rows, RANKS, wide).transpose(2, 1, 0, 3)
        six = six.reshape(RANKS, part_rows, 7 * wide)
        ff_cols = ff_in[0].reshape(part_rows, seqs, RANKS, ff_part).transpose(2, 0, 1, 3)
        ff_cols = ff_cols.reshape(RANKS, part_rows, ff)
        pack = jnp.concatenate(
            [six, jnp.broadcast_to(vec, (RANKS, part_rows, 64)), ff_cols], 2
        )
        pack = lax.all_to_all(pack, "blk", 0, 0, tiled=True).reshape(RANKS * part_rows, -1)
        pack = jnp.concatenate([pack, ff_out[0]], 1)
        pack = lax.all_gather(pack, "seq", axis=0, tiled=True)
        slabs, ff_slabs = [pack[:, :slab_cols]], [pack[:, slab_cols:]]
        (xw,) = join_rows(xw_own, *spread(xw_own))

    def place(slots, last, *args):
        outs = [((width, 6 * wide), bf16), ((width, 128), bf16), ((width, wide - 64), bf16)]
        if last:
            outs += [((width * 3 // 2, 128), bf16), ((8, width), f32)]
        body = place_last_body if last else place_body
        same = len(args) - len(slots)
        name = "place_last" if last else "place"
        return call(lambda *r: body(slots, *r), name, outs, same=same)(*args)

    if direct:
        ready = place((0, 1, 2, 3, 4), False, *slabs[:5])
        wq, _, _, wo_col, norms = place((5, 6, 7), True, *ready, *slabs[5:])
    else:
        blank = [jnp.zeros((width, n), bf16) for n in (6 * wide, 128, wide - 64)]
        wq, _, _, wo_col, norms = place((0,), True, *blank, slabs[0])
    wa, wb = swap(wo_col, 2), swap(wo_col, 1)
    attend = call(
        lambda *r: attend_body(wide, factor, *r),
        "attend",
        [((mine, wide), bf16)] * 4
        + [((rows, wide), bf16)] * 4
        + [((rows // 128, rows, 128 * hl), bf16)],
        [pltpu.VMEM((rows, wide), bf16)],
        us=7,
        vmem=16,
    )
    *ctx, qw, qe, kk, vv, prob = attend(xw, xe, wq, segq, segk)
    if direct:
        ctx = after(ctx, wb)
    ctx = [ctx[0]] + swapped(ctx[1:])
    wos = [wo_col, wb, wa, swap(after(wa, ctx), 1)]
    if direct:
        f3, y1 = along_ring(f2), swap(after(f1, ctx), 2)
    join_out = call(
        join_out_body,
        "join_out",
        [((width, width), bf16)],
        [pltpu.VMEM((RANKS, width * 3 // 2, 128), bf16)],
    )
    (wo,) = join_out(*(after(wos, f3) if direct else wos))
    mix = call(
        mix_body,
        "mix",
        [((mine, width), bf16), ((mine, width), f32), ((mine, 1), f32)],
    )
    hr, n1, i1 = mix(*ctx, wo, norms, xw_own, xe)

    def place_ff(slots, *args):
        outs = [((width, ff), bf16), ((ff, width), bf16)]
        same = len(args) - len(slots)
        return call(lambda *r: place_ff_body(slots, *r), "place_ff", outs, same=same)(*args)

    across, beside = swap_ff(hr, 2, direct), swap(hr, 1)
    if direct:
        fb, y2 = along_ring(after(y0, hr), -1), swap(after(f2, hr), 2)
        ready = place_ff((0, 1, 2, 3, 4, 6), ff_slab, y0, f1, y1, f2, f3)
        across = after(across, ready)
        ff_slabs = [ff_slab, y0, f1, y1, f2, y2, f3, fb]
    hs = [hr, beside, across, swap(across, 1)]
    if direct:
        w1, w2 = place_ff((5, 7), *ready, ff_slabs[5], ff_slabs[7])
    else:
        w1, w2 = place_ff((0,), ff_slabs[0])
    feed = call(
        feed_body,
        "feed",
        [((mine, width), f32), ((mine, width), bf16), ((2, mine, width), bf16)]
        + [((RANKS, mine, ff), bf16)] * 2,
        us=3,
        vmem=14,
    )
    own, across, core, g_all, gp_all = feed(*hs, w1, w2)
    core = swap(core, 1)
    fs = [own, core, swap_ff(plus(across, core[0]), 2, direct)]
    turn = call(
        turn_body,
        "turn",
        [((local, width), bf16), ((share, width), bf16), ((mine, width), bf16)]
        + [((mine, width), f32), ((8, width), f32)],
    )
    yw, ye, df, du2, sums = turn(*fs, n1, norms, grad_words[0], grad_entities[0])

    across, beside = swap_ff(df, 2, direct), swap(df, 1)
    ds = [df, beside, across, swap(across, 1)]
    half_dz = ((2, mine, ff), bf16)
    feed_back_near = call(
        feed_back_near_body,
        "feed_back_near",
        [((mine, width), f32), ((mine, width), bf16), half_dz],
        vmem=12,
    )
    feed_back_far = call(
        feed_back_far_body,
        "feed_back_far",
        [((mine, width), bf16), ((2, mine, width), bf16), half_dz],
        vmem=12,
    )
    own, beside, dz_near = feed_back_near(*ds[:2], gp_all, w1, w2)
    across, core, dz_far = feed_back_far(*ds[2:], gp_all, w1, w2, beside)
    core = swap(core, 1)
    feed_grads = call(
        feed_grads_body,
        "feed_grads",
        [((width // shards, ff + width), bf16)] * shards,
        [pltpu.VMEM((width, ff), bf16), pltpu.VMEM((ff, width), bf16)],
        us=3,
        vmem=16,
    )
    sent = plus(across, core[0])
    ff_chunks = feed_grads(*ds, *hs, g_all, dz_near, after(dz_far, sent))
    dhs = [own, core, swap_ff(sent, 2, direct)]
    if direct:
        ff0, ff1, ff2, ff3, ff4, ff5, ff6, ff7 = ff_chunks
        fy, fz = swap(ff5, 2), along_ring(ff2)
        part = plus(ff4, after(fy, fz))
        dhs[2] = after(dhs[2], ff_chunks)
        fl = along_ring(part, -1)

    packed = width * 3 // 2 + 8 * (width // 128)
    norm_one = call(
        norm_one_body,
        "norm_one",
        [((mine, wide), bf16)] * 3
        + [((2 * packed + mine * 3 // 2, 128), bf16), ((mine, width), f32)]
        + [((packed, 128), bf16)] * 2,
        [pltpu.VMEM((RANKS, packed, 128), bf16)],
        vmem=12,
    )
    d0, d2, d3, core, du1, wo_own, across = norm_one(
        *dhs, du2, n1, i1, norms, sums, wo, *ctx
    )
    dcs = [d0, swap(core, 1), swap(d2, 2), swap(d3, 3)]
    sent = plus(across, after(dcs[1], dcs[2], dcs[3])[:packed])
    outs = [wo_own, dcs[1], swap(sent, 2)]
    dcs = after(dcs, sent)
    attend_back = call(
        lambda *r: attend_back_body(factor, *r),
        "attend_back",
        [((rows, 4 * wide), bf16)],
        [pltpu.VMEM((rows, wide), bf16)] + [pltpu.VMEM((rows, wide), f32)] * 4,
        us=7,
        vmem=16,
    )
    (dqkv,) = attend_back(*dcs, qw, qe, kk, vv, prob)
    to_input = call(
        input_body,
        "to_input",
        [((local, width), f32)]
        + [((n * local + ents + share, width), bf16) for n in (1, 2)],
        [pltpu.VMEM((rows, width), f32)],
        us=2,
        vmem=12,
    )
    own, across, core = to_input(dqkv, wq, du1, ye)
    if direct:
        own = after(own, fl)
    core = swap(core, 1)
    proj_grads = call(
        proj_grads_body,
        "proj_grads",
        [((width // shards, slab_cols), bf16)] * shards,
        [pltpu.VMEM((width, slab_cols), bf16)],
        us=2,
        vmem=14,
    )
    chunks = proj_grads(after(dqkv, own), xw, xe, *outs)
    if direct:
        fl = along_ring(plus(ff6, after(fl, dqkv)), -1)
        fb, fc = along_ring(after(ff3, dqkv)), along_ring(after(ff7, chunks), -1)
        part = plus(chunks[2], after(over_x(chunks[3]), fl, fb))
        cx, cz = over_x(after(chunks[5], part)), along_ring(part, -1)
        core = after(core, part)
    (sent,) = call(input_pair_body, "input_pair", [((local + ents + 2 * share, width), bf16)])(across, core)
    came = swap(sent, 2)
    input_sum = call(
        input_sum_body,
        "input_sum",
        [((local, width), f32), ((ents, width), f32), ((ents, width), bf16)],
    )
    if not direct:
        gxw, gxe, ye = input_sum(own, core, sent, came)

    if direct:
        last_ff = call(
            last_ff_body,
            "last_ff",
            [((ff_part, width), f32)] + [((part_rows, ff), bf16)] * 4,
            [pltpu.VMEM((RANKS * part_rows, ff), f32)],
        )
        part = plus(chunks[4], cz, cx)
        cx, cz = over_x(after(chunks[7], part)), along_ring(part, -1)
        fy_last = swap(plus(ff1, fb, after(fc, part)), 2)
        part = plus(chunks[6], after(cz, came), cx)
        cx, cz = over_x(after(chunks[1], part)), along_ring(part, -1)
        grad_ff_out, *back = last_ff(ff0, fz, fl, after(fy_last, part))
        back = [back[0]] + [swap_ff(back[k], k, direct) for k in (1, 2, 3)]
        spread_ff = call(
            spread_ff_body,
            "spread_ff",
            [((part_rows, RANKS * ff), f32)],
            [pltpu.VMEM((RANKS, part_rows, ff), f32)],
        )
        (grad_ff_in,) = spread_ff(*back)
        gxw, gxe, ye = input_sum(own, core, sent, after(came, part))
        last = call(
            last_body,
            "last",
            [((part_rows, slab_cols), bf16)] * 4,
            [pltpu.VMEM((RANKS * part_rows, slab_cols), f32)],
        )
        back = last(chunks[0], after(cz, grad_ff_in, gxw), cx)
        back = [back[0]] + swapped(back[1:])
        finish = call(
            finish_body,
            "finish",
            [((4, part_rows, width), f32), ((2, part_rows, width), f32), ((part_rows, width), f32)]
            + [((2, part_rows), f32)] * 2,
            [pltpu.VMEM((RANKS, part_rows, slab_cols), f32)],
        )
        grad_query, grad_kv, grad_out, grad_gain, grad_bias = finish(*back)
    else:
        both = jnp.concatenate([chunks[0], ff_chunks[0]], 1)
        both = lax.psum_scatter(both, "seq", scatter_dimension=0, tiled=True)
        grad_ff_out = both[:, slab_cols + ff :].astype(f32)
        both = both[:, : slab_cols + ff].reshape(RANKS, part_rows, slab_cols + ff)
        both = lax.all_to_all(both, "blk", 0, 0, tiled=True).astype(f32)
        seven = both[:, :, : 7 * wide].reshape(RANKS, part_rows, 7, wide)
        seven = seven.transpose(2, 1, 0, 3).reshape(7, part_rows, width)
        grad_query = jnp.concatenate([seven[:2], seven[4:6]], 0)
        grad_kv, grad_out = seven[2:4], seven[6]
        vecs = both[0, :, 7 * wide : 7 * wide + 4].T
        grad_gain, grad_bias = vecs[:2], vecs[2:]
        grad_ff_in = both[:, :, slab_cols:].reshape(RANKS, part_rows, seqs, ff_part)
        grad_ff_in = grad_ff_in.transpose(1, 2, 0, 3).reshape(part_rows, RANKS * ff)
    return (
        yw[None],
        ye[None],
        gxw[None],
        gxe[None],
        grad_query[None],
        grad_kv[None],
        grad_out[None],
        grad_ff_in[None],
        grad_ff_out[None],
        grad_gain[None],
        grad_bias[None],
    )


def solution(mesh):
    placed = (
        P("seq", "blk", None),
        P("seq", None, None),
        P("seq", None),
        P("seq"),
        P("seq", None),
        P(None, None, ("seq", "blk"), None),
        P(None, None, ("seq", "blk"), None),
        P(None, ("seq", "blk"), None),
        P(None, ("seq", "blk"), None),
        P(None, ("seq", "blk"), None),
        P(None, None, ("seq", "blk")),
        P(None, None, ("seq", "blk")),
        P("seq", "blk", None),
        P("seq", None, None),
    )
    return jax.shard_map(
        per_device,
        mesh=mesh,
        in_specs=placed,
        out_specs=(
            P("seq", "blk", None),
            P("seq", None, None),
            P("seq", "blk", None),
            P("seq", None, None),
            P(None, None, ("seq", "blk"), None),
            P(None, None, ("seq", "blk"), None),
            P(None, ("seq", "blk"), None),
            P(None, ("seq", "blk"), None),
            P(None, ("seq", "blk"), None),
            P(None, None, ("seq", "blk")),
            P(None, None, ("seq", "blk")),
        ),
        check_vma=False,
    )
```

```python
import jax
import jax.numpy as jnp
from jax import lax
from jax.experimental import pallas as pl
from jax.experimental.pallas import tpu as pltpu
from jax.sharding import PartitionSpec as P

HEADS = 12
RANKS = 4
epsilon = 1e-05
masked_score = -1e30
bf16 = jnp.bfloat16
f32 = jnp.float32


def dot_nn(a, b):
    return jnp.dot(a, b, preferred_element_type=f32)


def dot_nt(a, b):
    return lax.dot_general(a, b, (((1,), (1,)), ((), ())), preferred_element_type=f32)


def dot_tn(a, b):
    return lax.dot_general(a, b, (((0,), (0,)), ((), ())), preferred_element_type=f32)


def block(ref, index, size):
    return pl.ds(pl.multiple_of(index * size, size), size)


def call(body, name, outs, scratch=(), vmem=10, us=1, held=0, same=0):
    def run(*args):
        return pl.pallas_call(
            body,
            name=name,
            out_shape=[jax.ShapeDtypeStruct(s, t) for s, t in outs],
            in_specs=[pl.BlockSpec(memory_space=pltpu.HBM)] * held
            + [pl.BlockSpec(memory_space=pltpu.VMEM)] * (len(args) - held),
            out_specs=[pl.BlockSpec(memory_space=pltpu.VMEM)] * len(outs),
            scratch_shapes=list(scratch),
            input_output_aliases={i: i for i in range(same)},
            compiler_params=pltpu.CompilerParams(vmem_limit_bytes=vmem << 20),
            cost_estimate=pl.CostEstimate(
                flops=int(us * 1e6), bytes_accessed=int(us * 1e3), transcendentals=0
            ),
        )(*args)

    return run


def partner(k):
    return jnp.bitwise_xor(lax.axis_index("blk"), k)


def ring_seat(k, e):
    s = lax.axis_index("seq")
    z = lax.div(s, 2)
    at = lax.rem(jnp.bitwise_xor(z, lax.div(z, 2)) + (k + 4), 4)
    return 2 * jnp.bitwise_xor(at, lax.div(at, 2)) + jnp.bitwise_xor(lax.rem(s, 2), e)


def ff_rank():
    return 2 * lax.rem(lax.axis_index("seq"), 2) + lax.rem(lax.axis_index("blk"), 2)


def ff_seat(k, e):
    z = lax.div(lax.axis_index("seq"), 2)
    at = lax.rem(jnp.bitwise_xor(z, lax.div(z, 2)) + (k + 4), 4)
    y = jnp.bitwise_xor(lax.div(lax.axis_index("blk"), 2), e)
    return 2 * jnp.bitwise_xor(at, lax.div(at, 2)) + y


def ff_column(rank, j, part):
    return (8 * (j // 2) + 4 * (rank // 2) + 2 * (j % 2) + rank % 2) * part


def ff_rows(seat, x, rows):
    at = 4 * lax.div(seat, 2) + 2 * x + lax.rem(seat, 2)
    return pl.ds(pl.multiple_of(2 * rows * at, 16), 2 * rows)


def norm_stats(u):
    center = u - jnp.mean(u, axis=-1, keepdims=True)
    inverse = lax.rsqrt(jnp.mean(center * center, axis=-1, keepdims=True) + epsilon)
    return center * inverse, inverse


def norm_pull(scaled, normed, inverse):
    return inverse * (
        scaled
        - jnp.mean(scaled, axis=-1, keepdims=True)
        - normed * jnp.mean(scaled * normed, axis=-1, keepdims=True)
    )


def fetch(refs, sems):
    half = len(refs) // 2
    copies = [
        pltpu.make_async_copy(source, target, sems.at[i])
        for i, (source, target) in enumerate(zip(refs[:half], refs[half:]))
    ]
    for copy in copies:
        copy.start()
    for copy in copies:
        copy.wait()


def pack_body(*refs):
    sources, outs, scr, here, sems = refs[:5], refs[5:9], refs[9], refs[10:15], refs[15]
    fetch((*sources, *here), sems)
    q, kv, wo, gain, bias = here
    rows, wide = q.shape[1], q.shape[2] // RANKS
    eye = lax.broadcasted_iota(jnp.int32, (rows, rows), 0) == lax.broadcasted_iota(
        jnp.int32, (rows, rows), 1
    )
    lane = lax.broadcasted_iota(jnp.int32, (rows, 64), 1)
    vec = jnp.zeros((rows, 64), f32)
    for j, row in enumerate((gain[0:1], gain[1:2], bias[0:1], bias[1:2])):
        column = jnp.sum(jnp.where(eye, row.astype(f32), 0.0), axis=1, keepdims=True)
        vec = jnp.where(lane == j, column, vec)
    for t in range(RANKS):
        cut = slice(wide * t, wide * t + wide)
        for j, piece in enumerate((q[0], q[1], kv[0], kv[1], q[2], q[3], wo[...])):
            scr[t, :, wide * j : wide * j + wide] = piece[:, cut]
        scr[t, :, 7 * wide :] = vec.astype(bf16)
    for k in range(RANKS):
        outs[k][...] = scr[partner(k)]


def pack_ff_body(ff, *refs):
    outs, scr = refs[:RANKS], refs[RANKS]
    part = ff.shape[1] // (8 * RANKS)
    for t in range(RANKS):
        for j in range(8):
            at = ff_column(t, j, part)
            scr[t, :, part * j : part * j + part] = ff[:, at : at + part]
    for k in range(RANKS):
        outs[k][...] = scr[jnp.bitwise_xor(ff_rank(), k)]


def arrange_own_body(p0, out):
    out[block(out, partner(0), p0.shape[0])] = p0[...].astype(f32)


def arrange_body(own, p1, p2, p3, slab, scr):
    rows = p1.shape[0]
    scr[...] = own[...]
    for k, p in ((1, p1), (2, p2), (3, p3)):
        scr[block(scr, partner(k), rows)] = p[...].astype(f32)
    slab[...] = scr[...].astype(bf16)


def arrange_ff_body(p0, p1, p2, p3, ff_out, slab, scr):
    rows, cols = p0.shape
    for k, p in enumerate((p0, p1, p2, p3)):
        scr[block(scr, jnp.bitwise_xor(ff_rank(), k), rows)] = p[...].astype(f32)
    slab[:, :cols] = scr[...].astype(bf16)
    slab[:, cols:] = ff_out[...]


def place_body(slots, *refs):
    shards, (wq, wo_first, rest) = refs[-3 - len(slots) : -3], refs[-3:]
    rows, first = shards[0].shape[0], wq.shape[1]
    for j, shard in zip(slots, shards):
        at = block(shard, ring_seat(-(j // 2), j % 2) if rows < wq.shape[0] else 0, rows)
        wq[at] = shard[:, :first]
        wo_first[at] = shard[:, first : first + 128]
        rest[at] = shard[:, first + 128 :]


def place_last_body(slots, *refs):
    wide = refs[0].shape[1] // 6
    ins, (wq, wo_first, rest, wo_col, norms) = refs[:-5], refs[-5:]
    place_body(slots, *ins, wq, wo_first, rest)
    width = wq.shape[0]
    half = width // 2
    tail = rest[...]
    wo_col[:width] = wo_first[...]
    wo_col[width:] = jnp.concatenate([tail[:half, : wide - 128], tail[half:, : wide - 128]], 1)
    norms[...] = tail.astype(f32).T[wide - 128 : wide - 120]


def place_ff_body(slots, *refs):
    shards, w1, w2 = refs[-2 - len(slots) : -2], refs[-2], refs[-1]
    rows, cut = shards[0].shape[0], w1.shape[1]
    if rows == w1.shape[0]:
        w1[...] = shards[0][:, :cut]
        w2[...] = shards[0][:, cut:]
        return
    for j, shard in zip(slots, shards):
        seat = ff_seat(-(j // 2), j % 2)
        for x in (0, 1):
            w1[ff_rows(seat, x, rows // 4)] = shard[rows // 2 * x : rows // 2 * (x + 1), :cut]
        w2[block(shard, seat, rows)] = shard[:, cut:]


def join_out_body(w0, w1, w2, w3, wo, scr):
    wide = wo.shape[1] // RANKS
    half = wo.shape[0] // 2
    for k, w in enumerate((w0, w1, w2, w3)):
        scr[partner(k)] = w[...]
    for t in range(RANKS):
        wo[:, wide * t : wide * t + 128] = scr[t, : 2 * half]
        tail = scr[t, 2 * half :]
        wo[:half, wide * t + 128 : wide * t + wide] = tail[:, : wide - 128]
        wo[half:, wide * t + 128 : wide * t + wide] = tail[:, wide - 128 :]


def join_rows_body(x0, x1, x2, x3, xw):
    local = x0.shape[0]
    for k, x in enumerate((x0, x1, x2, x3)):
        xw[block(xw, partner(k), local)] = x[...]


def attend_body(wide, factor, xw, xe, wq, segq, segk, c0, c1, c2, c3, qw, qe, kk, vv, p_ref, c_scr):
    words, ents = xw.shape[0], xe.shape[0]
    local = words // RANKS
    share = ents // RANKS
    hl = HEADS // RANKS
    dh = wide // hl
    rows = words + ents
    w = dot_nn(xw[...], wq[:, : 4 * wide])
    e_kv = dot_nn(xe[...], wq[:, 2 * wide : 4 * wide])
    e_q = dot_nn(xe[...], wq[:, 4 * wide :])
    qw[:words] = (w[:, :wide] * factor).astype(bf16)
    qe[:words] = (w[:, wide : 2 * wide] * factor).astype(bf16)
    kk[:words] = w[:, 2 * wide : 3 * wide].astype(bf16)
    vv[:words] = w[:, 3 * wide :].astype(bf16)
    qw[words:] = (e_q[:, :wide] * factor).astype(bf16)
    qe[words:] = (e_q[:, wide:] * factor).astype(bf16)
    kk[words:] = e_kv[:, :wide].astype(bf16)
    vv[words:] = e_kv[:, wide:].astype(bf16)
    values_t = vv[...].astype(f32).T.astype(bf16)
    lane_head = lax.broadcasted_iota(jnp.int32, (128, wide), 1) // dh
    segcol = segk[...]

    def query_block(i, carry):
        at = pl.ds(pl.multiple_of(i * 128, 128), 128)
        q_word, q_ent = qw[at], qe[at]
        zero = jnp.zeros_like(q_word)
        stack_w = jnp.concatenate([jnp.where(lane_head == h, q_word, zero) for h in range(hl)], 0)
        stack_e = jnp.concatenate([jnp.where(lane_head == h, q_ent, zero) for h in range(hl)], 0)
        s_w = dot_nt(kk[:words], stack_w)
        s_e = dot_nt(kk[words:], stack_e)
        allowed = segcol == segq[0:1, at]
        probs = []
        for h in range(hl):
            lanes = slice(128 * h, 128 * h + 128)
            s = jnp.concatenate([s_w[:, lanes], s_e[:, lanes]], 0)
            s = jnp.where(allowed, s, masked_score)
            top = jnp.max(s, axis=0, keepdims=True)
            e = jnp.exp(s - top)
            probs.append((e * (1.0 / jnp.sum(e, axis=0, keepdims=True))).astype(bf16))
        prob = jnp.concatenate(probs, 1)
        p_ref[i] = prob
        ctx = dot_nn(values_t, prob)
        ctx = jnp.concatenate(
            [ctx[dh * h : dh * h + dh, 128 * h : 128 * h + 128] for h in range(hl)], 0
        )
        c_scr[at] = ctx.T.astype(bf16)
        return carry

    lax.fori_loop(0, rows // 128, query_block, 0, unroll=True)
    b = lax.axis_index("blk")
    for k, out in enumerate((c0, c1, c2, c3)):
        to = jnp.bitwise_xor(b, k)
        out[:local] = c_scr[block(c_scr, to, local)]
        out[local:] = c_scr[pl.ds(pl.multiple_of(words + to * share, share), share)]


def mix_body(c0, c1, c2, c3, wo, norms, xw, xe, hr, n1, i1):
    b = lax.axis_index("blk")
    wide = c0.shape[1]
    share = hr.shape[0] - xw.shape[0]
    u = jnp.concatenate([xw[...].astype(f32), xe[block(xe, b, share)].astype(f32)], 0)
    for k, c in enumerate((c0, c1, c2, c3)):
        u = u + dot_nn(c[...], wo[block(wo, partner(k), wide)])
    normed, inverse = norm_stats(u)
    n1[...] = normed
    i1[...] = inverse
    hr[...] = (normed * norms[0:1] + norms[2:3]).astype(bf16)


def feed_body(h0, h1, h2, h3, w1, w2, own, across, core, g_all, gp_all):
    outs = (own, core.at[1], across, core.at[0])
    for k, h in enumerate((h0, h1, h2, h3)):
        z = dot_nn(h[...], w1[...])
        cdf = 0.5 * (1.0 + lax.erf(z * 0.7071067811865476))
        g = (z * cdf).astype(bf16)
        g_all[k] = g
        gp_all[k] = (cdf + z * (0.3989422804014327 * jnp.exp(-0.5 * z * z))).astype(bf16)
        outs[k][...] = dot_nn(g, w2[...]).astype(outs[k].dtype)


def turn_body(f0, f1, f2, n1, norms, gw, ge, yw, ye, df, du2, sums):
    b = lax.axis_index("blk")
    local = gw.shape[0]
    rows = n1.shape[0]
    share = rows - local
    n = norms[...]
    u = n1[...] * n[0:1] + n[2:3]
    u = u + (f0[...] + f1[1].astype(f32) + f2[...].astype(f32))
    normed, inverse = norm_stats(u)
    y = (normed * n[1:2] + n[3:4]).astype(bf16)
    yw[...] = y[:local]
    ye[...] = y[local:]
    dy = jnp.concatenate([gw[...].astype(f32), ge[block(ge, b, share)].astype(f32)], 0)
    sums[...] = jnp.concatenate(
        [jnp.sum(dy * normed, axis=0, keepdims=True), jnp.sum(dy, axis=0, keepdims=True)]
        + [jnp.zeros((6, dy.shape[1]), f32)],
        0,
    )
    d = norm_pull(dy * n[1:2], normed, inverse)
    du2[...] = d
    df[...] = d.astype(bf16)


def feed_back_near_body(d0, d1, gp_all, w1, w2, own, beside, dz):
    for k, (d, out) in enumerate(((d0, own), (d1, beside))):
        z = (dot_nt(d[...], w2[...]) * gp_all[k].astype(f32)).astype(bf16)
        dz[k] = z
        out[...] = dot_nt(z, w1[...]).astype(out.dtype)


def feed_back_far_body(d2, d3, gp_all, w1, w2, beside, across, core, dz):
    core[1] = beside[...]
    for k, (d, out) in enumerate(((d2, across), (d3, core.at[0]))):
        z = (dot_nt(d[...], w2[...]) * gp_all[2 + k].astype(f32)).astype(bf16)
        dz[k] = z
        out[...] = dot_nt(z, w1[...]).astype(out.dtype)


def feed_grads_body(d0, d1, d2, d3, h0, h1, h2, h3, g_all, dz_near, dz_far, *refs):
    outs, g_in, g_out = refs[:-2], refs[-2], refs[-1]
    d = jnp.concatenate([x[...] for x in (d0, d1, d2, d3)], 0)
    h = jnp.concatenate([x[...] for x in (h0, h1, h2, h3)], 0)
    g = jnp.concatenate([g_all[k] for k in range(RANKS)], 0)
    z = jnp.concatenate([dz_near[0], dz_near[1], dz_far[0], dz_far[1]], 0)
    g_in[...] = dot_tn(h, z).astype(bf16)
    g_out[...] = dot_tn(g, d).astype(bf16)
    cut = g_in.shape[1]
    if len(outs) == 1:
        outs[0][:, :cut] = g_in[...]
        outs[0][:, cut:] = g_out[...]
        return
    for j, out in enumerate(outs):
        seat = ff_seat(j // 2, j % 2)
        rows = out.shape[0]
        for x in (0, 1):
            out[rows // 2 * x : rows // 2 * (x + 1), :cut] = g_in[ff_rows(seat, x, rows // 4)]
        out[:, cut:] = g_out[block(out, seat, rows)]


def norm_one_body(h0, h1, h2, du2, n1, i1, norms, two, wo, c0, c1, c2, c3, *refs):
    d0, d2, d3, core, du1, w_own, w_across, scr, whole = refs
    wide = d0.shape[1]
    dh = du2[...] + (h0[...] + h1[1].astype(f32) + h2[...].astype(f32))
    width = dh.shape[1]
    normed = n1[...]
    d = norm_pull(dh * norms[0:1], normed, i1[...])
    du1[...] = d
    low = d.astype(bf16)
    dc = [dot_nt(low, wo[block(wo, partner(k), wide)]).astype(bf16) for k in range(RANKS)]
    d0[...] = dc[0]
    base = 2 * scr.shape[1]
    mine = dc[1].shape[0]
    core[base : base + mine] = dc[1][:, :128]
    core[base + mine :] = jnp.concatenate([dc[1][: mine // 2, 128:], dc[1][mine // 2 :, 128:]], 1)
    d2[...] = dc[2]
    d3[...] = dc[3]
    sums = jnp.concatenate(
        [jnp.sum(dh * normed, axis=0, keepdims=True), two[0:1]]
        + [jnp.sum(dh, axis=0, keepdims=True), two[1:2], jnp.zeros((124, width), f32)],
        0,
    )
    half = width // 2
    for k, c in enumerate((c0, c1, c2, c3)):
        whole[block(whole, partner(k), wide)] = dot_tn(c[...], low).astype(bf16)
    for t in range(RANKS):
        at = wide * t
        scr[t, :width] = whole[:, at : at + 128]
        rest = slice(at + 128, at + wide)
        scr[t, width : width + half] = jnp.concatenate([whole[:half, rest], whole[half:, rest]], 1)

    low_sums = sums[:8].astype(bf16)
    for t in range(RANKS):
        for j in range(width // 128):
            at = width + half + 8 * j
            scr[t, at : at + 8] = low_sums[:, 128 * j : 128 * j + 128]
    rows = scr.shape[1]
    w_own[...] = scr[partner(0)]
    core[:rows] = scr[partner(3)]
    core[rows : 2 * rows] = scr[partner(1)]
    w_across[...] = scr[partner(2)]


def attend_back_body(factor, d0, core, d2, d3, qw, qe, kk, vv, p_ref, dqkv, dc, dqw, dqe, dk, dv):
    b = lax.axis_index("blk")
    rows, wide = qw.shape
    local = rows * 4 // 5 // RANKS
    words = local * RANKS
    share = (rows - words) // RANKS
    hl = HEADS // RANKS
    dh = wide // hl
    mine = d0.shape[0]
    base = core.shape[0] - mine * 3 // 2
    tail = core[base + mine :]
    d1 = jnp.concatenate(
        [core[base : base + mine], jnp.concatenate([tail[:, :64], tail[:, 64:]], 0)], 1
    )
    for k, d in enumerate((d0[...], d1, d2[...], d3[...])):
        to = jnp.bitwise_xor(b, k)
        dc[block(dc, to, local)] = d[:local]
        dc[pl.ds(pl.multiple_of(words + to * share, share), share)] = d[local:]
    keys_t = kk[...].astype(f32).T.astype(bf16)
    lane_head = lax.broadcasted_iota(jnp.int32, (128, wide), 1) // dh
    dk[...] = jnp.zeros_like(dk)
    dv[...] = jnp.zeros_like(dv)

    def query_block(i, carry):
        at = pl.ds(pl.multiple_of(i * 128, 128), 128)
        zero = jnp.zeros((128, wide), bf16)

        def stacked(x):
            return jnp.concatenate([jnp.where(lane_head == h, x, zero) for h in range(hl)], 0)

        stack_d = stacked(dc[at])
        prob = p_ref[i]
        dp = dot_nt(vv[...], stack_d)
        parts = []
        for h in range(hl):
            lanes = slice(128 * h, 128 * h + 128)
            p = prob[:, lanes].astype(f32)
            g = dp[:, lanes]
            delta = jnp.sum(p * g, axis=0, keepdims=True)
            parts.append((p * (g - delta)).astype(bf16))
        ds = jnp.concatenate(parts, 1)
        dv[...] += dot_nn(prob, stack_d)
        dk[:words] += dot_nn(ds[:words], stacked(qw[at]))
        dk[words:] += dot_nn(ds[words:], stacked(qe[at]))
        for keys, ds_part, out in ((keys_t[:, :words], ds[:words], dqw), (keys_t[:, words:], ds[words:], dqe)):
            t = dot_nn(keys, ds_part)
            t = jnp.concatenate(
                [t[dh * h : dh * h + dh, 128 * h : 128 * h + 128] for h in range(hl)], 0
            )
            out[at] = t.T
        return carry

    lax.fori_loop(0, rows // 128, query_block, 0, unroll=True)
    dqkv[:, :wide] = (dqw[...] * factor).astype(bf16)
    dqkv[:, wide : 2 * wide] = (dqe[...] * factor).astype(bf16)
    dqkv[:, 2 * wide : 3 * wide] = dk[...].astype(bf16)
    dqkv[:, 3 * wide :] = dv[...].astype(bf16)


def proj_grads_body(dqkv, xw, xe, o0, o1, o2, *refs):
    outs, scr = refs[:-1], refs[-1]
    words = xw.shape[0]
    out_rows = o0.shape[0]
    half = dqkv.shape[1] // 2
    w = dot_tn(xw[...], dqkv[:words])
    e = dot_tn(xe[...], dqkv[words:])
    scr[:, :half] = w[:, :half].astype(bf16)
    scr[:, half : 2 * half] = (w[:, half:] + e[:, half:]).astype(bf16)
    scr[:, 2 * half : 3 * half] = e[:, :half].astype(bf16)
    o = o0[...].astype(f32) + o1[out_rows : 2 * out_rows].astype(f32) + o2[...].astype(f32)
    width = scr.shape[0]
    middle = width // 2
    tail = o[width : width + middle]
    scr[:, 3 * half : 3 * half + 128] = o[:width].astype(bf16)
    scr[:middle, 3 * half + 128 : 3 * half + 192] = tail[:, :64].astype(bf16)
    scr[middle:, 3 * half + 128 : 3 * half + 192] = tail[:, 64:].astype(bf16)
    vec = o[width + middle :]
    sums = jnp.concatenate([vec[8 * j : 8 * j + 8] for j in range(width // 128)], 1)
    sums = jnp.concatenate([sums, jnp.zeros((120, width), f32)], 0).T
    scr[:, 3 * half + 192 :] = sums[:, :64].astype(bf16)
    for j, out in enumerate(outs):
        to = ring_seat(j // 2, j % 2) if len(outs) > 1 else 0
        out[...] = scr[block(scr, to, out.shape[0])]


def total_of(*parts):
    total = parts[0][...].astype(f32)
    for part in parts[1:]:
        total = total + part[...].astype(f32)
    return total


def last_ff_body(a0, a1, a2, a3, w_out, c0, c1, c2, c3, scr):
    rows = c0.shape[0]
    width = c0.shape[1]
    t = total_of(a0, a1, a2, a3)
    w_out[...] = t[:, width:]
    scr[...] = t[:, :width]
    for k, c in enumerate((c0, c1, c2, c3)):
        c[...] = scr[block(scr, jnp.bitwise_xor(ff_rank(), k), rows)].astype(bf16)


def spread_ff_body(c0, c1, c2, c3, out, scr):
    part = out.shape[1] // (8 * RANKS)
    for k, c in enumerate((c0, c1, c2, c3)):
        scr[jnp.bitwise_xor(ff_rank(), k)] = c[...].astype(f32)
    for t in range(RANKS):
        for j in range(8):
            at = ff_column(t, j, part)
            out[:, at : at + part] = scr[t, :, part * j : part * j + part]


def last_body(a0, a1, a2, c0, c1, c2, c3, scr):
    rows = c0.shape[0]
    scr[...] = total_of(a0, a1, a2)
    for k, c in enumerate((c0, c1, c2, c3)):
        c[...] = scr[block(scr, partner(k), rows)].astype(bf16)


def finish_body(c0, c1, c2, c3, gq, gkv, go, gg, gb, scr):
    wide = go.shape[1] // RANKS
    for k, c in enumerate((c0, c1, c2, c3)):
        scr[partner(k)] = c[...].astype(f32)
    for t in range(RANKS):
        cut = slice(wide * t, wide * t + wide)
        for j, (out, i) in enumerate(((gq, 0), (gq, 1), (gkv, 0), (gkv, 1), (gq, 2), (gq, 3))):
            out[i, :, cut] = scr[t, :, wide * j : wide * j + wide]
        go[:, cut] = scr[t, :, 6 * wide : 7 * wide]
    at = 7 * wide + 64 - 128
    v = c0[:, at:].astype(f32).T
    gg[...] = v[64:66]
    gb[...] = v[66:68]


def input_body(dqkv, wq, du1, ye, own, across, core, part):
    b = lax.axis_index("blk")
    local, share = own.shape[0], ye.shape[0]
    words = RANKS * local
    half = dqkv.shape[1] // 2
    part[:words] = dot_nt(dqkv[:words], wq[:, : 2 * half])
    part[words:] = dot_nt(dqkv[words:, half:], wq[:, half : 2 * half]) + dot_nt(
        dqkv[words:, :half], wq[:, 2 * half :]
    )
    part[pl.ds(pl.multiple_of(words + b * share, share), share)] += du1[local:]
    own[...] = part[block(part, b, local)] + du1[:local]
    low = part[words:].astype(bf16)
    core[:local] = part[block(part, partner(3), local)].astype(bf16)
    core[local : 2 * local] = part[block(part, partner(1), local)].astype(bf16)
    core[2 * local : -share] = low
    core[-share:] = ye[...]
    across[:local] = part[block(part, partner(2), local)].astype(bf16)
    across[local:-share] = low
    across[-share:] = ye[...]


def input_pair_body(across, came, sent):
    share = sent.shape[0] - across.shape[0]
    local = came.shape[0] - across.shape[0]
    sent[:local] = (across[:local].astype(f32) + came[:local].astype(f32)).astype(bf16)
    pair = across[local:-share].astype(f32) + came[2 * local : -share].astype(f32)
    sent[local : -2 * share] = pair.astype(bf16)
    sent[-2 * share : -share] = across[-share:]
    sent[-share:] = came[-share:]


def input_sum_body(own, core, sent, came, gw, ge, ye):
    local = own.shape[0]
    share = ye.shape[0] // RANKS
    two = 2 * share
    gw[...] = own[...] + core[local : 2 * local].astype(f32) + came[:local].astype(f32)
    ge[...] = sent[local:-two].astype(f32) + came[local:-two].astype(f32)
    for k, rows in enumerate((sent[-two:-share], sent[-share:], came[-two:-share], came[-share:])):
        ye[block(ye, partner(k), share)] = rows


def swap(x, k):
    return lax.ppermute(x, "blk", [(i, i ^ k) for i in range(RANKS)])


def swapped(send):
    return [swap(send[k - 1], k) for k in (1, 2, 3)]


def spread(x):
    across = swap(x, 2)
    beside = swap(x, 1)
    return [beside, across, swap(across, 1)]


def plus(*parts):
    total = parts[0].astype(f32)
    for part in parts[1:]:
        total = total + part.astype(f32)
    return total.astype(bf16)


def over_x(x):
    return lax.ppermute(x, "seq", [(i, i ^ 1) for i in range(8)])


ring = (0, 1, 3, 2)


def swap_ff(x, k, direct):
    if not direct or k == 1:
        return swap(x, k)
    if k == 2:
        return over_x(x)
    return lax.ppermute(x, ("seq", "blk"), [(i, i ^ 5) for i in range(32)])


def along_ring(x, step=1):
    route = [(ring[i], ring[(i + step) % 4]) for i in range(4)]
    return lax.ppermute(x, "seq", [(2 * z + i, 2 * to + i) for z, to in route for i in (0, 1)])


def fence(*groups):
    return lax.optimization_barrier(groups)


def after(x, *before):
    return lax.optimization_barrier((x, before))[0]


def per_device(
    words,
    entities,
    segments,
    entity_counts,
    entity_anchor,
    query_weights,
    kv_weights,
    out_weight,
    ff_in,
    ff_out,
    norm_gain,
    norm_bias,
    grad_words,
    grad_entities,
):
    seqs = lax.axis_size("seq")
    direct = seqs == 8
    _, local, width = words.shape
    ents = entities.shape[1]
    share = ents // RANKS
    total = local * RANKS
    rows = total + ents
    mine = local + share
    wide = width // RANKS
    hl = HEADS // RANKS
    factor = (width // HEADS) ** (-0.5)
    part_rows = query_weights.shape[2]
    ff_part = ff_out.shape[1]
    ff = ff_part * seqs
    shards = 8 if direct else 1
    slab_cols = 7 * wide + 64
    xw_own, xe = words[0], entities[0]

    seg_ents = jnp.take_along_axis(segments, entity_anchor, axis=1)
    live = jnp.arange(ents, dtype=jnp.int32)[None, :] < entity_counts[:, None]
    segq = jnp.concatenate([segments, seg_ents], 1)
    segk = jnp.concatenate([segments, jnp.where(live, seg_ents, -1)], 1).T
    join_rows = call(join_rows_body, "join_rows", [((total, width), bf16)])

    if direct:
        pack = call(
            pack_body,
            "pack",
            [((part_rows, slab_cols), bf16)] * 4,
            [pltpu.VMEM((RANKS, part_rows, slab_cols), bf16)]
            + [pltpu.VMEM((n, part_rows, width), bf16) for n in (4, 2)]
            + [pltpu.VMEM((part_rows, width), bf16)]
            + [pltpu.VMEM((2, part_rows), bf16)] * 2
            + [pltpu.SemaphoreType.DMA((5,))],
            held=5,
            vmem=60,
        )
        pieces = pack(
            query_weights[0], kv_weights[0], out_weight[0], norm_gain[0], norm_bias[0]
        )
        pack_ff = call(
            pack_ff_body,
            "pack_ff",
            [((part_rows, ff), bf16)] * 4,
            [pltpu.VMEM((RANKS, part_rows, ff), bf16)],
        )
        ff_pieces = pack_ff(after(ff_in[0], pieces[0]))
        own = call(
            arrange_own_body, "arrange_own", [((RANKS * part_rows, slab_cols), f32)]
        )(pieces[0])
        pieces = [own[0], *swapped(pieces[1:])]

        arrange = call(
            arrange_body,
            "arrange",
            [((RANKS * part_rows, slab_cols), bf16)],
            [pltpu.VMEM((RANKS * part_rows, slab_cols), f32)],
        )
        arrange_ff = call(
            arrange_ff_body,
            "arrange_ff",
            [((RANKS * part_rows, ff + width), bf16)],
            [pltpu.VMEM((RANKS * part_rows, ff), f32)],
        )
        (slab,) = arrange(*pieces)
        xw_own, slab = fence(xw_own, slab)
        xb, xa = swap(xw_own, 1), swap(xw_own, 2)
        x0, g1 = over_x(slab), along_ring(slab)
        g1, x0, xb, ff_pieces = fence(g1, x0, xb, ff_pieces)
        x1, g2 = over_x(g1), along_ring(g1)
        came = [swap_ff(ff_pieces[k], k, direct) for k in (1, 2, 3)]
        (ff_slab,) = arrange_ff(ff_pieces[0], *came, ff_out[0])
        g2, x1, ff_slab, xa = fence(g2, x1, ff_slab, xa)
        x2, g3 = over_x(g2), along_ring(g2)
        y0, xc = swap(ff_slab, 2), swap(xa, 1)
        g3, x2, xc, segq, segk = fence(g3, x2, xc, segq, segk)
        f1, x3 = along_ring(after(ff_slab, g3)), over_x(g3)
        (xw,) = join_rows(xw_own, xb, xa, xc)
        x3, y0 = after((x3, y0), xw)
        f2 = along_ring(after(f1, y0, x3))
        slabs = [slab, x0, g1, x1, g2, x2, g3, x3]
    else:
        vec = jnp.concatenate([norm_gain[0], norm_bias[0]], 0).T
        vec = jnp.pad(vec, ((0, 0), (0, 60)))
        six = jnp.concatenate(
            [query_weights[0, :2], kv_weights[0], query_weights[0, 2:], out_weight], 0
        )
        six = six.reshape(7, part_rows, RANKS, wide).transpose(2, 1, 0, 3)
        six = six.reshape(RANKS, part_rows, 7 * wide)
        ff_cols = ff_in[0].reshape(part_rows, seqs, RANKS, ff_part).transpose(2, 0, 1, 3)
        ff_cols = ff_cols.reshape(RANKS, part_rows, ff)
        pack = jnp.concatenate(
            [six, jnp.broadcast_to(vec, (RANKS, part_rows, 64)), ff_cols], 2
        )
        pack = lax.all_to_all(pack, "blk", 0, 0, tiled=True).reshape(RANKS * part_rows, -1)
        pack = jnp.concatenate([pack, ff_out[0]], 1)
        pack = lax.all_gather(pack, "seq", axis=0, tiled=True)
        slabs, ff_slabs = [pack[:, :slab_cols]], [pack[:, slab_cols:]]
        (xw,) = join_rows(xw_own, *spread(xw_own))

    def place(slots, last, *args):
        outs = [((width, 6 * wide), bf16), ((width, 128), bf16), ((width, wide - 64), bf16)]
        if last:
            outs += [((width * 3 // 2, 128), bf16), ((8, width), f32)]
        body = place_last_body if last else place_body
        same = len(args) - len(slots)
        name = "place_last" if last else "place"
        return call(lambda *r: body(slots, *r), name, outs, same=same)(*args)

    if direct:
        ready = place((0, 1, 2, 3, 4), False, *slabs[:5])
        wq, _, _, wo_col, norms = place((5, 6, 7), True, *ready, *slabs[5:])
    else:
        blank = [jnp.zeros((width, n), bf16) for n in (6 * wide, 128, wide - 64)]
        wq, _, _, wo_col, norms = place((0,), True, *blank, slabs[0])
    wa, wb = swap(wo_col, 2), swap(wo_col, 1)
    attend = call(
        lambda *r: attend_body(wide, factor, *r),
        "attend",
        [((mine, wide), bf16)] * 4
        + [((rows, wide), bf16)] * 4
        + [((rows // 128, rows, 128 * hl), bf16)],
        [pltpu.VMEM((rows, wide), bf16)],
        us=7,
        vmem=16,
    )
    *ctx, qw, qe, kk, vv, prob = attend(xw, xe, wq, segq, segk)
    if direct:
        ctx = after(ctx, wb)
    ctx = [ctx[0]] + swapped(ctx[1:])
    wos = [wo_col, wb, wa, swap(after(wa, ctx), 1)]
    if direct:
        f3, y1 = along_ring(f2), swap(after(f1, ctx), 2)
    join_out = call(
        join_out_body,
        "join_out",
        [((width, width), bf16)],
        [pltpu.VMEM((RANKS, width * 3 // 2, 128), bf16)],
    )
    (wo,) = join_out(*(after(wos, f3) if direct else wos))
    mix = call(
        mix_body,
        "mix",
        [((mine, width), bf16), ((mine, width), f32), ((mine, 1), f32)],
    )
    hr, n1, i1 = mix(*ctx, wo, norms, xw_own, xe)

    def place_ff(slots, *args):
        outs = [((width, ff), bf16), ((ff, width), bf16)]
        same = len(args) - len(slots)
        return call(lambda *r: place_ff_body(slots, *r), "place_ff", outs, same=same)(*args)

    across, beside = swap_ff(hr, 2, direct), swap(hr, 1)
    if direct:
        fb, y2 = along_ring(after(y0, hr), -1), swap(after(f2, hr), 2)
        ready = place_ff((0, 1, 2, 3, 4, 6), ff_slab, y0, f1, y1, f2, f3)
        across = after(across, ready)
        ff_slabs = [ff_slab, y0, f1, y1, f2, y2, f3, fb]
    hs = [hr, beside, across, swap(across, 1)]
    if direct:
        w1, w2 = place_ff((5, 7), *ready, ff_slabs[5], ff_slabs[7])
    else:
        w1, w2 = place_ff((0,), ff_slabs[0])
    feed = call(
        feed_body,
        "feed",
        [((mine, width), f32), ((mine, width), bf16), ((2, mine, width), bf16)]
        + [((RANKS, mine, ff), bf16)] * 2,
        us=3,
        vmem=14,
    )
    own, across, core, g_all, gp_all = feed(*hs, w1, w2)
    core = swap(core, 1)
    fs = [own, core, swap_ff(plus(across, core[0]), 2, direct)]
    turn = call(
        turn_body,
        "turn",
        [((local, width), bf16), ((share, width), bf16), ((mine, width), bf16)]
        + [((mine, width), f32), ((8, width), f32)],
    )
    yw, ye, df, du2, sums = turn(*fs, n1, norms, grad_words[0], grad_entities[0])

    across, beside = swap_ff(df, 2, direct), swap(df, 1)
    ds = [df, beside, across, swap(across, 1)]
    half_dz = ((2, mine, ff), bf16)
    feed_back_near = call(
        feed_back_near_body,
        "feed_back_near",
        [((mine, width), f32), ((mine, width), bf16), half_dz],
        vmem=12,
    )
    feed_back_far = call(
        feed_back_far_body,
        "feed_back_far",
        [((mine, width), bf16), ((2, mine, width), bf16), half_dz],
        vmem=12,
    )
    own, beside, dz_near = feed_back_near(*ds[:2], gp_all, w1, w2)
    across, core, dz_far = feed_back_far(*ds[2:], gp_all, w1, w2, beside)
    core = swap(core, 1)
    feed_grads = call(
        feed_grads_body,
        "feed_grads",
        [((width // shards, ff + width), bf16)] * shards,
        [pltpu.VMEM((width, ff), bf16), pltpu.VMEM((ff, width), bf16)],
        us=3,
        vmem=16,
    )
    sent = plus(across, core[0])
    ff_chunks = feed_grads(*ds, *hs, g_all, dz_near, after(dz_far, sent))
    dhs = [own, core, swap_ff(sent, 2, direct)]
    if direct:
        ff0, ff1, ff2, ff3, ff4, ff5, ff6, ff7 = ff_chunks
        fy, fz = swap(ff5, 2), along_ring(ff2)
        part = plus(ff4, after(fy, fz))
        dhs[2] = after(dhs[2], ff_chunks)
        fl = along_ring(part, -1)

    packed = width * 3 // 2 + 8 * (width // 128)
    norm_one = call(
        norm_one_body,
        "norm_one",
        [((mine, wide), bf16)] * 3
        + [((2 * packed + mine * 3 // 2, 128), bf16), ((mine, width), f32)]
        + [((packed, 128), bf16)] * 2,
        [pltpu.VMEM((RANKS, packed, 128), bf16), pltpu.VMEM((width, width), bf16)],
        vmem=12,
    )
    d0, d2, d3, core, du1, wo_own, across = norm_one(
        *dhs, du2, n1, i1, norms, sums, wo, *ctx
    )
    dcs = [d0, swap(core, 1), swap(d2, 2), swap(d3, 3)]
    sent = plus(across, after(dcs[1], dcs[2], dcs[3])[:packed])
    outs = [wo_own, dcs[1], swap(sent, 2)]
    dcs = after(dcs, sent)
    attend_back = call(
        lambda *r: attend_back_body(factor, *r),
        "attend_back",
        [((rows, 4 * wide), bf16)],
        [pltpu.VMEM((rows, wide), bf16)] + [pltpu.VMEM((rows, wide), f32)] * 4,
        us=7,
        vmem=16,
    )
    (dqkv,) = attend_back(*dcs, qw, qe, kk, vv, prob)
    to_input = call(
        input_body,
        "to_input",
        [((local, width), f32)]
        + [((n * local + ents + share, width), bf16) for n in (1, 2)],
        [pltpu.VMEM((rows, width), f32)],
        us=2,
        vmem=12,
    )
    own, across, core = to_input(dqkv, wq, du1, ye)
    if direct:
        own = after(own, fl)
    core = swap(core, 1)
    proj_grads = call(
        proj_grads_body,
        "proj_grads",
        [((width // shards, slab_cols), bf16)] * shards,
        [pltpu.VMEM((width, slab_cols), bf16)],
        us=2,
        vmem=14,
    )
    chunks = proj_grads(after(dqkv, own), xw, xe, *outs)
    if direct:
        fl = along_ring(plus(ff6, after(fl, dqkv)), -1)
        fb, fc = along_ring(after(ff3, dqkv)), along_ring(after(ff7, chunks), -1)
        part = plus(chunks[2], after(over_x(chunks[3]), fl, fb))
        cx, cz = over_x(after(chunks[5], part)), along_ring(part, -1)
        core = after(core, part)
    (sent,) = call(input_pair_body, "input_pair", [((local + ents + 2 * share, width), bf16)])(across, core)
    came = swap(sent, 2)
    input_sum = call(
        input_sum_body,
        "input_sum",
        [((local, width), f32), ((ents, width), f32), ((ents, width), bf16)],
    )
    if not direct:
        gxw, gxe, ye = input_sum(own, core, sent, came)

    if direct:
        last_ff = call(
            last_ff_body,
            "last_ff",
            [((ff_part, width), f32)] + [((part_rows, ff), bf16)] * 4,
            [pltpu.VMEM((RANKS * part_rows, ff), f32)],
        )
        part = plus(chunks[4], cz, cx)
        cx, cz = over_x(after(chunks[7], part)), along_ring(part, -1)
        fy_last = swap(plus(ff1, fb, after(fc, part)), 2)
        part = plus(chunks[6], after(cz, came), cx)
        cx, cz = over_x(after(chunks[1], part)), along_ring(part, -1)
        grad_ff_out, *back = last_ff(ff0, fz, fl, after(fy_last, part))
        back = [back[0]] + [swap_ff(back[k], k, direct) for k in (1, 2, 3)]
        spread_ff = call(
            spread_ff_body,
            "spread_ff",
            [((part_rows, RANKS * ff), f32)],
            [pltpu.VMEM((RANKS, part_rows, ff), f32)],
        )
        (grad_ff_in,) = spread_ff(*back)
        gxw, gxe, ye = input_sum(own, core, sent, after(came, part))
        last = call(
            last_body,
            "last",
            [((part_rows, slab_cols), bf16)] * 4,
            [pltpu.VMEM((RANKS * part_rows, slab_cols), f32)],
        )
        back = last(chunks[0], after(cz, grad_ff_in, gxw), cx)
        back = [back[0]] + swapped(back[1:])
        finish = call(
            finish_body,
            "finish",
            [((4, part_rows, width), f32), ((2, part_rows, width), f32), ((part_rows, width), f32)]
            + [((2, part_rows), f32)] * 2,
            [pltpu.VMEM((RANKS, part_rows, slab_cols), f32)],
        )
        grad_query, grad_kv, grad_out, grad_gain, grad_bias = finish(*back)
    else:
        both = jnp.concatenate([chunks[0], ff_chunks[0]], 1)
        both = lax.psum_scatter(both, "seq", scatter_dimension=0, tiled=True)
        grad_ff_out = both[:, slab_cols + ff :].astype(f32)
        both = both[:, : slab_cols + ff].reshape(RANKS, part_rows, slab_cols + ff)
        both = lax.all_to_all(both, "blk", 0, 0, tiled=True).astype(f32)
        seven = both[:, :, : 7 * wide].reshape(RANKS, part_rows, 7, wide)
        seven = seven.transpose(2, 1, 0, 3).reshape(7, part_rows, width)
        grad_query = jnp.concatenate([seven[:2], seven[4:6]], 0)
        grad_kv, grad_out = seven[2:4], seven[6]
        vecs = both[0, :, 7 * wide : 7 * wide + 4].T
        grad_gain, grad_bias = vecs[:2], vecs[2:]
        grad_ff_in = both[:, :, slab_cols:].reshape(RANKS, part_rows, seqs, ff_part)
        grad_ff_in = grad_ff_in.transpose(1, 2, 0, 3).reshape(part_rows, RANKS * ff)
    return (
        yw[None],
        ye[None],
        gxw[None],
        gxe[None],
        grad_query[None],
        grad_kv[None],
        grad_out[None],
        grad_ff_in[None],
        grad_ff_out[None],
        grad_gain[None],
        grad_bias[None],
    )


def solution(mesh):
    placed = (
        P("seq", "blk", None),
        P("seq", None, None),
        P("seq", None),
        P("seq"),
        P("seq", None),
        P(None, None, ("seq", "blk"), None),
        P(None, None, ("seq", "blk"), None),
        P(None, ("seq", "blk"), None),
        P(None, ("seq", "blk"), None),
        P(None, ("seq", "blk"), None),
        P(None, None, ("seq", "blk")),
        P(None, None, ("seq", "blk")),
        P("seq", "blk", None),
        P("seq", None, None),
    )
    return jax.shard_map(
        per_device,
        mesh=mesh,
        in_specs=placed,
        out_specs=(
            P("seq", "blk", None),
            P("seq", None, None),
            P("seq", "blk", None),
            P("seq", None, None),
            P(None, None, ("seq", "blk"), None),
            P(None, None, ("seq", "blk"), None),
            P(None, ("seq", "blk"), None),
            P(None, ("seq", "blk"), None),
            P(None, ("seq", "blk"), None),
            P(None, None, ("seq", "blk")),
            P(None, None, ("seq", "blk")),
        ),
        check_vma=False,
    )
```

```python
import jax
import jax.numpy as jnp
from jax import lax
from jax.experimental import pallas as pl
from jax.experimental.pallas import tpu as pltpu
from jax.sharding import PartitionSpec as P

HEADS = 12
RANKS = 4
epsilon = 1e-05
masked_score = -1e30
bf16 = jnp.bfloat16
f32 = jnp.float32


def dot_nn(a, b):
    return jnp.dot(a, b, preferred_element_type=f32)


def dot_nt(a, b):
    return lax.dot_general(a, b, (((1,), (1,)), ((), ())), preferred_element_type=f32)


def dot_tn(a, b):
    return lax.dot_general(a, b, (((0,), (0,)), ((), ())), preferred_element_type=f32)


def block(ref, index, size):
    return pl.ds(pl.multiple_of(index * size, size), size)


def call(body, name, outs, scratch=(), vmem=10, us=1, held=0, same=0):
    def run(*args):
        return pl.pallas_call(
            body,
            name=name,
            out_shape=[jax.ShapeDtypeStruct(s, t) for s, t in outs],
            in_specs=[pl.BlockSpec(memory_space=pltpu.HBM)] * held
            + [pl.BlockSpec(memory_space=pltpu.VMEM)] * (len(args) - held),
            out_specs=[pl.BlockSpec(memory_space=pltpu.VMEM)] * len(outs),
            scratch_shapes=list(scratch),
            input_output_aliases={i: i for i in range(same)},
            compiler_params=pltpu.CompilerParams(vmem_limit_bytes=vmem << 20),
            cost_estimate=pl.CostEstimate(
                flops=int(us * 1e6), bytes_accessed=int(us * 1e3), transcendentals=0
            ),
        )(*args)

    return run


def partner(k):
    return jnp.bitwise_xor(lax.axis_index("blk"), k)


def ring_seat(k, e):
    s = lax.axis_index("seq")
    z = lax.div(s, 2)
    at = lax.rem(jnp.bitwise_xor(z, lax.div(z, 2)) + (k + 4), 4)
    return 2 * jnp.bitwise_xor(at, lax.div(at, 2)) + jnp.bitwise_xor(lax.rem(s, 2), e)


def ff_rank():
    return 2 * lax.rem(lax.axis_index("seq"), 2) + lax.rem(lax.axis_index("blk"), 2)


def ff_seat(k, e):
    z = lax.div(lax.axis_index("seq"), 2)
    at = lax.rem(jnp.bitwise_xor(z, lax.div(z, 2)) + (k + 4), 4)
    y = jnp.bitwise_xor(lax.div(lax.axis_index("blk"), 2), e)
    return 2 * jnp.bitwise_xor(at, lax.div(at, 2)) + y


def ff_column(rank, j, part):
    return (8 * (j // 2) + 4 * (rank // 2) + 2 * (j % 2) + rank % 2) * part


def ff_rows(seat, x, rows):
    at = 4 * lax.div(seat, 2) + 2 * x + lax.rem(seat, 2)
    return pl.ds(pl.multiple_of(2 * rows * at, 16), 2 * rows)


def norm_stats(u):
    center = u - jnp.mean(u, axis=-1, keepdims=True)
    inverse = lax.rsqrt(jnp.mean(center * center, axis=-1, keepdims=True) + epsilon)
    return center * inverse, inverse


def norm_pull(scaled, normed, inverse):
    return inverse * (
        scaled
        - jnp.mean(scaled, axis=-1, keepdims=True)
        - normed * jnp.mean(scaled * normed, axis=-1, keepdims=True)
    )


def fetch(refs, sems):
    half = len(refs) // 2
    copies = [
        pltpu.make_async_copy(source, target, sems.at[i])
        for i, (source, target) in enumerate(zip(refs[:half], refs[half:]))
    ]
    for copy in copies:
        copy.start()
    for copy in copies:
        copy.wait()


def pack_body(*refs):
    sources, outs, scr, here, sems = refs[:5], refs[5:9], refs[9], refs[10:15], refs[15]
    fetch((*sources, *here), sems)
    q, kv, wo, gain, bias = here
    rows, wide = q.shape[1], q.shape[2] // RANKS
    eye = lax.broadcasted_iota(jnp.int32, (rows, rows), 0) == lax.broadcasted_iota(
        jnp.int32, (rows, rows), 1
    )
    lane = lax.broadcasted_iota(jnp.int32, (rows, 64), 1)
    vec = jnp.zeros((rows, 64), f32)
    for j, row in enumerate((gain[0:1], gain[1:2], bias[0:1], bias[1:2])):
        column = jnp.sum(jnp.where(eye, row.astype(f32), 0.0), axis=1, keepdims=True)
        vec = jnp.where(lane == j, column, vec)
    for t in range(RANKS):
        cut = slice(wide * t, wide * t + wide)
        for j, piece in enumerate((q[0], q[1], kv[0], kv[1], q[2], q[3], wo[...])):
            scr[t, :, wide * j : wide * j + wide] = piece[:, cut]
        scr[t, :, 7 * wide :] = vec.astype(bf16)
    for k in range(RANKS):
        outs[k][...] = scr[partner(k)]


def pack_ff_body(ff, *refs):
    outs, scr = refs[:RANKS], refs[RANKS]
    part = ff.shape[1] // (8 * RANKS)
    for t in range(RANKS):
        for j in range(8):
            at = ff_column(t, j, part)
            scr[t, :, part * j : part * j + part] = ff[:, at : at + part]
    for k in range(RANKS):
        outs[k][...] = scr[jnp.bitwise_xor(ff_rank(), k)]


def arrange_own_body(p0, out):
    out[block(out, partner(0), p0.shape[0])] = p0[...].astype(f32)


def arrange_body(own, p1, p2, p3, slab, scr):
    rows = p1.shape[0]
    scr[...] = own[...]
    for k, p in ((1, p1), (2, p2), (3, p3)):
        scr[block(scr, partner(k), rows)] = p[...].astype(f32)
    slab[...] = scr[...].astype(bf16)


def arrange_ff_body(p0, p1, p2, p3, ff_out, slab, scr):
    rows, cols = p0.shape
    for k, p in enumerate((p0, p1, p2, p3)):
        scr[block(scr, jnp.bitwise_xor(ff_rank(), k), rows)] = p[...].astype(f32)
    slab[:, :cols] = scr[...].astype(bf16)
    slab[:, cols:] = ff_out[...]


def place_body(slots, *refs):
    shards, (wq, wo_first, rest) = refs[-3 - len(slots) : -3], refs[-3:]
    rows, first = shards[0].shape[0], wq.shape[1]
    for j, shard in zip(slots, shards):
        at = block(shard, ring_seat(-(j // 2), j % 2) if rows < wq.shape[0] else 0, rows)
        wq[at] = shard[:, :first]
        wo_first[at] = shard[:, first : first + 128]
        rest[at] = shard[:, first + 128 :]


def place_last_body(slots, *refs):
    wide = refs[0].shape[1] // 6
    ins, (wq, wo_first, rest, wo_col, norms) = refs[:-5], refs[-5:]
    place_body(slots, *ins, wq, wo_first, rest)
    width = wq.shape[0]
    half = width // 2
    tail = rest[...]
    wo_col[:width] = wo_first[...]
    wo_col[width:] = jnp.concatenate([tail[:half, : wide - 128], tail[half:, : wide - 128]], 1)
    norms[...] = tail.astype(f32).T[wide - 128 : wide - 120]


def place_ff_body(slots, *refs):
    shards, w1, w2 = refs[-2 - len(slots) : -2], refs[-2], refs[-1]
    rows, cut = shards[0].shape[0], w1.shape[1]
    if rows == w1.shape[0]:
        w1[...] = shards[0][:, :cut]
        w2[...] = shards[0][:, cut:]
        return
    for j, shard in zip(slots, shards):
        seat = ff_seat(-(j // 2), j % 2)
        for x in (0, 1):
            w1[ff_rows(seat, x, rows // 4)] = shard[rows // 2 * x : rows // 2 * (x + 1), :cut]
        w2[block(shard, seat, rows)] = shard[:, cut:]


def join_out_body(w0, w1, w2, w3, wo, scr):
    wide = wo.shape[1] // RANKS
    half = wo.shape[0] // 2
    for k, w in enumerate((w0, w1, w2, w3)):
        scr[partner(k)] = w[...]
    for t in range(RANKS):
        wo[:, wide * t : wide * t + 128] = scr[t, : 2 * half]
        tail = scr[t, 2 * half :]
        wo[:half, wide * t + 128 : wide * t + wide] = tail[:, : wide - 128]
        wo[half:, wide * t + 128 : wide * t + wide] = tail[:, wide - 128 :]


def join_rows_body(x0, x1, x2, x3, xw):
    local = x0.shape[0]
    for k, x in enumerate((x0, x1, x2, x3)):
        xw[block(xw, partner(k), local)] = x[...]


def attend_body(wide, factor, xw, xe, wq, segq, segk, c0, c1, c2, c3, qw, qe, kk, vv, p_ref, c_scr):
    words, ents = xw.shape[0], xe.shape[0]
    local = words // RANKS
    share = ents // RANKS
    hl = HEADS // RANKS
    dh = wide // hl
    rows = words + ents
    w = dot_nn(xw[...], wq[:, : 4 * wide])
    e_kv = dot_nn(xe[...], wq[:, 2 * wide : 4 * wide])
    e_q = dot_nn(xe[...], wq[:, 4 * wide :])
    qw[:words] = (w[:, :wide] * factor).astype(bf16)
    qe[:words] = (w[:, wide : 2 * wide] * factor).astype(bf16)
    kk[:words] = w[:, 2 * wide : 3 * wide].astype(bf16)
    vv[:words] = w[:, 3 * wide :].astype(bf16)
    qw[words:] = (e_q[:, :wide] * factor).astype(bf16)
    qe[words:] = (e_q[:, wide:] * factor).astype(bf16)
    kk[words:] = e_kv[:, :wide].astype(bf16)
    vv[words:] = e_kv[:, wide:].astype(bf16)
    values_t = vv[...].astype(f32).T.astype(bf16)
    lane_head = lax.broadcasted_iota(jnp.int32, (128, wide), 1) // dh
    segcol = segk[...]

    def query_block(i, carry):
        at = pl.ds(pl.multiple_of(i * 128, 128), 128)
        q_word, q_ent = qw[at], qe[at]
        zero = jnp.zeros_like(q_word)
        stack_w = jnp.concatenate([jnp.where(lane_head == h, q_word, zero) for h in range(hl)], 0)
        stack_e = jnp.concatenate([jnp.where(lane_head == h, q_ent, zero) for h in range(hl)], 0)
        s_w = dot_nt(kk[:words], stack_w)
        s_e = dot_nt(kk[words:], stack_e)
        allowed = segcol == segq[0:1, at]
        probs = []
        for h in range(hl):
            lanes = slice(128 * h, 128 * h + 128)
            s = jnp.concatenate([s_w[:, lanes], s_e[:, lanes]], 0)
            s = jnp.where(allowed, s, masked_score)
            top = jnp.max(s, axis=0, keepdims=True)
            e = jnp.exp(s - top)
            probs.append((e * (1.0 / jnp.sum(e, axis=0, keepdims=True))).astype(bf16))
        prob = jnp.concatenate(probs, 1)
        p_ref[i] = prob
        ctx = dot_nn(values_t, prob)
        ctx = jnp.concatenate(
            [ctx[dh * h : dh * h + dh, 128 * h : 128 * h + 128] for h in range(hl)], 0
        )
        c_scr[at] = ctx.T.astype(bf16)
        return carry

    lax.fori_loop(0, rows // 128, query_block, 0, unroll=True)
    b = lax.axis_index("blk")
    for k, out in enumerate((c0, c1, c2, c3)):
        to = jnp.bitwise_xor(b, k)
        out[:local] = c_scr[block(c_scr, to, local)]
        out[local:] = c_scr[pl.ds(pl.multiple_of(words + to * share, share), share)]


def mix_body(c0, c1, c2, c3, wo, norms, xw, xe, hr, n1, i1):
    b = lax.axis_index("blk")
    wide = c0.shape[1]
    share = hr.shape[0] - xw.shape[0]
    u = jnp.concatenate([xw[...].astype(f32), xe[block(xe, b, share)].astype(f32)], 0)
    for k, c in enumerate((c0, c1, c2, c3)):
        u = u + dot_nn(c[...], wo[block(wo, partner(k), wide)])
    normed, inverse = norm_stats(u)
    n1[...] = normed
    i1[...] = inverse
    hr[...] = (normed * norms[0:1] + norms[2:3]).astype(bf16)


def feed_body(h0, h1, h2, h3, w1, w2, own, across, core, g_all, gp_all):
    outs = (own, core.at[1], across, core.at[0])
    for k, h in enumerate((h0, h1, h2, h3)):
        z = dot_nn(h[...], w1[...])
        cdf = 0.5 * (1.0 + lax.erf(z * 0.7071067811865476))
        g = (z * cdf).astype(bf16)
        g_all[k] = g
        gp_all[k] = (cdf + z * (0.3989422804014327 * jnp.exp(-0.5 * z * z))).astype(bf16)
        outs[k][...] = dot_nn(g, w2[...]).astype(outs[k].dtype)


def turn_body(f0, f1, f2, n1, norms, gw, ge, yw, ye, df, du2, sums):
    b = lax.axis_index("blk")
    local = gw.shape[0]
    rows = n1.shape[0]
    share = rows - local
    n = norms[...]
    u = n1[...] * n[0:1] + n[2:3]
    u = u + (f0[...] + f1[1].astype(f32) + f2[...].astype(f32))
    normed, inverse = norm_stats(u)
    y = (normed * n[1:2] + n[3:4]).astype(bf16)
    yw[...] = y[:local]
    ye[...] = y[local:]
    dy = jnp.concatenate([gw[...].astype(f32), ge[block(ge, b, share)].astype(f32)], 0)
    sums[...] = jnp.concatenate(
        [jnp.sum(dy * normed, axis=0, keepdims=True), jnp.sum(dy, axis=0, keepdims=True)]
        + [jnp.zeros((6, dy.shape[1]), f32)],
        0,
    )
    d = norm_pull(dy * n[1:2], normed, inverse)
    du2[...] = d
    df[...] = d.astype(bf16)


def feed_back_near_body(d0, d1, gp_all, w1, w2, own, beside, dz):
    for k, (d, out) in enumerate(((d0, own), (d1, beside))):
        z = (dot_nt(d[...], w2[...]) * gp_all[k].astype(f32)).astype(bf16)
        dz[k] = z
        out[...] = dot_nt(z, w1[...]).astype(out.dtype)


def feed_back_far_body(d2, d3, gp_all, w1, w2, beside, across, core, dz):
    core[1] = beside[...]
    for k, (d, out) in enumerate(((d2, across), (d3, core.at[0]))):
        z = (dot_nt(d[...], w2[...]) * gp_all[2 + k].astype(f32)).astype(bf16)
        dz[k] = z
        out[...] = dot_nt(z, w1[...]).astype(out.dtype)


def feed_grads_body(d0, d1, d2, d3, h0, h1, h2, h3, g_all, dz_near, dz_far, *refs):
    outs, g_in, g_out = refs[:-2], refs[-2], refs[-1]
    d = jnp.concatenate([x[...] for x in (d0, d1, d2, d3)], 0)
    h = jnp.concatenate([x[...] for x in (h0, h1, h2, h3)], 0)
    g = jnp.concatenate([g_all[k] for k in range(RANKS)], 0)
    z = jnp.concatenate([dz_near[0], dz_near[1], dz_far[0], dz_far[1]], 0)
    g_in[...] = dot_tn(h, z).astype(bf16)
    g_out[...] = dot_tn(g, d).astype(bf16)
    cut = g_in.shape[1]
    if len(outs) == 1:
        outs[0][:, :cut] = g_in[...]
        outs[0][:, cut:] = g_out[...]
        return
    for j, out in enumerate(outs):
        seat = ff_seat(j // 2, j % 2)
        rows = out.shape[0]
        for x in (0, 1):
            out[rows // 2 * x : rows // 2 * (x + 1), :cut] = g_in[ff_rows(seat, x, rows // 4)]
        out[:, cut:] = g_out[block(out, seat, rows)]


def norm_one_body(h0, h1, h2, du2, n1, i1, norms, two, wo, c0, c1, c2, c3, *refs):
    d0, d2, d3, core, du1, w_own, w_across, scr, whole = refs
    wide = d0.shape[1]
    dh = du2[...] + (h0[...] + h1[1].astype(f32) + h2[...].astype(f32))
    width = dh.shape[1]
    normed = n1[...]
    d = norm_pull(dh * norms[0:1], normed, i1[...])
    du1[...] = d
    low = d.astype(bf16)
    dc = [dot_nt(low, wo[block(wo, partner(k), wide)]).astype(bf16) for k in range(RANKS)]
    d0[...] = dc[0]
    base = 2 * scr.shape[1]
    mine = dc[1].shape[0]
    core[base : base + mine] = dc[1][:, :128]
    core[base + mine :] = jnp.concatenate([dc[1][: mine // 2, 128:], dc[1][mine // 2 :, 128:]], 1)
    d2[...] = dc[2]
    d3[...] = dc[3]
    sums = jnp.concatenate(
        [jnp.sum(dh * normed, axis=0, keepdims=True), two[0:1]]
        + [jnp.sum(dh, axis=0, keepdims=True), two[1:2], jnp.zeros((124, width), f32)],
        0,
    )
    half = width // 2
    for k, c in enumerate((c0, c1, c2, c3)):
        whole[block(whole, partner(k), wide)] = dot_tn(c[...], low).astype(bf16)
    for t in range(RANKS):
        at = wide * t
        scr[t, :width] = whole[:, at : at + 128]
        rest = slice(at + 128, at + wide)
        scr[t, width : width + half] = jnp.concatenate([whole[:half, rest], whole[half:, rest]], 1)

    low_sums = sums[:8].astype(bf16)
    for t in range(RANKS):
        for j in range(width // 128):
            at = width + half + 8 * j
            scr[t, at : at + 8] = low_sums[:, 128 * j : 128 * j + 128]
    rows = scr.shape[1]
    w_own[...] = scr[partner(0)]
    core[:rows] = scr[partner(3)]
    core[rows : 2 * rows] = scr[partner(1)]
    w_across[...] = scr[partner(2)]


def attend_back_body(factor, d0, core, d2, d3, qw, qe, kk, vv, p_ref, dqkv, dc, dqw, dqe, dk, dv):
    b = lax.axis_index("blk")
    rows, wide = qw.shape
    local = rows * 4 // 5 // RANKS
    words = local * RANKS
    share = (rows - words) // RANKS
    hl = HEADS // RANKS
    dh = wide // hl
    mine = d0.shape[0]
    base = core.shape[0] - mine * 3 // 2
    tail = core[base + mine :]
    d1 = jnp.concatenate(
        [core[base : base + mine], jnp.concatenate([tail[:, :64], tail[:, 64:]], 0)], 1
    )
    for k, d in enumerate((d0[...], d1, d2[...], d3[...])):
        to = jnp.bitwise_xor(b, k)
        dc[block(dc, to, local)] = d[:local]
        dc[pl.ds(pl.multiple_of(words + to * share, share), share)] = d[local:]
    keys_t = kk[...].astype(f32).T.astype(bf16)
    lane_head = lax.broadcasted_iota(jnp.int32, (128, wide), 1) // dh
    dk[...] = jnp.zeros_like(dk)
    dv[...] = jnp.zeros_like(dv)

    def query_block(i, carry):
        at = pl.ds(pl.multiple_of(i * 128, 128), 128)
        zero = jnp.zeros((128, wide), bf16)

        def stacked(x):
            return jnp.concatenate([jnp.where(lane_head == h, x, zero) for h in range(hl)], 0)

        stack_d = stacked(dc[at])
        prob = p_ref[i]
        dp = dot_nt(vv[...], stack_d)
        parts = []
        for h in range(hl):
            lanes = slice(128 * h, 128 * h + 128)
            p = prob[:, lanes].astype(f32)
            g = dp[:, lanes]
            delta = jnp.sum(p * g, axis=0, keepdims=True)
            parts.append((p * (g - delta)).astype(bf16))
        ds = jnp.concatenate(parts, 1)
        dv[...] += dot_nn(prob, stack_d)
        dk[:words] += dot_nn(ds[:words], stacked(qw[at]))
        dk[words:] += dot_nn(ds[words:], stacked(qe[at]))
        for keys, ds_part, out in ((keys_t[:, :words], ds[:words], dqw), (keys_t[:, words:], ds[words:], dqe)):
            t = dot_nn(keys, ds_part)
            t = jnp.concatenate(
                [t[dh * h : dh * h + dh, 128 * h : 128 * h + 128] for h in range(hl)], 0
            )
            out[at] = t.T
        return carry

    lax.fori_loop(0, rows // 128, query_block, 0, unroll=True)
    dqkv[:, :wide] = (dqw[...] * factor).astype(bf16)
    dqkv[:, wide : 2 * wide] = (dqe[...] * factor).astype(bf16)
    dqkv[:, 2 * wide : 3 * wide] = dk[...].astype(bf16)
    dqkv[:, 3 * wide :] = dv[...].astype(bf16)


def proj_grads_body(dqkv, xw, xe, o0, o1, o2, *refs):
    outs, scr = refs[:-1], refs[-1]
    words = xw.shape[0]
    out_rows = o0.shape[0]
    half = dqkv.shape[1] // 2
    w = dot_tn(xw[...], dqkv[:words])
    e = dot_tn(xe[...], dqkv[words:])
    scr[:, :half] = w[:, :half].astype(bf16)
    scr[:, half : 2 * half] = (w[:, half:] + e[:, half:]).astype(bf16)
    scr[:, 2 * half : 3 * half] = e[:, :half].astype(bf16)
    o = o0[...].astype(f32) + o1[out_rows : 2 * out_rows].astype(f32) + o2[...].astype(f32)
    width = scr.shape[0]
    middle = width // 2
    tail = o[width : width + middle]
    scr[:, 3 * half : 3 * half + 128] = o[:width].astype(bf16)
    scr[:middle, 3 * half + 128 : 3 * half + 192] = tail[:, :64].astype(bf16)
    scr[middle:, 3 * half + 128 : 3 * half + 192] = tail[:, 64:].astype(bf16)
    vec = o[width + middle :]
    sums = jnp.concatenate([vec[8 * j : 8 * j + 8] for j in range(width // 128)], 1)
    sums = jnp.concatenate([sums, jnp.zeros((120, width), f32)], 0).T
    scr[:, 3 * half + 192 :] = sums[:, :64].astype(bf16)
    for j, out in enumerate(outs):
        to = ring_seat(j // 2, j % 2) if len(outs) > 1 else 0
        out[...] = scr[block(scr, to, out.shape[0])]


def total_of(*parts):
    total = parts[0][...].astype(f32)
    for part in parts[1:]:
        total = total + part[...].astype(f32)
    return total


def last_ff_body(a0, a1, a2, a3, w_out, c0, c1, c2, c3, scr):
    rows = c0.shape[0]
    width = c0.shape[1]
    t = total_of(a0, a1, a2, a3)
    w_out[...] = t[:, width:]
    scr[...] = t[:, :width]
    for k, c in enumerate((c0, c1, c2, c3)):
        c[...] = scr[block(scr, jnp.bitwise_xor(ff_rank(), k), rows)].astype(bf16)


def spread_ff_body(c0, c1, c2, c3, out, scr):
    part = out.shape[1] // (8 * RANKS)
    for k, c in enumerate((c0, c1, c2, c3)):
        scr[jnp.bitwise_xor(ff_rank(), k)] = c[...].astype(f32)
    for t in range(RANKS):
        for j in range(8):
            at = ff_column(t, j, part)
            out[:, at : at + part] = scr[t, :, part * j : part * j + part]


def last_body(a0, a1, a2, c0, c1, c2, c3, scr):
    rows = c0.shape[0]
    scr[...] = total_of(a0, a1, a2)
    for k, c in enumerate((c0, c1, c2, c3)):
        c[...] = scr[block(scr, partner(k), rows)].astype(bf16)


def finish_body(c0, c1, c2, c3, gq, gkv, go, gg, gb, scr):
    wide = go.shape[1] // RANKS
    for k, c in enumerate((c0, c1, c2, c3)):
        scr[partner(k)] = c[...].astype(f32)
    for t in range(RANKS):
        cut = slice(wide * t, wide * t + wide)
        for j, (out, i) in enumerate(((gq, 0), (gq, 1), (gkv, 0), (gkv, 1), (gq, 2), (gq, 3))):
            out[i, :, cut] = scr[t, :, wide * j : wide * j + wide]
        go[:, cut] = scr[t, :, 6 * wide : 7 * wide]
    at = 7 * wide + 64 - 128
    v = c0[:, at:].astype(f32).T
    gg[...] = v[64:66]
    gb[...] = v[66:68]


def input_body(dqkv, wq, du1, ye, own, across, core, part):
    b = lax.axis_index("blk")
    local, share = own.shape[0], ye.shape[0]
    words = RANKS * local
    half = dqkv.shape[1] // 2
    part[:words] = dot_nt(dqkv[:words], wq[:, : 2 * half])
    part[words:] = dot_nt(dqkv[words:, half:], wq[:, half : 2 * half]) + dot_nt(
        dqkv[words:, :half], wq[:, 2 * half :]
    )
    part[pl.ds(pl.multiple_of(words + b * share, share), share)] += du1[local:]
    own[...] = part[block(part, b, local)] + du1[:local]
    low = part[words:].astype(bf16)
    core[:local] = part[block(part, partner(3), local)].astype(bf16)
    core[local : 2 * local] = part[block(part, partner(1), local)].astype(bf16)
    core[2 * local : -share] = low
    core[-share:] = ye[...]
    across[:local] = part[block(part, partner(2), local)].astype(bf16)
    across[local:-share] = low
    across[-share:] = ye[...]


def input_pair_body(across, came, sent):
    share = sent.shape[0] - across.shape[0]
    local = came.shape[0] - across.shape[0]
    sent[:local] = (across[:local].astype(f32) + came[:local].astype(f32)).astype(bf16)
    pair = across[local:-share].astype(f32) + came[2 * local : -share].astype(f32)
    sent[local : -2 * share] = pair.astype(bf16)
    sent[-2 * share : -share] = across[-share:]
    sent[-share:] = came[-share:]


def input_sum_body(own, core, sent, came, gw, ge, ye):
    local = own.shape[0]
    share = ye.shape[0] // RANKS
    two = 2 * share
    gw[...] = own[...] + core[local : 2 * local].astype(f32) + came[:local].astype(f32)
    ge[...] = sent[local:-two].astype(f32) + came[local:-two].astype(f32)
    for k, rows in enumerate((sent[-two:-share], sent[-share:], came[-two:-share], came[-share:])):
        ye[block(ye, partner(k), share)] = rows


def swap(x, k):
    return lax.ppermute(x, "blk", [(i, i ^ k) for i in range(RANKS)])


def swapped(send):
    return [swap(send[k - 1], k) for k in (1, 2, 3)]


def spread(x):
    across = swap(x, 2)
    beside = swap(x, 1)
    return [beside, across, swap(across, 1)]


def plus(*parts):
    total = parts[0].astype(f32)
    for part in parts[1:]:
        total = total + part.astype(f32)
    return total.astype(bf16)


def over_x(x):
    return lax.ppermute(x, "seq", [(i, i ^ 1) for i in range(8)])


ring = (0, 1, 3, 2)


def swap_ff(x, k, direct):
    if not direct or k == 1:
        return swap(x, k)
    if k == 2:
        return over_x(x)
    return lax.ppermute(x, ("seq", "blk"), [(i, i ^ 5) for i in range(32)])


def along_ring(x, step=1):
    route = [(ring[i], ring[(i + step) % 4]) for i in range(4)]
    return lax.ppermute(x, "seq", [(2 * z + i, 2 * to + i) for z, to in route for i in (0, 1)])


def fence(*groups):
    return lax.optimization_barrier(groups)


def after(x, *before):
    return lax.optimization_barrier((x, before))[0]


def per_device(
    words,
    entities,
    segments,
    entity_counts,
    entity_anchor,
    query_weights,
    kv_weights,
    out_weight,
    ff_in,
    ff_out,
    norm_gain,
    norm_bias,
    grad_words,
    grad_entities,
):
    seqs = lax.axis_size("seq")
    direct = seqs == 8
    _, local, width = words.shape
    ents = entities.shape[1]
    share = ents // RANKS
    total = local * RANKS
    rows = total + ents
    mine = local + share
    wide = width // RANKS
    hl = HEADS // RANKS
    factor = (width // HEADS) ** (-0.5)
    part_rows = query_weights.shape[2]
    ff_part = ff_out.shape[1]
    ff = ff_part * seqs
    shards = 8 if direct else 1
    slab_cols = 7 * wide + 64
    xw_own, xe = words[0], entities[0]

    seg_ents = jnp.take_along_axis(segments, entity_anchor, axis=1)
    live = jnp.arange(ents, dtype=jnp.int32)[None, :] < entity_counts[:, None]
    segq = jnp.concatenate([segments, seg_ents], 1)
    segk = jnp.concatenate([segments, jnp.where(live, seg_ents, -1)], 1).T
    join_rows = call(join_rows_body, "join_rows", [((total, width), bf16)])

    if direct:
        pack = call(
            pack_body,
            "pack",
            [((part_rows, slab_cols), bf16)] * 4,
            [pltpu.VMEM((RANKS, part_rows, slab_cols), bf16)]
            + [pltpu.VMEM((n, part_rows, width), bf16) for n in (4, 2)]
            + [pltpu.VMEM((part_rows, width), bf16)]
            + [pltpu.VMEM((2, part_rows), bf16)] * 2
            + [pltpu.SemaphoreType.DMA((5,))],
            held=5,
            vmem=60,
        )
        pieces = pack(
            query_weights[0], kv_weights[0], out_weight[0], norm_gain[0], norm_bias[0]
        )
        pack_ff = call(
            pack_ff_body,
            "pack_ff",
            [((part_rows, ff), bf16)] * 4,
            [pltpu.VMEM((RANKS, part_rows, ff), bf16)],
        )
        ff_pieces = pack_ff(after(ff_in[0], pieces[0]))
        own = call(
            arrange_own_body, "arrange_own", [((RANKS * part_rows, slab_cols), f32)]
        )(pieces[0])
        pieces = [own[0], *swapped(pieces[1:])]

        arrange = call(
            arrange_body,
            "arrange",
            [((RANKS * part_rows, slab_cols), bf16)],
            [pltpu.VMEM((RANKS * part_rows, slab_cols), f32)],
        )
        arrange_ff = call(
            arrange_ff_body,
            "arrange_ff",
            [((RANKS * part_rows, ff + width), bf16)],
            [pltpu.VMEM((RANKS * part_rows, ff), f32)],
        )
        (slab,) = arrange(*pieces)
        xw_own, slab = fence(xw_own, slab)
        xb, xa = swap(xw_own, 1), swap(xw_own, 2)
        x0, g1 = over_x(slab), along_ring(slab)
        g1, x0, xb, ff_pieces = fence(g1, x0, xb, ff_pieces)
        x1, g2 = over_x(g1), along_ring(g1)
        came = [swap_ff(ff_pieces[k], k, direct) for k in (1, 2, 3)]
        (ff_slab,) = arrange_ff(ff_pieces[0], *came, ff_out[0])
        g2, x1, ff_slab, xa = fence(g2, x1, ff_slab, xa)
        x2, g3 = over_x(g2), along_ring(g2)
        y0, xc = swap(ff_slab, 2), swap(xa, 1)
        g3, x2, xc, segq, segk = fence(g3, x2, xc, segq, segk)
        f1, x3 = along_ring(after(ff_slab, g3)), over_x(g3)
        (xw,) = join_rows(xw_own, xb, xa, xc)
        x3, y0 = after((x3, y0), xw)
        f2 = along_ring(after(f1, y0, x3))
        slabs = [slab, x0, g1, x1, g2, x2, g3, x3]
    else:
        vec = jnp.concatenate([norm_gain[0], norm_bias[0]], 0).T
        vec = jnp.pad(vec, ((0, 0), (0, 60)))
        six = jnp.concatenate(
            [query_weights[0, :2], kv_weights[0], query_weights[0, 2:], out_weight], 0
        )
        six = six.reshape(7, part_rows, RANKS, wide).transpose(2, 1, 0, 3)
        six = six.reshape(RANKS, part_rows, 7 * wide)
        ff_cols = ff_in[0].reshape(part_rows, seqs, RANKS, ff_part).transpose(2, 0, 1, 3)
        ff_cols = ff_cols.reshape(RANKS, part_rows, ff)
        pack = jnp.concatenate(
            [six, jnp.broadcast_to(vec, (RANKS, part_rows, 64)), ff_cols], 2
        )
        pack = lax.all_to_all(pack, "blk", 0, 0, tiled=True).reshape(RANKS * part_rows, -1)
        pack = jnp.concatenate([pack, ff_out[0]], 1)
        pack = lax.all_gather(pack, "seq", axis=0, tiled=True)
        slabs, ff_slabs = [pack[:, :slab_cols]], [pack[:, slab_cols:]]
        (xw,) = join_rows(xw_own, *spread(xw_own))

    def place(slots, last, *args):
        outs = [((width, 6 * wide), bf16), ((width, 128), bf16), ((width, wide - 64), bf16)]
        if last:
            outs += [((width * 3 // 2, 128), bf16), ((8, width), f32)]
        body = place_last_body if last else place_body
        same = len(args) - len(slots)
        name = "place_last" if last else "place"
        return call(lambda *r: body(slots, *r), name, outs, same=same)(*args)

    if direct:
        ready = place((0, 1, 2, 3, 4), False, *slabs[:5])
        wq, _, _, wo_col, norms = place((5, 6, 7), True, *ready, *slabs[5:])
    else:
        blank = [jnp.zeros((width, n), bf16) for n in (6 * wide, 128, wide - 64)]
        wq, _, _, wo_col, norms = place((0,), True, *blank, slabs[0])
    wa, wb = swap(wo_col, 2), swap(wo_col, 1)
    attend = call(
        lambda *r: attend_body(wide, factor, *r),
        "attend",
        [((mine, wide), bf16)] * 4
        + [((rows, wide), bf16)] * 4
        + [((rows // 128, rows, 128 * hl), bf16)],
        [pltpu.VMEM((rows, wide), bf16)],
        us=7,
        vmem=16,
    )
    *ctx, qw, qe, kk, vv, prob = attend(xw, xe, wq, segq, segk)
    if direct:
        ctx = after(ctx, wb)
    ctx = [ctx[0]] + swapped(ctx[1:])
    wos = [wo_col, wb, wa, swap(after(wa, ctx), 1)]
    if direct:
        f3, y1 = along_ring(f2), swap(after(f1, ctx), 2)
    join_out = call(
        join_out_body,
        "join_out",
        [((width, width), bf16)],
        [pltpu.VMEM((RANKS, width * 3 // 2, 128), bf16)],
    )
    (wo,) = join_out(*(after(wos, f3) if direct else wos))
    mix = call(
        mix_body,
        "mix",
        [((mine, width), bf16), ((mine, width), f32), ((mine, 1), f32)],
    )
    hr, n1, i1 = mix(*ctx, wo, norms, xw_own, xe)

    def place_ff(slots, *args):
        outs = [((width, ff), bf16), ((ff, width), bf16)]
        same = len(args) - len(slots)
        return call(lambda *r: place_ff_body(slots, *r), "place_ff", outs, same=same)(*args)

    across, beside = swap_ff(hr, 2, direct), swap(hr, 1)
    if direct:
        fb, y2 = along_ring(after(y0, hr), -1), swap(after(f2, hr), 2)
        ready = place_ff((0, 1, 2, 3, 4, 6), ff_slab, y0, f1, y1, f2, f3)
        across = after(across, ready)
        ff_slabs = [ff_slab, y0, f1, y1, f2, y2, f3, fb]
    hs = [hr, beside, across, swap(across, 1)]
    if direct:
        w1, w2 = place_ff((5, 7), *ready, ff_slabs[5], ff_slabs[7])
    else:
        w1, w2 = place_ff((0,), ff_slabs[0])
    feed = call(
        feed_body,
        "feed",
        [((mine, width), f32), ((mine, width), bf16), ((2, mine, width), bf16)]
        + [((RANKS, mine, ff), bf16)] * 2,
        us=3,
        vmem=14,
    )
    own, across, core, g_all, gp_all = feed(*hs, w1, w2)
    core = swap(core, 1)
    fs = [own, core, swap_ff(plus(across, core[0]), 2, direct)]
    turn = call(
        turn_body,
        "turn",
        [((local, width), bf16), ((share, width), bf16), ((mine, width), bf16)]
        + [((mine, width), f32), ((8, width), f32)],
    )
    yw, ye, df, du2, sums = turn(*fs, n1, norms, grad_words[0], grad_entities[0])

    across, beside = swap_ff(df, 2, direct), swap(df, 1)
    ds = [df, beside, across, swap(across, 1)]
    half_dz = ((2, mine, ff), bf16)
    feed_back_near = call(
        feed_back_near_body,
        "feed_back_near",
        [((mine, width), f32), ((mine, width), bf16), half_dz],
        vmem=12,
    )
    feed_back_far = call(
        feed_back_far_body,
        "feed_back_far",
        [((mine, width), bf16), ((2, mine, width), bf16), half_dz],
        vmem=12,
    )
    own, beside, dz_near = feed_back_near(*ds[:2], gp_all, w1, w2)
    across, core, dz_far = feed_back_far(*ds[2:], gp_all, w1, w2, beside)
    core = swap(core, 1)
    feed_grads = call(
        feed_grads_body,
        "feed_grads",
        [((width // shards, ff + width), bf16)] * shards,
        [pltpu.VMEM((width, ff), bf16), pltpu.VMEM((ff, width), bf16)],
        us=3,
        vmem=16,
    )
    sent = plus(across, core[0])
    ff_chunks = feed_grads(*ds, *hs, g_all, dz_near, after(dz_far, sent))
    dhs = [own, core, swap_ff(sent, 2, direct)]
    if direct:
        ff0, ff1, ff2, ff3, ff4, ff5, ff6, ff7 = ff_chunks
        fy, fz = swap(ff5, 2), along_ring(ff2)
        part = plus(ff4, after(fy, fz))
        dhs[2] = after(dhs[2], ff_chunks)
        fl = along_ring(part, -1)

    packed = width * 3 // 2 + 8 * (width // 128)
    norm_one = call(
        norm_one_body,
        "norm_one",
        [((mine, wide), bf16)] * 3
        + [((2 * packed + mine * 3 // 2, 128), bf16), ((mine, width), f32)]
        + [((packed, 128), bf16)] * 2,
        [pltpu.VMEM((RANKS, packed, 128), bf16), pltpu.VMEM((width, width), bf16)],
        vmem=12,
    )
    d0, d2, d3, core, du1, wo_own, across = norm_one(
        *dhs, du2, n1, i1, norms, sums, wo, *ctx
    )
    dcs = [d0, swap(core, 1), swap(d2, 2), swap(d3, 3)]
    sent = plus(across, after(dcs[1], dcs[2], dcs[3])[:packed])
    outs = [wo_own, dcs[1], swap(sent, 2)]
    dcs = after(dcs, sent)
    attend_back = call(
        lambda *r: attend_back_body(factor, *r),
        "attend_back",
        [((rows, 4 * wide), bf16)],
        [pltpu.VMEM((rows, wide), bf16)] + [pltpu.VMEM((rows, wide), f32)] * 4,
        us=7,
        vmem=16,
    )
    (dqkv,) = attend_back(*dcs, qw, qe, kk, vv, prob)
    to_input = call(
        input_body,
        "to_input",
        [((local, width), f32)]
        + [((n * local + ents + share, width), bf16) for n in (1, 2)],
        [pltpu.VMEM((rows, width), f32)],
        us=2,
        vmem=12,
    )
    own, across, core = to_input(dqkv, wq, du1, ye)
    if direct:
        own = after(own, fl)
    core = swap(core, 1)
    proj_grads = call(
        proj_grads_body,
        "proj_grads",
        [((width // shards, slab_cols), bf16)] * shards,
        [pltpu.VMEM((width, slab_cols), bf16)],
        us=2,
        vmem=14,
    )
    chunks = proj_grads(after(dqkv, own), xw, xe, *outs)
    if direct:
        fl = along_ring(plus(ff6, after(fl, dqkv)), -1)
        fb, fc = along_ring(after(ff3, dqkv)), along_ring(after(ff7, chunks), -1)
        part = plus(chunks[2], after(over_x(chunks[3]), fl))
        cx, cz = over_x(after(chunks[5], part, fb)), along_ring(part, -1)
        core = after(core, part)
    (sent,) = call(input_pair_body, "input_pair", [((local + ents + 2 * share, width), bf16)])(across, core)
    came = swap(sent, 2)
    input_sum = call(
        input_sum_body,
        "input_sum",
        [((local, width), f32), ((ents, width), f32), ((ents, width), bf16)],
    )
    if not direct:
        gxw, gxe, ye = input_sum(own, core, sent, came)

    if direct:
        last_ff = call(
            last_ff_body,
            "last_ff",
            [((ff_part, width), f32)] + [((part_rows, ff), bf16)] * 4,
            [pltpu.VMEM((RANKS * part_rows, ff), f32)],
        )
        part = plus(chunks[4], cz, cx)
        cx, cz = over_x(after(chunks[7], part)), along_ring(part, -1)
        fy_last = swap(plus(ff1, fb, after(fc, part)), 2)
        part = plus(chunks[6], after(cz, came), cx)
        cx, cz = over_x(after(chunks[1], part)), along_ring(part, -1)
        grad_ff_out, *back = last_ff(ff0, fz, fl, after(fy_last, part))
        back = [back[0]] + [swap_ff(back[k], k, direct) for k in (1, 2, 3)]
        spread_ff = call(
            spread_ff_body,
            "spread_ff",
            [((part_rows, RANKS * ff), f32)],
            [pltpu.VMEM((RANKS, part_rows, ff), f32)],
        )
        (grad_ff_in,) = spread_ff(*back)
        gxw, gxe, ye = input_sum(own, core, sent, after(came, part))
        last = call(
            last_body,
            "last",
            [((part_rows, slab_cols), bf16)] * 4,
            [pltpu.VMEM((RANKS * part_rows, slab_cols), f32)],
        )
        back = last(chunks[0], after(cz, grad_ff_in, gxw), cx)
        back = [back[0]] + swapped(back[1:])
        finish = call(
            finish_body,
            "finish",
            [((4, part_rows, width), f32), ((2, part_rows, width), f32), ((part_rows, width), f32)]
            + [((2, part_rows), f32)] * 2,
            [pltpu.VMEM((RANKS, part_rows, slab_cols), f32)],
        )
        grad_query, grad_kv, grad_out, grad_gain, grad_bias = finish(*back)
    else:
        both = jnp.concatenate([chunks[0], ff_chunks[0]], 1)
        both = lax.psum_scatter(both, "seq", scatter_dimension=0, tiled=True)
        grad_ff_out = both[:, slab_cols + ff :].astype(f32)
        both = both[:, : slab_cols + ff].reshape(RANKS, part_rows, slab_cols + ff)
        both = lax.all_to_all(both, "blk", 0, 0, tiled=True).astype(f32)
        seven = both[:, :, : 7 * wide].reshape(RANKS, part_rows, 7, wide)
        seven = seven.transpose(2, 1, 0, 3).reshape(7, part_rows, width)
        grad_query = jnp.concatenate([seven[:2], seven[4:6]], 0)
        grad_kv, grad_out = seven[2:4], seven[6]
        vecs = both[0, :, 7 * wide : 7 * wide + 4].T
        grad_gain, grad_bias = vecs[:2], vecs[2:]
        grad_ff_in = both[:, :, slab_cols:].reshape(RANKS, part_rows, seqs, ff_part)
        grad_ff_in = grad_ff_in.transpose(1, 2, 0, 3).reshape(part_rows, RANKS * ff)
    return (
        yw[None],
        ye[None],
        gxw[None],
        gxe[None],
        grad_query[None],
        grad_kv[None],
        grad_out[None],
        grad_ff_in[None],
        grad_ff_out[None],
        grad_gain[None],
        grad_bias[None],
    )


def solution(mesh):
    placed = (
        P("seq", "blk", None),
        P("seq", None, None),
        P("seq", None),
        P("seq"),
        P("seq", None),
        P(None, None, ("seq", "blk"), None),
        P(None, None, ("seq", "blk"), None),
        P(None, ("seq", "blk"), None),
        P(None, ("seq", "blk"), None),
        P(None, ("seq", "blk"), None),
        P(None, None, ("seq", "blk")),
        P(None, None, ("seq", "blk")),
        P("seq", "blk", None),
        P("seq", None, None),
    )
    return jax.shard_map(
        per_device,
        mesh=mesh,
        in_specs=placed,
        out_specs=(
            P("seq", "blk", None),
            P("seq", None, None),
            P("seq", "blk", None),
            P("seq", None, None),
            P(None, None, ("seq", "blk"), None),
            P(None, None, ("seq", "blk"), None),
            P(None, ("seq", "blk"), None),
            P(None, ("seq", "blk"), None),
            P(None, ("seq", "blk"), None),
            P(None, None, ("seq", "blk")),
            P(None, None, ("seq", "blk")),
        ),
        check_vma=False,
    )
```

```python
import jax
import jax.numpy as jnp
from jax import lax
from jax.experimental import pallas as pl
from jax.experimental.pallas import tpu as pltpu
from jax.sharding import PartitionSpec as P

HEADS = 12
RANKS = 4
epsilon = 1e-05
masked_score = -1e30
bf16 = jnp.bfloat16
f32 = jnp.float32


def dot_nn(a, b):
    return jnp.dot(a, b, preferred_element_type=f32)


def dot_nt(a, b):
    return lax.dot_general(a, b, (((1,), (1,)), ((), ())), preferred_element_type=f32)


def dot_tn(a, b):
    return lax.dot_general(a, b, (((0,), (0,)), ((), ())), preferred_element_type=f32)


def block(ref, index, size):
    return pl.ds(pl.multiple_of(index * size, size), size)


def call(body, name, outs, scratch=(), vmem=10, us=1, held=0, same=0):
    def run(*args):
        return pl.pallas_call(
            body,
            name=name,
            out_shape=[jax.ShapeDtypeStruct(s, t) for s, t in outs],
            in_specs=[pl.BlockSpec(memory_space=pltpu.HBM)] * held
            + [pl.BlockSpec(memory_space=pltpu.VMEM)] * (len(args) - held),
            out_specs=[pl.BlockSpec(memory_space=pltpu.VMEM)] * len(outs),
            scratch_shapes=list(scratch),
            input_output_aliases={i: i for i in range(same)},
            compiler_params=pltpu.CompilerParams(vmem_limit_bytes=vmem << 20),
            cost_estimate=pl.CostEstimate(
                flops=int(us * 1e6), bytes_accessed=int(us * 1e3), transcendentals=0
            ),
        )(*args)

    return run


def partner(k):
    return jnp.bitwise_xor(lax.axis_index("blk"), k)


def ring_seat(k, e):
    s = lax.axis_index("seq")
    z = lax.div(s, 2)
    at = lax.rem(jnp.bitwise_xor(z, lax.div(z, 2)) + (k + 4), 4)
    return 2 * jnp.bitwise_xor(at, lax.div(at, 2)) + jnp.bitwise_xor(lax.rem(s, 2), e)


def ff_rank():
    return 2 * lax.rem(lax.axis_index("seq"), 2) + lax.rem(lax.axis_index("blk"), 2)


def ff_seat(k, e):
    z = lax.div(lax.axis_index("seq"), 2)
    at = lax.rem(jnp.bitwise_xor(z, lax.div(z, 2)) + (k + 4), 4)
    y = jnp.bitwise_xor(lax.div(lax.axis_index("blk"), 2), e)
    return 2 * jnp.bitwise_xor(at, lax.div(at, 2)) + y


def ff_column(rank, j, part):
    return (8 * (j // 2) + 4 * (rank // 2) + 2 * (j % 2) + rank % 2) * part


def ff_rows(seat, x, rows):
    at = 4 * lax.div(seat, 2) + 2 * x + lax.rem(seat, 2)
    return pl.ds(pl.multiple_of(2 * rows * at, 16), 2 * rows)


def norm_stats(u):
    center = u - jnp.mean(u, axis=-1, keepdims=True)
    inverse = lax.rsqrt(jnp.mean(center * center, axis=-1, keepdims=True) + epsilon)
    return center * inverse, inverse


def norm_pull(scaled, normed, inverse):
    return inverse * (
        scaled
        - jnp.mean(scaled, axis=-1, keepdims=True)
        - normed * jnp.mean(scaled * normed, axis=-1, keepdims=True)
    )


def fetch(refs, sems):
    half = len(refs) // 2
    copies = [
        pltpu.make_async_copy(source, target, sems.at[i])
        for i, (source, target) in enumerate(zip(refs[:half], refs[half:]))
    ]
    for copy in copies:
        copy.start()
    for copy in copies:
        copy.wait()


def pack_body(*refs):
    sources, outs, scr, here, sems = refs[:5], refs[5:9], refs[9], refs[10:15], refs[15]
    fetch((*sources, *here), sems)
    q, kv, wo, gain, bias = here
    rows, wide = q.shape[1], q.shape[2] // RANKS
    eye = lax.broadcasted_iota(jnp.int32, (rows, rows), 0) == lax.broadcasted_iota(
        jnp.int32, (rows, rows), 1
    )
    lane = lax.broadcasted_iota(jnp.int32, (rows, 64), 1)
    vec = jnp.zeros((rows, 64), f32)
    for j, row in enumerate((gain[0:1], gain[1:2], bias[0:1], bias[1:2])):
        column = jnp.sum(jnp.where(eye, row.astype(f32), 0.0), axis=1, keepdims=True)
        vec = jnp.where(lane == j, column, vec)
    for t in range(RANKS):
        cut = slice(wide * t, wide * t + wide)
        for j, piece in enumerate((q[0], q[1], kv[0], kv[1], q[2], q[3], wo[...])):
            scr[t, :, wide * j : wide * j + wide] = piece[:, cut]
        scr[t, :, 7 * wide :] = vec.astype(bf16)
    for k in range(RANKS):
        outs[k][...] = scr[partner(k)]


def pack_ff_body(ff, *refs):
    outs, scr = refs[:RANKS], refs[RANKS]
    part = ff.shape[1] // (8 * RANKS)
    for t in range(RANKS):
        for j in range(8):
            at = ff_column(t, j, part)
            scr[t, :, part * j : part * j + part] = ff[:, at : at + part]
    for k in range(RANKS):
        outs[k][...] = scr[jnp.bitwise_xor(ff_rank(), k)]


def arrange_own_body(p0, out):
    out[block(out, partner(0), p0.shape[0])] = p0[...].astype(f32)


def arrange_body(own, p1, p2, p3, slab, scr):
    rows = p1.shape[0]
    scr[...] = own[...]
    for k, p in ((1, p1), (2, p2), (3, p3)):
        scr[block(scr, partner(k), rows)] = p[...].astype(f32)
    slab[...] = scr[...].astype(bf16)


def arrange_ff_body(p0, p1, p2, p3, ff_out, slab, scr):
    rows, cols = p0.shape
    for k, p in enumerate((p0, p1, p2, p3)):
        scr[block(scr, jnp.bitwise_xor(ff_rank(), k), rows)] = p[...].astype(f32)
    slab[:, :cols] = scr[...].astype(bf16)
    slab[:, cols:] = ff_out[...]


def place_body(slots, *refs):
    shards, (wq, wo_first, rest) = refs[-3 - len(slots) : -3], refs[-3:]
    rows, first = shards[0].shape[0], wq.shape[1]
    for j, shard in zip(slots, shards):
        at = block(shard, ring_seat(-(j // 2), j % 2) if rows < wq.shape[0] else 0, rows)
        wq[at] = shard[:, :first]
        wo_first[at] = shard[:, first : first + 128]
        rest[at] = shard[:, first + 128 :]


def place_last_body(slots, *refs):
    wide = refs[0].shape[1] // 6
    ins, (wq, wo_first, rest, wo_col, norms) = refs[:-5], refs[-5:]
    place_body(slots, *ins, wq, wo_first, rest)
    width = wq.shape[0]
    half = width // 2
    tail = rest[...]
    wo_col[:width] = wo_first[...]
    wo_col[width:] = jnp.concatenate([tail[:half, : wide - 128], tail[half:, : wide - 128]], 1)
    norms[...] = tail.astype(f32).T[wide - 128 : wide - 120]


def place_ff_body(slots, *refs):
    shards, w1, w2 = refs[-2 - len(slots) : -2], refs[-2], refs[-1]
    rows, cut = shards[0].shape[0], w1.shape[1]
    if rows == w1.shape[0]:
        w1[...] = shards[0][:, :cut]
        w2[...] = shards[0][:, cut:]
        return
    for j, shard in zip(slots, shards):
        seat = ff_seat(-(j // 2), j % 2)
        for x in (0, 1):
            w1[ff_rows(seat, x, rows // 4)] = shard[rows // 2 * x : rows // 2 * (x + 1), :cut]
        w2[block(shard, seat, rows)] = shard[:, cut:]


def join_out_body(w0, w1, w2, w3, wo, scr):
    wide = wo.shape[1] // RANKS
    half = wo.shape[0] // 2
    for k, w in enumerate((w0, w1, w2, w3)):
        scr[partner(k)] = w[...]
    for t in range(RANKS):
        wo[:, wide * t : wide * t + 128] = scr[t, : 2 * half]
        tail = scr[t, 2 * half :]
        wo[:half, wide * t + 128 : wide * t + wide] = tail[:, : wide - 128]
        wo[half:, wide * t + 128 : wide * t + wide] = tail[:, wide - 128 :]


def join_rows_body(x0, x1, x2, x3, xw):
    local = x0.shape[0]
    for k, x in enumerate((x0, x1, x2, x3)):
        xw[block(xw, partner(k), local)] = x[...]


def attend_body(wide, factor, xw, xe, wq, segq, segk, c0, c1, c2, c3, qw, qe, kk, vv, p_ref, c_scr):
    words, ents = xw.shape[0], xe.shape[0]
    local = words // RANKS
    share = ents // RANKS
    hl = HEADS // RANKS
    dh = wide // hl
    rows = words + ents
    w = dot_nn(xw[...], wq[:, : 4 * wide])
    e_kv = dot_nn(xe[...], wq[:, 2 * wide : 4 * wide])
    e_q = dot_nn(xe[...], wq[:, 4 * wide :])
    qw[:words] = (w[:, :wide] * factor).astype(bf16)
    qe[:words] = (w[:, wide : 2 * wide] * factor).astype(bf16)
    kk[:words] = w[:, 2 * wide : 3 * wide].astype(bf16)
    vv[:words] = w[:, 3 * wide :].astype(bf16)
    qw[words:] = (e_q[:, :wide] * factor).astype(bf16)
    qe[words:] = (e_q[:, wide:] * factor).astype(bf16)
    kk[words:] = e_kv[:, :wide].astype(bf16)
    vv[words:] = e_kv[:, wide:].astype(bf16)
    values_t = vv[...].astype(f32).T.astype(bf16)
    lane_head = lax.broadcasted_iota(jnp.int32, (128, wide), 1) // dh
    segcol = segk[...]

    def query_block(i, carry):
        at = pl.ds(pl.multiple_of(i * 128, 128), 128)
        q_word, q_ent = qw[at], qe[at]
        zero = jnp.zeros_like(q_word)
        stack_w = jnp.concatenate([jnp.where(lane_head == h, q_word, zero) for h in range(hl)], 0)
        stack_e = jnp.concatenate([jnp.where(lane_head == h, q_ent, zero) for h in range(hl)], 0)
        s_w = dot_nt(kk[:words], stack_w)
        s_e = dot_nt(kk[words:], stack_e)
        allowed = segcol == segq[0:1, at]
        probs = []
        for h in range(hl):
            lanes = slice(128 * h, 128 * h + 128)
            s = jnp.concatenate([s_w[:, lanes], s_e[:, lanes]], 0)
            s = jnp.where(allowed, s, masked_score)
            top = jnp.max(s, axis=0, keepdims=True)
            e = jnp.exp(s - top)
            probs.append((e * (1.0 / jnp.sum(e, axis=0, keepdims=True))).astype(bf16))
        prob = jnp.concatenate(probs, 1)
        p_ref[i] = prob
        ctx = dot_nn(values_t, prob)
        ctx = jnp.concatenate(
            [ctx[dh * h : dh * h + dh, 128 * h : 128 * h + 128] for h in range(hl)], 0
        )
        c_scr[at] = ctx.T.astype(bf16)
        return carry

    lax.fori_loop(0, rows // 128, query_block, 0, unroll=True)
    b = lax.axis_index("blk")
    for k, out in enumerate((c0, c1, c2, c3)):
        to = jnp.bitwise_xor(b, k)
        out[:local] = c_scr[block(c_scr, to, local)]
        out[local:] = c_scr[pl.ds(pl.multiple_of(words + to * share, share), share)]


def mix_body(c0, c1, c2, c3, wo, norms, xw, xe, hr, n1, i1):
    b = lax.axis_index("blk")
    wide = c0.shape[1]
    share = hr.shape[0] - xw.shape[0]
    u = jnp.concatenate([xw[...].astype(f32), xe[block(xe, b, share)].astype(f32)], 0)
    for k, c in enumerate((c0, c1, c2, c3)):
        u = u + dot_nn(c[...], wo[block(wo, partner(k), wide)])
    normed, inverse = norm_stats(u)
    n1[...] = normed
    i1[...] = inverse
    hr[...] = (normed * norms[0:1] + norms[2:3]).astype(bf16)


def feed_body(h0, h1, h2, h3, w1, w2, own, across, core, g_all, gp_all):
    outs = (own, core.at[1], across, core.at[0])
    for k, h in enumerate((h0, h1, h2, h3)):
        z = dot_nn(h[...], w1[...])
        cdf = 0.5 * (1.0 + lax.erf(z * 0.7071067811865476))
        g = (z * cdf).astype(bf16)
        g_all[k] = g
        gp_all[k] = (cdf + z * (0.3989422804014327 * jnp.exp(-0.5 * z * z))).astype(bf16)
        outs[k][...] = dot_nn(g, w2[...]).astype(outs[k].dtype)


def turn_body(f0, f1, f2, n1, norms, gw, ge, yw, ye, df, du2, sums):
    b = lax.axis_index("blk")
    local = gw.shape[0]
    rows = n1.shape[0]
    share = rows - local
    n = norms[...]
    u = n1[...] * n[0:1] + n[2:3]
    u = u + (f0[...] + f1[1].astype(f32) + f2[...].astype(f32))
    normed, inverse = norm_stats(u)
    y = (normed * n[1:2] + n[3:4]).astype(bf16)
    yw[...] = y[:local]
    ye[...] = y[local:]
    dy = jnp.concatenate([gw[...].astype(f32), ge[block(ge, b, share)].astype(f32)], 0)
    sums[...] = jnp.concatenate(
        [jnp.sum(dy * normed, axis=0, keepdims=True), jnp.sum(dy, axis=0, keepdims=True)]
        + [jnp.zeros((6, dy.shape[1]), f32)],
        0,
    )
    d = norm_pull(dy * n[1:2], normed, inverse)
    du2[...] = d
    df[...] = d.astype(bf16)


def feed_back_near_body(d0, d1, gp_all, w1, w2, own, beside, dz):
    for k, (d, out) in enumerate(((d0, own), (d1, beside))):
        z = (dot_nt(d[...], w2[...]) * gp_all[k].astype(f32)).astype(bf16)
        dz[k] = z
        out[...] = dot_nt(z, w1[...]).astype(out.dtype)


def feed_back_far_body(d2, d3, gp_all, w1, w2, beside, across, core, dz):
    core[1] = beside[...]
    for k, (d, out) in enumerate(((d2, across), (d3, core.at[0]))):
        z = (dot_nt(d[...], w2[...]) * gp_all[2 + k].astype(f32)).astype(bf16)
        dz[k] = z
        out[...] = dot_nt(z, w1[...]).astype(out.dtype)


def feed_grads_body(d0, d1, d2, d3, h0, h1, h2, h3, g_all, dz_near, dz_far, *refs):
    outs, g_in, g_out = refs[:-2], refs[-2], refs[-1]
    d = jnp.concatenate([x[...] for x in (d0, d1, d2, d3)], 0)
    h = jnp.concatenate([x[...] for x in (h0, h1, h2, h3)], 0)
    g = jnp.concatenate([g_all[k] for k in range(RANKS)], 0)
    z = jnp.concatenate([dz_near[0], dz_near[1], dz_far[0], dz_far[1]], 0)
    g_in[...] = dot_tn(h, z).astype(bf16)
    g_out[...] = dot_tn(g, d).astype(bf16)
    cut = g_in.shape[1]
    if len(outs) == 1:
        outs[0][:, :cut] = g_in[...]
        outs[0][:, cut:] = g_out[...]
        return
    for j, out in enumerate(outs):
        seat = ff_seat(j // 2, j % 2)
        rows = out.shape[0]
        for x in (0, 1):
            out[rows // 2 * x : rows // 2 * (x + 1), :cut] = g_in[ff_rows(seat, x, rows // 4)]
        out[:, cut:] = g_out[block(out, seat, rows)]


def norm_one_body(h0, h1, h2, du2, n1, i1, norms, two, wo, c0, c1, c2, c3, *refs):
    d0, d2, d3, core, du1, w_own, w_across, scr, whole = refs
    wide = d0.shape[1]
    dh = du2[...] + (h0[...] + h1[1].astype(f32) + h2[...].astype(f32))
    width = dh.shape[1]
    normed = n1[...]
    d = norm_pull(dh * norms[0:1], normed, i1[...])
    du1[...] = d
    low = d.astype(bf16)
    dc = [dot_nt(low, wo[block(wo, partner(k), wide)]).astype(bf16) for k in range(RANKS)]
    d0[...] = dc[0]
    base = 2 * scr.shape[1]
    mine = dc[1].shape[0]
    core[base : base + mine] = dc[1][:, :128]
    core[base + mine :] = jnp.concatenate([dc[1][: mine // 2, 128:], dc[1][mine // 2 :, 128:]], 1)
    d2[...] = dc[2]
    d3[...] = dc[3]
    sums = jnp.concatenate(
        [jnp.sum(dh * normed, axis=0, keepdims=True), two[0:1]]
        + [jnp.sum(dh, axis=0, keepdims=True), two[1:2], jnp.zeros((124, width), f32)],
        0,
    )
    half = width // 2
    for k, c in enumerate((c0, c1, c2, c3)):
        whole[block(whole, partner(k), wide)] = dot_tn(c[...], low).astype(bf16)
    for t in range(RANKS):
        at = wide * t
        scr[t, :width] = whole[:, at : at + 128]
        rest = slice(at + 128, at + wide)
        scr[t, width : width + half] = jnp.concatenate([whole[:half, rest], whole[half:, rest]], 1)

    low_sums = sums[:8].astype(bf16)
    for t in range(RANKS):
        for j in range(width // 128):
            at = width + half + 8 * j
            scr[t, at : at + 8] = low_sums[:, 128 * j : 128 * j + 128]
    rows = scr.shape[1]
    w_own[...] = scr[partner(0)]
    core[:rows] = scr[partner(3)]
    core[rows : 2 * rows] = scr[partner(1)]
    w_across[...] = scr[partner(2)]


def attend_back_body(factor, d0, core, d2, d3, qw, qe, kk, vv, p_ref, dqkv, dc, dqw, dqe, dk, dv):
    b = lax.axis_index("blk")
    rows, wide = qw.shape
    local = rows * 4 // 5 // RANKS
    words = local * RANKS
    share = (rows - words) // RANKS
    hl = HEADS // RANKS
    dh = wide // hl
    mine = d0.shape[0]
    base = core.shape[0] - mine * 3 // 2
    tail = core[base + mine :]
    d1 = jnp.concatenate(
        [core[base : base + mine], jnp.concatenate([tail[:, :64], tail[:, 64:]], 0)], 1
    )
    for k, d in enumerate((d0[...], d1, d2[...], d3[...])):
        to = jnp.bitwise_xor(b, k)
        dc[block(dc, to, local)] = d[:local]
        dc[pl.ds(pl.multiple_of(words + to * share, share), share)] = d[local:]
    keys_t = kk[...].astype(f32).T.astype(bf16)
    lane_head = lax.broadcasted_iota(jnp.int32, (128, wide), 1) // dh
    dk[...] = jnp.zeros_like(dk)
    dv[...] = jnp.zeros_like(dv)

    def query_block(i, carry):
        at = pl.ds(pl.multiple_of(i * 128, 128), 128)
        zero = jnp.zeros((128, wide), bf16)

        def stacked(x):
            return jnp.concatenate([jnp.where(lane_head == h, x, zero) for h in range(hl)], 0)

        stack_d = stacked(dc[at])
        prob = p_ref[i]
        dp = dot_nt(vv[...], stack_d)
        parts = []
        for h in range(hl):
            lanes = slice(128 * h, 128 * h + 128)
            p = prob[:, lanes].astype(f32)
            g = dp[:, lanes]
            delta = jnp.sum(p * g, axis=0, keepdims=True)
            parts.append((p * (g - delta)).astype(bf16))
        ds = jnp.concatenate(parts, 1)
        dv[...] += dot_nn(prob, stack_d)
        dk[:words] += dot_nn(ds[:words], stacked(qw[at]))
        dk[words:] += dot_nn(ds[words:], stacked(qe[at]))
        for keys, ds_part, out in ((keys_t[:, :words], ds[:words], dqw), (keys_t[:, words:], ds[words:], dqe)):
            t = dot_nn(keys, ds_part)
            t = jnp.concatenate(
                [t[dh * h : dh * h + dh, 128 * h : 128 * h + 128] for h in range(hl)], 0
            )
            out[at] = t.T
        return carry

    lax.fori_loop(0, rows // 128, query_block, 0, unroll=True)
    dqkv[:, :wide] = (dqw[...] * factor).astype(bf16)
    dqkv[:, wide : 2 * wide] = (dqe[...] * factor).astype(bf16)
    dqkv[:, 2 * wide : 3 * wide] = dk[...].astype(bf16)
    dqkv[:, 3 * wide :] = dv[...].astype(bf16)


def proj_grads_body(dqkv, xw, xe, o0, o1, o2, *refs):
    outs, scr = refs[:-1], refs[-1]
    words = xw.shape[0]
    out_rows = o0.shape[0]
    half = dqkv.shape[1] // 2
    w = dot_tn(xw[...], dqkv[:words])
    e = dot_tn(xe[...], dqkv[words:])
    scr[:, :half] = w[:, :half].astype(bf16)
    scr[:, half : 2 * half] = (w[:, half:] + e[:, half:]).astype(bf16)
    scr[:, 2 * half : 3 * half] = e[:, :half].astype(bf16)
    o = o0[...].astype(f32) + o1[out_rows : 2 * out_rows].astype(f32) + o2[...].astype(f32)
    width = scr.shape[0]
    middle = width // 2
    tail = o[width : width + middle]
    scr[:, 3 * half : 3 * half + 128] = o[:width].astype(bf16)
    scr[:middle, 3 * half + 128 : 3 * half + 192] = tail[:, :64].astype(bf16)
    scr[middle:, 3 * half + 128 : 3 * half + 192] = tail[:, 64:].astype(bf16)
    vec = o[width + middle :]
    sums = jnp.concatenate([vec[8 * j : 8 * j + 8] for j in range(width // 128)], 1)
    sums = jnp.concatenate([sums, jnp.zeros((120, width), f32)], 0).T
    scr[:, 3 * half + 192 :] = sums[:, :64].astype(bf16)
    for j, out in enumerate(outs):
        to = ring_seat(j // 2, j % 2) if len(outs) > 1 else 0
        out[...] = scr[block(scr, to, out.shape[0])]


def total_of(*parts):
    total = parts[0][...].astype(f32)
    for part in parts[1:]:
        total = total + part[...].astype(f32)
    return total


def last_ff_body(a0, a1, a2, a3, w_out, c0, c1, c2, c3, scr):
    rows = c0.shape[0]
    width = c0.shape[1]
    t = total_of(a0, a1, a2, a3)
    w_out[...] = t[:, width:]
    scr[...] = t[:, :width]
    for k, c in enumerate((c0, c1, c2, c3)):
        c[...] = scr[block(scr, jnp.bitwise_xor(ff_rank(), k), rows)].astype(bf16)


def spread_ff_body(c0, c1, c2, c3, out, scr):
    part = out.shape[1] // (8 * RANKS)
    for k, c in enumerate((c0, c1, c2, c3)):
        scr[jnp.bitwise_xor(ff_rank(), k)] = c[...].astype(f32)
    for t in range(RANKS):
        for j in range(8):
            at = ff_column(t, j, part)
            out[:, at : at + part] = scr[t, :, part * j : part * j + part]


def last_body(a0, a1, a2, c0, c1, c2, c3, scr):
    rows = c0.shape[0]
    scr[...] = total_of(a0, a1, a2)
    for k, c in enumerate((c0, c1, c2, c3)):
        c[...] = scr[block(scr, partner(k), rows)].astype(bf16)


def finish_body(c0, c1, c2, c3, gq, gkv, go, gg, gb, scr):
    wide = go.shape[1] // RANKS
    for k, c in enumerate((c0, c1, c2, c3)):
        scr[partner(k)] = c[...].astype(f32)
    for t in range(RANKS):
        cut = slice(wide * t, wide * t + wide)
        for j, (out, i) in enumerate(((gq, 0), (gq, 1), (gkv, 0), (gkv, 1), (gq, 2), (gq, 3))):
            out[i, :, cut] = scr[t, :, wide * j : wide * j + wide]
        go[:, cut] = scr[t, :, 6 * wide : 7 * wide]
    at = 7 * wide + 64 - 128
    v = c0[:, at:].astype(f32).T
    gg[...] = v[64:66]
    gb[...] = v[66:68]


def input_body(dqkv, wq, du1, ye, own, across, core, part):
    b = lax.axis_index("blk")
    local, share = own.shape[0], ye.shape[0]
    words = RANKS * local
    half = dqkv.shape[1] // 2
    part[:words] = dot_nt(dqkv[:words], wq[:, : 2 * half])
    part[words:] = dot_nt(dqkv[words:, half:], wq[:, half : 2 * half]) + dot_nt(
        dqkv[words:, :half], wq[:, 2 * half :]
    )
    part[pl.ds(pl.multiple_of(words + b * share, share), share)] += du1[local:]
    own[...] = part[block(part, b, local)] + du1[:local]
    low = part[words:].astype(bf16)
    core[:local] = part[block(part, partner(3), local)].astype(bf16)
    core[local : 2 * local] = part[block(part, partner(1), local)].astype(bf16)
    core[2 * local : -share] = low
    core[-share:] = ye[...]
    across[:local] = part[block(part, partner(2), local)].astype(bf16)
    across[local:-share] = low
    across[-share:] = ye[...]


def input_pair_body(across, came, sent):
    share = sent.shape[0] - across.shape[0]
    local = came.shape[0] - across.shape[0]
    sent[:local] = (across[:local].astype(f32) + came[:local].astype(f32)).astype(bf16)
    pair = across[local:-share].astype(f32) + came[2 * local : -share].astype(f32)
    sent[local : -2 * share] = pair.astype(bf16)
    sent[-2 * share : -share] = across[-share:]
    sent[-share:] = came[-share:]


def input_sum_body(own, core, sent, came, gw, ge, ye):
    local = own.shape[0]
    share = ye.shape[0] // RANKS
    two = 2 * share
    gw[...] = own[...] + core[local : 2 * local].astype(f32) + came[:local].astype(f32)
    ge[...] = sent[local:-two].astype(f32) + came[local:-two].astype(f32)
    for k, rows in enumerate((sent[-two:-share], sent[-share:], came[-two:-share], came[-share:])):
        ye[block(ye, partner(k), share)] = rows


def swap(x, k):
    return lax.ppermute(x, "blk", [(i, i ^ k) for i in range(RANKS)])


def swapped(send):
    return [swap(send[k - 1], k) for k in (1, 2, 3)]


def spread(x):
    across = swap(x, 2)
    beside = swap(x, 1)
    return [beside, across, swap(across, 1)]


def plus(*parts):
    total = parts[0].astype(f32)
    for part in parts[1:]:
        total = total + part.astype(f32)
    return total.astype(bf16)


def over_x(x):
    return lax.ppermute(x, "seq", [(i, i ^ 1) for i in range(8)])


ring = (0, 1, 3, 2)


def swap_ff(x, k, direct):
    if not direct or k == 1:
        return swap(x, k)
    if k == 2:
        return over_x(x)
    return lax.ppermute(x, ("seq", "blk"), [(i, i ^ 5) for i in range(32)])


def along_ring(x, step=1):
    route = [(ring[i], ring[(i + step) % 4]) for i in range(4)]
    return lax.ppermute(x, "seq", [(2 * z + i, 2 * to + i) for z, to in route for i in (0, 1)])


def fence(*groups):
    return lax.optimization_barrier(groups)


def after(x, *before):
    return lax.optimization_barrier((x, before))[0]


def per_device(
    words,
    entities,
    segments,
    entity_counts,
    entity_anchor,
    query_weights,
    kv_weights,
    out_weight,
    ff_in,
    ff_out,
    norm_gain,
    norm_bias,
    grad_words,
    grad_entities,
):
    seqs = lax.axis_size("seq")
    direct = seqs == 8
    _, local, width = words.shape
    ents = entities.shape[1]
    share = ents // RANKS
    total = local * RANKS
    rows = total + ents
    mine = local + share
    wide = width // RANKS
    hl = HEADS // RANKS
    factor = (width // HEADS) ** (-0.5)
    part_rows = query_weights.shape[2]
    ff_part = ff_out.shape[1]
    ff = ff_part * seqs
    shards = 8 if direct else 1
    slab_cols = 7 * wide + 64
    xw_own, xe = words[0], entities[0]

    seg_ents = jnp.take_along_axis(segments, entity_anchor, axis=1)
    live = jnp.arange(ents, dtype=jnp.int32)[None, :] < entity_counts[:, None]
    segq = jnp.concatenate([segments, seg_ents], 1)
    segk = jnp.concatenate([segments, jnp.where(live, seg_ents, -1)], 1).T
    join_rows = call(join_rows_body, "join_rows", [((total, width), bf16)])

    if direct:
        pack = call(
            pack_body,
            "pack",
            [((part_rows, slab_cols), bf16)] * 4,
            [pltpu.VMEM((RANKS, part_rows, slab_cols), bf16)]
            + [pltpu.VMEM((n, part_rows, width), bf16) for n in (4, 2)]
            + [pltpu.VMEM((part_rows, width), bf16)]
            + [pltpu.VMEM((2, part_rows), bf16)] * 2
            + [pltpu.SemaphoreType.DMA((5,))],
            held=5,
            vmem=60,
        )
        pieces = pack(
            query_weights[0], kv_weights[0], out_weight[0], norm_gain[0], norm_bias[0]
        )
        pack_ff = call(
            pack_ff_body,
            "pack_ff",
            [((part_rows, ff), bf16)] * 4,
            [pltpu.VMEM((RANKS, part_rows, ff), bf16)],
        )
        ff_pieces = pack_ff(after(ff_in[0], pieces[0]))
        own = call(
            arrange_own_body, "arrange_own", [((RANKS * part_rows, slab_cols), f32)]
        )(pieces[0])
        pieces = [own[0], *swapped(pieces[1:])]

        arrange = call(
            arrange_body,
            "arrange",
            [((RANKS * part_rows, slab_cols), bf16)],
            [pltpu.VMEM((RANKS * part_rows, slab_cols), f32)],
        )
        arrange_ff = call(
            arrange_ff_body,
            "arrange_ff",
            [((RANKS * part_rows, ff + width), bf16)],
            [pltpu.VMEM((RANKS * part_rows, ff), f32)],
        )
        (slab,) = arrange(*pieces)
        xw_own, slab = fence(xw_own, slab)
        xb, xa = swap(xw_own, 1), swap(xw_own, 2)
        x0, g1 = over_x(slab), along_ring(slab)
        g1, x0, xb, ff_pieces = fence(g1, x0, xb, ff_pieces)
        x1, g2 = over_x(g1), along_ring(g1)
        came = [swap_ff(ff_pieces[k], k, direct) for k in (1, 2, 3)]
        (ff_slab,) = arrange_ff(ff_pieces[0], *came, ff_out[0])
        g2, x1, ff_slab, xa = fence(g2, x1, ff_slab, xa)
        x2, g3 = over_x(g2), along_ring(g2)
        y0, xc = swap(ff_slab, 2), swap(xa, 1)
        g3, x2, xc, segq, segk = fence(g3, x2, xc, segq, segk)
        f1, x3 = along_ring(after(ff_slab, g3)), over_x(g3)
        (xw,) = join_rows(xw_own, xb, xa, xc)
        x3, y0 = after((x3, y0), xw)
        f2 = along_ring(after(f1, y0, x3))
        slabs = [slab, x0, g1, x1, g2, x2, g3, x3]
    else:
        vec = jnp.concatenate([norm_gain[0], norm_bias[0]], 0).T
        vec = jnp.pad(vec, ((0, 0), (0, 60)))
        six = jnp.concatenate(
            [query_weights[0, :2], kv_weights[0], query_weights[0, 2:], out_weight], 0
        )
        six = six.reshape(7, part_rows, RANKS, wide).transpose(2, 1, 0, 3)
        six = six.reshape(RANKS, part_rows, 7 * wide)
        ff_cols = ff_in[0].reshape(part_rows, seqs, RANKS, ff_part).transpose(2, 0, 1, 3)
        ff_cols = ff_cols.reshape(RANKS, part_rows, ff)
        pack = jnp.concatenate(
            [six, jnp.broadcast_to(vec, (RANKS, part_rows, 64)), ff_cols], 2
        )
        pack = lax.all_to_all(pack, "blk", 0, 0, tiled=True).reshape(RANKS * part_rows, -1)
        pack = jnp.concatenate([pack, ff_out[0]], 1)
        pack = lax.all_gather(pack, "seq", axis=0, tiled=True)
        slabs, ff_slabs = [pack[:, :slab_cols]], [pack[:, slab_cols:]]
        (xw,) = join_rows(xw_own, *spread(xw_own))

    def place(slots, last, *args):
        outs = [((width, 6 * wide), bf16), ((width, 128), bf16), ((width, wide - 64), bf16)]
        if last:
            outs += [((width * 3 // 2, 128), bf16), ((8, width), f32)]
        body = place_last_body if last else place_body
        same = len(args) - len(slots)
        name = "place_last" if last else "place"
        return call(lambda *r: body(slots, *r), name, outs, same=same)(*args)

    if direct:
        ready = place((0, 1, 2, 3, 4, 5, 6), False, *slabs[:7])
        wq, _, _, wo_col, norms = place((7,), True, *ready, slabs[7])
    else:
        blank = [jnp.zeros((width, n), bf16) for n in (6 * wide, 128, wide - 64)]
        wq, _, _, wo_col, norms = place((0,), True, *blank, slabs[0])
    wa, wb = swap(wo_col, 2), swap(wo_col, 1)
    attend = call(
        lambda *r: attend_body(wide, factor, *r),
        "attend",
        [((mine, wide), bf16)] * 4
        + [((rows, wide), bf16)] * 4
        + [((rows // 128, rows, 128 * hl), bf16)],
        [pltpu.VMEM((rows, wide), bf16)],
        us=7,
        vmem=16,
    )
    *ctx, qw, qe, kk, vv, prob = attend(xw, xe, wq, segq, segk)
    if direct:
        ctx = after(ctx, wb)
    ctx = [ctx[0]] + swapped(ctx[1:])
    wos = [wo_col, wb, wa, swap(after(wa, ctx), 1)]
    if direct:
        f3, y1 = along_ring(f2), swap(after(f1, ctx), 2)
    join_out = call(
        join_out_body,
        "join_out",
        [((width, width), bf16)],
        [pltpu.VMEM((RANKS, width * 3 // 2, 128), bf16)],
    )
    (wo,) = join_out(*(after(wos, f3) if direct else wos))
    mix = call(
        mix_body,
        "mix",
        [((mine, width), bf16), ((mine, width), f32), ((mine, 1), f32)],
    )
    hr, n1, i1 = mix(*ctx, wo, norms, xw_own, xe)

    def place_ff(slots, *args):
        outs = [((width, ff), bf16), ((ff, width), bf16)]
        same = len(args) - len(slots)
        return call(lambda *r: place_ff_body(slots, *r), "place_ff", outs, same=same)(*args)

    across, beside = swap_ff(hr, 2, direct), swap(hr, 1)
    if direct:
        fb, y2 = along_ring(after(y0, hr), -1), swap(after(f2, hr), 2)
        ready = place_ff((0, 1, 2, 3, 4, 6), ff_slab, y0, f1, y1, f2, f3)
        across = after(across, ready)
        ff_slabs = [ff_slab, y0, f1, y1, f2, y2, f3, fb]
    hs = [hr, beside, across, swap(across, 1)]
    if direct:
        w1, w2 = place_ff((5, 7), *ready, ff_slabs[5], ff_slabs[7])
    else:
        w1, w2 = place_ff((0,), ff_slabs[0])
    feed = call(
        feed_body,
        "feed",
        [((mine, width), f32), ((mine, width), bf16), ((2, mine, width), bf16)]
        + [((RANKS, mine, ff), bf16)] * 2,
        us=3,
        vmem=14,
    )
    own, across, core, g_all, gp_all = feed(*hs, w1, w2)
    core = swap(core, 1)
    fs = [own, core, swap_ff(plus(across, core[0]), 2, direct)]
    turn = call(
        turn_body,
        "turn",
        [((local, width), bf16), ((share, width), bf16), ((mine, width), bf16)]
        + [((mine, width), f32), ((8, width), f32)],
    )
    yw, ye, df, du2, sums = turn(*fs, n1, norms, grad_words[0], grad_entities[0])

    across, beside = swap_ff(df, 2, direct), swap(df, 1)
    ds = [df, beside, across, swap(across, 1)]
    half_dz = ((2, mine, ff), bf16)
    feed_back_near = call(
        feed_back_near_body,
        "feed_back_near",
        [((mine, width), f32), ((mine, width), bf16), half_dz],
        vmem=12,
    )
    feed_back_far = call(
        feed_back_far_body,
        "feed_back_far",
        [((mine, width), bf16), ((2, mine, width), bf16), half_dz],
        vmem=12,
    )
    own, beside, dz_near = feed_back_near(*ds[:2], gp_all, w1, w2)
    across, core, dz_far = feed_back_far(*ds[2:], gp_all, w1, w2, beside)
    core = swap(core, 1)
    feed_grads = call(
        feed_grads_body,
        "feed_grads",
        [((width // shards, ff + width), bf16)] * shards,
        [pltpu.VMEM((width, ff), bf16), pltpu.VMEM((ff, width), bf16)],
        us=3,
        vmem=16,
    )
    sent = plus(across, core[0])
    ff_chunks = feed_grads(*ds, *hs, g_all, dz_near, after(dz_far, sent))
    dhs = [own, core, swap_ff(sent, 2, direct)]
    if direct:
        ff0, ff1, ff2, ff3, ff4, ff5, ff6, ff7 = ff_chunks
        fy, fz = swap(ff5, 2), along_ring(ff2)
        part = plus(ff4, after(fy, fz))
        dhs[2] = after(dhs[2], ff_chunks)
        fl = along_ring(part, -1)

    packed = width * 3 // 2 + 8 * (width // 128)
    norm_one = call(
        norm_one_body,
        "norm_one",
        [((mine, wide), bf16)] * 3
        + [((2 * packed + mine * 3 // 2, 128), bf16), ((mine, width), f32)]
        + [((packed, 128), bf16)] * 2,
        [pltpu.VMEM((RANKS, packed, 128), bf16), pltpu.VMEM((width, width), bf16)],
        vmem=12,
    )
    d0, d2, d3, core, du1, wo_own, across = norm_one(
        *dhs, du2, n1, i1, norms, sums, wo, *ctx
    )
    dcs = [d0, swap(core, 1), swap(d2, 2), swap(d3, 3)]
    sent = plus(across, after(dcs[1], dcs[2], dcs[3])[:packed])
    outs = [wo_own, dcs[1], swap(sent, 2)]
    dcs = after(dcs, sent)
    attend_back = call(
        lambda *r: attend_back_body(factor, *r),
        "attend_back",
        [((rows, 4 * wide), bf16)],
        [pltpu.VMEM((rows, wide), bf16)] + [pltpu.VMEM((rows, wide), f32)] * 4,
        us=7,
        vmem=16,
    )
    (dqkv,) = attend_back(*dcs, qw, qe, kk, vv, prob)
    to_input = call(
        input_body,
        "to_input",
        [((local, width), f32)]
        + [((n * local + ents + share, width), bf16) for n in (1, 2)],
        [pltpu.VMEM((rows, width), f32)],
        us=2,
        vmem=12,
    )
    own, across, core = to_input(dqkv, wq, du1, ye)
    if direct:
        own = after(own, fl)
    core = swap(core, 1)
    proj_grads = call(
        proj_grads_body,
        "proj_grads",
        [((width // shards, slab_cols), bf16)] * shards,
        [pltpu.VMEM((width, slab_cols), bf16)],
        us=2,
        vmem=14,
    )
    chunks = proj_grads(after(dqkv, own), xw, xe, *outs)
    if direct:
        fl = along_ring(plus(ff6, after(fl, dqkv)), -1)
        fb, fc = along_ring(after(ff3, dqkv)), along_ring(after(ff7, chunks), -1)
        part = plus(chunks[2], after(over_x(chunks[3]), fl, fb))
        cx, cz = over_x(after(chunks[5], part)), along_ring(part, -1)
        core = after(core, part)
    (sent,) = call(input_pair_body, "input_pair", [((local + ents + 2 * share, width), bf16)])(across, core)
    came = swap(sent, 2)
    input_sum = call(
        input_sum_body,
        "input_sum",
        [((local, width), f32), ((ents, width), f32), ((ents, width), bf16)],
    )
    if not direct:
        gxw, gxe, ye = input_sum(own, core, sent, came)

    if direct:
        last_ff = call(
            last_ff_body,
            "last_ff",
            [((ff_part, width), f32)] + [((part_rows, ff), bf16)] * 4,
            [pltpu.VMEM((RANKS * part_rows, ff), f32)],
        )
        part = plus(chunks[4], cz, cx)
        cx, cz = over_x(after(chunks[7], part)), along_ring(part, -1)
        fy_last = swap(plus(ff1, fb, after(fc, part)), 2)
        part = plus(chunks[6], after(cz, came), cx)
        cx, cz = over_x(after(chunks[1], part)), along_ring(part, -1)
        grad_ff_out, *back = last_ff(ff0, fz, fl, after(fy_last, part))
        back = [back[0]] + [swap_ff(back[k], k, direct) for k in (1, 2, 3)]
        spread_ff = call(
            spread_ff_body,
            "spread_ff",
            [((part_rows, RANKS * ff), f32)],
            [pltpu.VMEM((RANKS, part_rows, ff), f32)],
        )
        (grad_ff_in,) = spread_ff(*back)
        gxw, gxe, ye = input_sum(own, core, sent, after(came, part))
        last = call(
            last_body,
            "last",
            [((part_rows, slab_cols), bf16)] * 4,
            [pltpu.VMEM((RANKS * part_rows, slab_cols), f32)],
        )
        back = last(chunks[0], after(cz, grad_ff_in, gxw), cx)
        back = [back[0]] + swapped(back[1:])
        finish = call(
            finish_body,
            "finish",
            [((4, part_rows, width), f32), ((2, part_rows, width), f32), ((part_rows, width), f32)]
            + [((2, part_rows), f32)] * 2,
            [pltpu.VMEM((RANKS, part_rows, slab_cols), f32)],
        )
        grad_query, grad_kv, grad_out, grad_gain, grad_bias = finish(*back)
    else:
        both = jnp.concatenate([chunks[0], ff_chunks[0]], 1)
        both = lax.psum_scatter(both, "seq", scatter_dimension=0, tiled=True)
        grad_ff_out = both[:, slab_cols + ff :].astype(f32)
        both = both[:, : slab_cols + ff].reshape(RANKS, part_rows, slab_cols + ff)
        both = lax.all_to_all(both, "blk", 0, 0, tiled=True).astype(f32)
        seven = both[:, :, : 7 * wide].reshape(RANKS, part_rows, 7, wide)
        seven = seven.transpose(2, 1, 0, 3).reshape(7, part_rows, width)
        grad_query = jnp.concatenate([seven[:2], seven[4:6]], 0)
        grad_kv, grad_out = seven[2:4], seven[6]
        vecs = both[0, :, 7 * wide : 7 * wide + 4].T
        grad_gain, grad_bias = vecs[:2], vecs[2:]
        grad_ff_in = both[:, :, slab_cols:].reshape(RANKS, part_rows, seqs, ff_part)
        grad_ff_in = grad_ff_in.transpose(1, 2, 0, 3).reshape(part_rows, RANKS * ff)
    return (
        yw[None],
        ye[None],
        gxw[None],
        gxe[None],
        grad_query[None],
        grad_kv[None],
        grad_out[None],
        grad_ff_in[None],
        grad_ff_out[None],
        grad_gain[None],
        grad_bias[None],
    )


def solution(mesh):
    placed = (
        P("seq", "blk", None),
        P("seq", None, None),
        P("seq", None),
        P("seq"),
        P("seq", None),
        P(None, None, ("seq", "blk"), None),
        P(None, None, ("seq", "blk"), None),
        P(None, ("seq", "blk"), None),
        P(None, ("seq", "blk"), None),
        P(None, ("seq", "blk"), None),
        P(None, None, ("seq", "blk")),
        P(None, None, ("seq", "blk")),
        P("seq", "blk", None),
        P("seq", None, None),
    )
    return jax.shard_map(
        per_device,
        mesh=mesh,
        in_specs=placed,
        out_specs=(
            P("seq", "blk", None),
            P("seq", None, None),
            P("seq", "blk", None),
            P("seq", None, None),
            P(None, None, ("seq", "blk"), None),
            P(None, None, ("seq", "blk"), None),
            P(None, ("seq", "blk"), None),
            P(None, ("seq", "blk"), None),
            P(None, ("seq", "blk"), None),
            P(None, None, ("seq", "blk")),
            P(None, None, ("seq", "blk")),
        ),
        check_vma=False,
    )
```
